32 devices in a mesh: fsdp: 8 (over z, x), rep: 4 (over y, core).
Axes of the slice: x: 2, y: 2, z: 4, core: 2. Of those that a mesh axis runs over, the one named last changes fastest.
Arguments:
- layer_input: bfloat16 [32768, 768], P(('fsdp', 'rep')), may hold values from -6 to 6
- qkv_weight: bfloat16 [768, 2304], P('fsdp'), may hold values from -0.21875 to 0.21875
- attn_weight: bfloat16 [768, 768], P('fsdp'), may hold values from -1.75 to 1.75
- wide_weight: bfloat16 [768, 2304], P('fsdp'), may hold values from -0.21875 to 0.21875
- narrow_weight: bfloat16 [768, 1152], P('fsdp'), may hold values from -0.375 to 0.375
- first_gain: bfloat16 [768], P('fsdp'), may hold values from 0.099609375 to 1.8984375
- second_gain: bfloat16 [768], P('fsdp'), may hold values from 0.099609375 to 1.8984375
- out_grad: bfloat16 [32768, 768], P(('fsdp', 'rep')), may hold values from -12 to 12
- token_seg: int32 [32768], P(('fsdp', 'rep')), may hold values from 0 to 255, as said below
- token_live: int32 [32768], P(('fsdp', 'rep')), may hold values from 0 to 1, as said below
Outputs:
- layer_output: bfloat16 [32768, 768], P(('fsdp', 'rep'))
- input_grad: float32 [32768, 768], P(('fsdp', 'rep'))
- qkv_grad: float32 [768, 2304], P('fsdp')
- attn_grad: float32 [768, 768], P('fsdp')
- wide_grad: float32 [768, 2304], P('fsdp')
- narrow_grad: float32 [768, 1152], P('fsdp')
- first_grad: float32 [768], P('fsdp')
- second_grad: float32 [768], P('fsdp')
The draws below stay inside these ranges and needn't reach their ends.
Inputs may be any that keep to these rules, and one draw needn't show every extreme that they name: `token_seg`: numbers never fall along the slots; all slots of one number lie in one block of 1024 slots (one device's), and each number begins at a multiple of 128; every block begins a new number; the last tile of the last block begins a number of its own. `token_live`: within each number of token_seg the live slots come first and its first slot is live; in every draw one block of 1024 slots holds a single number with every slot live.
All inputs are finite; a program needn't handle non-finite values.
Results may differ from the reference program's by a relative error of at most 0.018.
Values may be sent and summed in bfloat16 or wider, within the bound.
A program may use at most 320 MiB of HBM per device.

```python
import math
import jax
import jax.numpy as jnp
from jax import lax

D = 768
FF = 1152
HDIM = 64
TILE = 128
TOK_DEV = 1024
TOKENS = 32768
N_FSDP = 8
N_REP = 4


def layout_draw(key):
    base = jax.random.fold_in(key, 7)
    key_star, key_used, key_cut, key_fill = jax.random.split(base, 4)
    buffers = TOKENS // TOK_DEV
    tiles = TOK_DEV // TILE
    chosen = jax.random.randint(key_star, (), 0, buffers - 1)
    is_star = (jnp.arange(buffers) == chosen)[:, None]
    is_last = (jnp.arange(buffers) == buffers - 1)[:, None]
    used = jax.random.randint(key_used, (buffers, 1), tiles - tiles // 2, tiles + 1)
    used = jnp.where(is_star | is_last, tiles, used)
    column = jnp.arange(tiles)[None, :]
    breaks = jax.random.randint(key_cut, (buffers, tiles), 0, 5) < 2
    breaks = breaks & (column < used) & jnp.logical_not(is_star) | (column == 0)
    breaks = breaks | is_last & (column == tiles - 1)
    start_col = lax.cummax(jnp.where(breaks, column, 0), axis=1)
    tile_seg = start_col + jnp.arange(buffers, dtype=jnp.int32)[:, None] * tiles
    following = jnp.concatenate([breaks[:, 1:], jnp.ones((buffers, 1), dtype=jnp.bool_)], axis=1)
    closing = (column < used) & ((column == used - 1) | following)
    partial_fill = jax.random.randint(key_fill, (buffers, tiles), 1, TILE + 1)
    counts = jnp.where(closing, partial_fill, TILE)
    counts = jnp.where(column >= used, 0, counts)
    counts = jnp.where(is_star, TILE, counts)
    seg_tokens = jnp.repeat(tile_seg, TILE, axis=1).reshape(-1).astype(jnp.int32)
    live_tokens = (jnp.arange(TILE)[None, None, :] < counts[:, :, None]).astype(jnp.int32).reshape(-1)
    return (seg_tokens, live_tokens)


def draw_token_seg(key, part):
    return layout_draw(key)[0]


def draw_token_live(key, part):
    return layout_draw(key)[1]


def with_spikes(array, rng, source, target, blocks, factor):
    def block_of(position):
        return (jnp.arange(array.shape[position]) // (array.shape[position] // blocks)).reshape((-1,) + (1,) * (array.ndim - 1 - position))

    first = jax.random.permutation(rng, blocks)[block_of(target)]
    second = (block_of(target) + blocks // 2) % blocks
    return jnp.where((block_of(source) == first) | (block_of(source) == second), factor * array, array)


def steps_of(key, dims, shards, least, largest):
    gain, own = 1.0, jax.random.fold_in(key, 6)
    for dim, parts in shards:
        draws = jnp.exp(jax.random.uniform(jax.random.fold_in(own, dim), (parts,), jnp.float32, least / len(shards), largest / len(shards)))
        gain = gain * jnp.repeat(draws, dims[dim] // parts).reshape([-1 if axis == dim else 1 for axis in range(len(dims))])
    return gain


def noise(key, dims, scale, reach, cuts=(), kind=jnp.bfloat16):
    array = scale * jax.random.normal(key, dims, jnp.float32)
    if cuts:
        array = array * steps_of(key, dims, cuts, -0.22, 0.18)
    return jnp.clip(array, -reach, reach).astype(kind)


def noise_with(rng, shape, scale, bound, shards, heavy, kind=jnp.bfloat16):
    entries = scale * jax.random.normal(rng, shape, jnp.float32)
    if shards:
        entries = entries * steps_of(rng, shape, shards, -0.22, 0.18)
    return jnp.clip(with_spikes(entries, jax.random.fold_in(rng, 3), *heavy), -bound, bound).astype(kind)


def setup_inputs(seed: int = 0) -> dict:
    splits = jax.random.split(jax.random.key(seed), 11)
    return {
        "layer_input": noise(splits[0], (TOKENS, D), 1.0, 6.0, ((0, 32),)),
        "qkv_weight": noise(splits[1], (D, 3 * D), D ** -0.5, 0.21875, ((0, 8),)),
        "attn_weight": noise(splits[2], (D, D), (D // 64) ** -0.5, 1.75, ((0, 8),)),
        "wide_weight": noise(splits[3], (D, 2 * FF), D ** -0.5, 0.21875, ((0, 8),)),
        "narrow_weight": noise(splits[4], (D, FF), (FF // 4) ** -0.5, 0.375, ((0, 8),)),
        "first_gain": jnp.clip(1.0 + 0.18 * jax.random.normal(splits[5], (D,), jnp.float32), 0.099609375, 1.8984375).astype(jnp.bfloat16),
        "second_gain": jnp.clip(1.0 + 0.18 * jax.random.normal(splits[6], (D,), jnp.float32), 0.099609375, 1.8984375).astype(jnp.bfloat16),
        "out_grad": noise_with(splits[7], (TOKENS, D), 1.0, 12.0, ((0, 32),), (0, 1, 32, 2.75)),
        "token_seg": draw_token_seg(jax.random.fold_in(splits[10], 71), 0),
        "token_live": draw_token_live(jax.random.fold_in(splits[10], 71), 0),
    }


rope_base = 160000.0
eps = 1e-05
masked_score = -1e+30
highest = lax.Precision.HIGHEST

@jax.custom_vjp
def low(v):
    return lax.optimization_barrier(v.astype(jnp.bfloat16)).astype(jnp.float32)

@jax.custom_vjp
def low_back(v):
    return v

def low_keep(v):
    return (low(v), None)

def low_pass(kept, grad):
    return (grad,)

def back_keep(v):
    return (v, None)

def back_low(kept, grad):
    return (low(grad),)
low.defvjp(low_keep, low_pass)
low_back.defvjp(back_keep, back_low)

def layer_norm(values, scales):
    center = values - lax.optimization_barrier(jnp.mean(values, axis=-1, keepdims=True))
    spread = lax.optimization_barrier(jnp.mean(center * center, axis=-1, keepdims=True))
    return center * lax.rsqrt(spread + eps) * scales

def rope_tables(seg_rows):
    length = seg_rows.shape[0]
    firsts = seg_rows[::TILE]
    before = lax.optimization_barrier(jnp.sum((firsts[None, :] < seg_rows[:, None]).astype(jnp.int32), axis=1))
    places = jnp.arange(length, dtype=jnp.int32) - TILE * before
    freq_index = jnp.arange(HDIM // 2, dtype=jnp.float32)
    inverse = jnp.exp(freq_index * (-2.0 * math.log(rope_base) / HDIM))
    angles = places.astype(jnp.float32)[:, None] * inverse[None, :]
    angles = jnp.concatenate([angles, angles], axis=1)
    return (jnp.cos(angles)[:, None, :], jnp.sin(angles)[:, None, :])

def rotate(values, cos_tab, sin_tab):
    half_dim = values.shape[-1] // 2
    turned = jnp.concatenate([-values[..., half_dim:], values[..., :half_dim]], axis=-1)
    return values * cos_tab + turned * sin_tab

def buffer_forward(params, rows_in, seg_rows, live_rows):
    qkv_w, attn_w, wide_w, narrow_w, gain_one, gain_two = params
    length = rows_in.shape[0]
    head_count = D // HDIM
    scaling = 1.0 / math.sqrt(HDIM)
    normed_one = low(layer_norm(rows_in, gain_one))
    packed = low_back(jnp.dot(normed_one, qkv_w, precision=highest))
    cos_tab, sin_tab = rope_tables(seg_rows)
    queries = low(rotate(packed[:, :D].reshape(length, head_count, HDIM), cos_tab, sin_tab))
    keyset = low(rotate(packed[:, D:2 * D].reshape(length, head_count, HDIM), cos_tab, sin_tab))
    valueset = low(packed[:, 2 * D:].reshape(length, head_count, HDIM))
    scores = low_back(jnp.einsum('qhd,khd->hqk', queries, keyset, precision=highest) * scaling)
    allowed = (seg_rows[:, None] == seg_rows[None, :]) & (live_rows[None, :] > 0)
    scores = jnp.where(allowed[None], scores, masked_score)
    weights_soft = low(jax.nn.softmax(scores, axis=-1))
    mixed_rows = low(low_back(jnp.einsum('hqk,khd->qhd', weights_soft, valueset, precision=highest).reshape(length, D)))
    middle = rows_in + low_back(jnp.dot(mixed_rows, attn_w, precision=highest))
    normed_two = low(layer_norm(middle, gain_two))
    lifted = low_back(jnp.dot(normed_two, wide_w, precision=highest))
    hidden = low(jax.nn.gelu(lifted[:, :FF], approximate=False) * lifted[:, FF:])
    return middle + low_back(jnp.einsum('tf,df->td', hidden, narrow_w, precision=highest))

def reference(layer_input, qkv_weight, attn_weight, wide_weight, narrow_weight, first_gain, second_gain, out_grad, token_seg, token_live):
    buffers = N_FSDP * N_REP
    inputs_f32 = layer_input.astype(jnp.float32)
    params = tuple((matrix.astype(jnp.float32) for matrix in (qkv_weight, attn_weight, wide_weight, narrow_weight, first_gain, second_gain)))
    seg_blocks = token_seg.reshape(buffers, TOK_DEV)
    live_blocks = token_live.reshape(buffers, TOK_DEV)
    step_fn = jax.checkpoint(buffer_forward)

    def whole(values, weights_all):
        blocks = values.reshape(buffers, TOK_DEV, D)
        outputs = lax.map(lambda triple: step_fn(weights_all, triple[0], triple[1], triple[2]), (blocks, seg_blocks, live_blocks))
        return outputs.reshape(buffers * TOK_DEV, D)
    result, pullback = jax.vjp(whole, inputs_f32, params)
    cotangent = out_grad.astype(jnp.float32) * token_live.astype(jnp.float32)[:, None]
    input_grad, grads = pullback(cotangent)
    return (result.astype(jnp.bfloat16), input_grad, grads[0], grads[1], grads[2], grads[3], grads[4], grads[5])
```

```python
import functools
import math

import jax
import jax.numpy as jnp
import numpy as np
from jax import lax
from jax.experimental import pallas as pl
from jax.experimental.pallas import tpu as pltpu
from jax.sharding import PartitionSpec as P

HDIM = 64
TILE = 128
PAIR = 128
QROWS = 256


rope_base = 160000.0
eps = 1e-05
masked_score = -1e30


def layer_norm(values, scales):
    center = values - jnp.mean(values, axis=-1, keepdims=True)
    spread = jnp.mean(center * center, axis=-1, keepdims=True)
    return center * lax.rsqrt(spread + eps) * scales


def rope_tables(seg_rows):
    length = seg_rows.shape[0]
    firsts = seg_rows[::TILE]
    before = jnp.sum((firsts[None, :] < seg_rows[:, None]).astype(jnp.int32), axis=1)
    places = jnp.arange(length, dtype=jnp.int32) - TILE * before
    freq_index = jnp.arange(HDIM // 2, dtype=jnp.float32)
    inverse = jnp.exp(freq_index * (-2.0 * math.log(rope_base) / HDIM))
    angles = places.astype(jnp.float32)[:, None] * inverse[None, :]
    cosine, sine = jnp.cos(angles), jnp.sin(angles)
    cos_tab = jnp.concatenate([cosine] * 4, axis=1)
    sin_tab = jnp.concatenate([-sine, sine, -sine, sine], axis=1)
    return cos_tab, sin_tab


def mask_columns(seg_rows, live_rows):
    length = seg_rows.shape[0]
    firsts = seg_rows[::TILE]
    same = seg_rows[:, None] == firsts[None, :]
    query_cols = jnp.where(same, 0.0, masked_score)
    key_cols = jnp.where(same, 1.0, 0.0)
    query_cols = jnp.concatenate([query_cols, jnp.ones((length, 1))], axis=1)
    dead = jnp.where(live_rows > 0, 0.0, masked_score)[:, None]
    key_cols = jnp.concatenate([key_cols, dead], axis=1)
    spare = ((0, 0), (0, HDIM - query_cols.shape[1]))
    return (
        jnp.pad(query_cols, spare).astype(jnp.bfloat16),
        jnp.pad(key_cols, spare).astype(jnp.bfloat16),
    )


def swap_halves(values):
    lane = lax.broadcasted_iota(jnp.int32, values.shape, 1)
    return jnp.where(
        lane % HDIM < HDIM // 2,
        pltpu.roll(values, PAIR - HDIM // 2, 1),
        pltpu.roll(values, HDIM // 2, 1),
    )


def rows_dot(left, right):
    return lax.dot_general(left, right, (((1,), (1,)), ((), ())), preferred_element_type=jnp.float32)


def attend_kernel(pq, pk, pv, cos_ref, sin_ref, qm, km, q_out, k_out, v_out, mixed_out, lse_out):
    cos_tab, sin_tab = cos_ref[...], sin_ref[...]
    length = cos_tab.shape[0]
    q_out[...] = ((pq[...] * cos_tab + swap_halves(pq[...]) * sin_tab).astype(jnp.bfloat16)) * 0.125
    k_out[...] = (pk[...] * cos_tab + swap_halves(pk[...]) * sin_tab).astype(jnp.bfloat16)
    v_out[...] = pv[...].astype(jnp.bfloat16)
    flipped = jnp.transpose(v_out[...])
    for begin in range(0, length, QROWS):
        parts = []
        for head in range(PAIR // HDIM):
            cols = slice(head * HDIM, (head + 1) * HDIM)
            keys = jnp.concatenate([k_out[:, cols], km[...]], axis=1)
            rows = jnp.concatenate(
                [q_out[begin : begin + QROWS, cols], qm[begin : begin + QROWS, :]], axis=1
            )
            scores = rows_dot(keys, rows)
            top = jnp.max(scores, axis=0, keepdims=True)
            expo = jnp.exp(scores - top)
            total = jnp.sum(expo, axis=0, keepdims=True)
            lse_out[0, head : head + 1, begin : begin + QROWS] = top + jnp.log(total)
            out = jnp.dot(
                flipped[cols, :], expo.astype(jnp.bfloat16), preferred_element_type=jnp.float32
            )
            parts.append(out / total)
        both = jnp.concatenate(parts, axis=0)
        mixed_out[begin : begin + QROWS, :] = jnp.transpose(both).astype(jnp.bfloat16)


def attend_back_kernel(
    q_ref, k_ref, v_ref, mixed_ref, go_ref, lse_ref, cos_ref, sin_ref, qm, km, gq_out, gk_out, gv_out
):
    cos_tab, sin_tab = cos_ref[...], sin_ref[...]
    length = cos_tab.shape[0]
    product = jnp.transpose(mixed_ref[...].astype(jnp.float32) * go_ref[...].astype(jnp.float32))
    flipped = jnp.transpose(k_ref[...])
    gq_parts, gk_parts, gv_parts = [], [], []
    for head in range(PAIR // HDIM):
        cols = slice(head * HDIM, (head + 1) * HDIM)
        delta = jnp.sum(product[cols, :], axis=0, keepdims=True)
        keys = jnp.concatenate([k_ref[:, cols], km[...]], axis=1)
        values = v_ref[:, cols]
        grad_k = jnp.zeros((length, HDIM), jnp.float32)
        grad_v = jnp.zeros((length, HDIM), jnp.float32)
        grad_q = []
        for begin in range(0, length, QROWS):
            span = slice(begin, begin + QROWS)
            low_q, low_go = q_ref[span, cols], go_ref[span, cols]
            scores = rows_dot(keys, jnp.concatenate([low_q, qm[span, :]], axis=1))
            probs = jnp.exp(scores - lse_ref[0, head : head + 1, span])
            grad_v += jnp.dot(probs.astype(jnp.bfloat16), low_go, preferred_element_type=jnp.float32)
            grad_p = rows_dot(values, low_go)
            grad_s = (probs * (grad_p - delta[:, span])).astype(jnp.bfloat16)
            grad_k += jnp.dot(grad_s, low_q, preferred_element_type=jnp.float32)
            grad_q.append(jnp.dot(flipped[cols, :], grad_s, preferred_element_type=jnp.float32))
        gq_parts.append(jnp.concatenate(grad_q, axis=1))
        gk_parts.append(grad_k)
        gv_parts.append(grad_v)
    grad_q = jnp.transpose(jnp.concatenate(gq_parts, axis=0)) * 0.125
    grad_k = jnp.concatenate(gk_parts, axis=1)
    gq_out[...] = (grad_q * cos_tab + swap_halves(grad_q * sin_tab)).astype(jnp.bfloat16)
    gk_out[...] = (grad_k * cos_tab + swap_halves(grad_k * sin_tab)).astype(jnp.bfloat16)
    gv_out[...] = jnp.concatenate(gv_parts, axis=1).astype(jnp.bfloat16)


def attend(packed, cos_tab, sin_tab, qm, km):
    length, width = packed.shape[0], packed.shape[1] // 3
    pairs = width // PAIR
    block = lambda shift: pl.BlockSpec((length, PAIR), lambda i: (0, i + shift))
    table = pl.BlockSpec((length, PAIR), lambda i: (0, 0))
    mask = pl.BlockSpec((length, HDIM), lambda i: (0, 0))
    rows = jax.ShapeDtypeStruct((length, width), jnp.bfloat16)
    return pl.pallas_call(
        attend_kernel,
        grid=(pairs,),
        in_specs=[block(0), block(pairs), block(2 * pairs), table, table, mask, mask],
        out_specs=[block(0)] * 4 + [pl.BlockSpec((1, 2, length), lambda i: (i, 0, 0))],
        out_shape=[rows] * 4 + [jax.ShapeDtypeStruct((pairs, 2, length), jnp.float32)],
        compiler_params=pltpu.CompilerParams(vmem_limit_bytes=40 << 20),
        cost_estimate=pl.CostEstimate(
            flops=16 * width * length * length, bytes_accessed=20 * length * width,
            transcendentals=pairs * 2 * length * length,
        ),
    )(packed, packed, packed, cos_tab, sin_tab, qm, km)


def attend_back(queries, keyset, valueset, mixed, grad_mixed, lse, cos_tab, sin_tab, qm, km):
    length, width = queries.shape
    pairs = width // PAIR
    block = pl.BlockSpec((length, PAIR), lambda i: (0, i))
    table = pl.BlockSpec((length, PAIR), lambda i: (0, 0))
    mask = pl.BlockSpec((length, HDIM), lambda i: (0, 0))
    rows = jax.ShapeDtypeStruct((length, width), jnp.bfloat16)
    return pl.pallas_call(
        attend_back_kernel,
        grid=(pairs,),
        in_specs=[block] * 5
        + [pl.BlockSpec((1, 2, length), lambda i: (i, 0, 0)), table, table, mask, mask],
        out_specs=[block] * 3,
        out_shape=[rows] * 3,
        compiler_params=pltpu.CompilerParams(vmem_limit_bytes=48 << 20),
        cost_estimate=pl.CostEstimate(
            flops=40 * width * length * length, bytes_accessed=16 * length * width,
            transcendentals=pairs * 2 * length * length,
        ),
    )(queries, keyset, valueset, mixed, grad_mixed, lse, cos_tab, sin_tab, qm, km)


def swap_with(array, axis, bit):
    size = lax.axis_size(axis)
    return lax.ppermute(array, axis, [(i, i ^ (1 << bit)) for i in range(size)])


def side_of(axis, bit):
    return (lax.axis_index(axis) >> bit) & 1


def bits_of(axis):
    return [(axis, bit) for bit in reversed(range(lax.axis_size(axis).bit_length() - 1))]


def gather_half(piece, order):
    canon = bits_of("fsdp") + bits_of("rep")
    have = []
    for axis, bit in order:
        other = swap_with(piece, axis, bit)
        side = side_of(axis, bit) == 0
        place = sum(canon.index(known) < canon.index((axis, bit)) for known in have)
        piece = jnp.stack(
            [jnp.where(side, piece, other), jnp.where(side, other, piece)], axis=place
        )
        have.append((axis, bit))
    return piece.reshape(-1, piece.shape[-1])


def pick(array, dim, side):
    return lax.dynamic_index_in_dim(array, side, dim, keepdims=False)


def orders():
    rep_bits, fsdp_bits = bits_of("rep")[::-1], bits_of("fsdp")[::-1]
    near, far = rep_bits[0], rep_bits[1:]
    one = [near] + far + fsdp_bits
    two = [near] + fsdp_bits[:1] + far + fsdp_bits[1:]
    return one, two


def gather_weights(arrays):
    joint = jnp.concatenate(arrays, axis=1)
    for axis, bit in bits_of("rep"):
        size = joint.shape[0] // 2
        joint = lax.dynamic_slice_in_dim(joint, side_of(axis, bit) * size, size, axis=0)
    cut = joint.shape[1] // 256 * 128
    one, two = orders()
    whole = jnp.concatenate(
        [gather_half(joint[:, :cut], one[::-1]), gather_half(joint[:, cut:], two[::-1])], axis=1
    )
    outs, start = [], 0
    for array in arrays:
        outs.append(whole[:, start : start + array.shape[1]])
        start += array.shape[1]
    return outs


def scatter_half(term, order):
    canon = bits_of("fsdp") + bits_of("rep")
    rows = term.shape[0] >> len(canon)
    acc = term.reshape([2] * len(canon) + [rows, term.shape[1]])
    left = list(canon)
    for axis, bit in order:
        dim = left.index((axis, bit))
        side = side_of(axis, bit)
        other = swap_with(pick(acc, dim, 1 - side), axis, bit)
        acc = pick(acc, dim, side).astype(jnp.float32) + other.astype(jnp.float32)
        acc = acc.astype(jnp.bfloat16)
        left.remove((axis, bit))
    rep_order = [entry for entry in order[::-1] if entry[0] == "rep"]
    have = []
    for axis, bit in rep_order:
        other = swap_with(acc, axis, bit)
        side = side_of(axis, bit) == 0
        place = sum(canon.index(known) < canon.index((axis, bit)) for known in have)
        acc = jnp.stack([jnp.where(side, acc, other), jnp.where(side, other, acc)], axis=place)
        have.append((axis, bit))
    return acc.reshape(-1, acc.shape[-1]).astype(jnp.float32)


def scatter_sums(terms):
    joint = jnp.concatenate([term.astype(jnp.bfloat16) for term in terms], axis=1)
    cut = joint.shape[1] // 256 * 128
    one, two = orders()
    whole = jnp.concatenate(
        [scatter_half(joint[:, :cut], one), scatter_half(joint[:, cut:], two)], axis=1
    )
    outs, start = [], 0
    for term in terms:
        outs.append(whole[:, start : start + term.shape[1]])
        start += term.shape[1]
    return outs


def geglu(lifted):
    half_ff = lifted.shape[1] // 2
    return jax.nn.gelu(lifted[:, :half_ff], approximate=False) * lifted[:, half_ff:]


MESH = pl.DeviceIdType.MESH
HALF = 48
AHEAD = 4
GATHER_LAGS = (3.0 - 2.1 * AHEAD, 3.0, 6.3, 9.5, 11.5)
PACE = 2.1
PAIR_US = 8.0
STEP = 16


def table_constants(length):
    places = np.arange(length, dtype=np.float32)
    freq_index = np.arange(HDIM // 2, dtype=np.float32)
    inverse = np.exp(freq_index * np.float32(-2.0 * math.log(rope_base) / HDIM)).astype(np.float32)
    angles = (places[:, None] * inverse[None, :]).astype(np.float32).astype(np.float64)
    cosine, sine = np.cos(angles), np.sin(angles)
    cos_tab = np.concatenate([cosine] * 4, axis=1).astype(np.float32)
    sin_tab = np.concatenate([-sine, sine, -sine, sine], axis=1).astype(np.float32)
    return cos_tab, sin_tab


class Place:
    def __init__(self):
        self.f = lax.axis_index("fsdp")
        self.r = lax.axis_index("rep")
        self.z = self.f // 2
        self.x = self.f % 2
        self.y = self.r // 2
        self.core = self.r % 2

    def flip(self, value, bit):
        size = 1 << bit
        return value + size - 2 * size * ((value // size) % 2)

    def along_z(self, d):
        z = self.z
        for bit in range(2):
            if (d >> bit) & 1:
                z = self.flip(z, bit)
        return z

    def fsdp_of(self, m):
        f = self.f
        for bit in range(3):
            if (m >> bit) & 1:
                f = self.flip(f, bit)
        return f

    def z_dev(self, d):
        return (2 * self.along_z(d) + self.x, self.r)

    def x_dev(self):
        return (self.flip(self.f, 0), self.r)

    def y_dev(self):
        return (self.f, self.flip(self.r, 1))

    def core_dev(self):
        return (self.f, self.flip(self.r, 0))

    def rows_zx(self):
        return pl.ds(pl.multiple_of(HALF * self.core + STEP * self.y, STEP), 2 * STEP)

    def rows_y(self):
        return pl.ds(pl.multiple_of(HALF * self.core + 2 * STEP * self.y, STEP), STEP)

    def rows_core(self):
        return pl.ds(pl.multiple_of(HALF * self.core, STEP), HALF)


def remote(src, dst, send, recv, dev):
    return pltpu.make_async_remote_copy(
        src_ref=src, dst_ref=dst, send_sem=send, recv_sem=recv, device_id=dev, device_id_type=MESH
    )


def staged(count, lags, pace):
    return sorted((lag + pace * k, stage, k) for stage, lag in enumerate(lags) for k in range(count))


class Gather:
    def __init__(self, place, sources, targets, send, recv, own):
        self.p, self.src, self.dst = place, sources, targets
        self.send, self.recv, self.own = send, recv, own
        self.count = len(sources)

    def z_copy(self, k, d):
        p, rows = self.p, self.p.rows_zx()
        return remote(
            self.src[k].at[rows, :],
            self.dst[k].at[p.z, p.x, rows, :],
            self.send.at[k, d - 1],
            self.recv.at[k, d - 1],
            p.z_dev(d),
        )

    def own_copy(self, k):
        p, rows = self.p, self.p.rows_zx()
        return pltpu.make_async_copy(
            self.src[k].at[rows, :], self.dst[k].at[p.z, p.x, rows, :], self.own.at[k]
        )

    def x_copy(self, k):
        p = self.p
        part = self.dst[k].at[:, p.x, p.rows_zx(), :]
        return remote(part, part, self.send.at[k, 3], self.recv.at[k, 3], p.x_dev())

    def y_copy(self, k):
        p = self.p
        part = self.dst[k].at[:, :, p.rows_y(), :]
        return remote(part, part, self.send.at[k, 4], self.recv.at[k, 4], p.y_dev())

    def core_copy(self, k):
        p = self.p
        part = self.dst[k].at[:, :, p.rows_core(), :]
        return remote(part, part, self.send.at[k, 5], self.recv.at[k, 5], p.core_dev())

    def step(self, stage, k):
        if stage == 0:
            self.own_copy(k).start()
            for d in (1, 2, 3):
                self.z_copy(k, d).start()
        elif stage == 1:
            self.own_copy(k).wait()
            for d in (1, 2, 3):
                self.z_copy(k, d).wait_recv()
            self.x_copy(k).start()
        elif stage == 2:
            self.x_copy(k).wait_recv()
            self.y_copy(k).start()
        elif stage == 3:
            self.y_copy(k).wait_recv()
            self.core_copy(k).start()
        else:
            self.core_copy(k).wait_recv()

    def finish(self):
        for k in range(self.count):
            for d in (1, 2, 3):
                self.z_copy(k, d).wait_send()
            self.x_copy(k).wait_send()
            self.y_copy(k).wait_send()
            self.core_copy(k).wait_send()


def greet(devices):
    barrier = pltpu.get_barrier_semaphore()
    for dev in devices:
        pl.semaphore_signal(barrier, inc=1, device_id=dev, device_id_type=MESH)
    pl.semaphore_wait(barrier, len(devices))


def forward_kernel(
    plan,
    seg_ref,
    x_ref,
    gain_in,
    live_ref,
    cos_in,
    sin_in,
    wq_in,
    wa_in,
    ww_in,
    wn_in,
    q_out,
    k_out,
    v_out,
    mixed_out,
    lse_out,
    normed_out,
    gain_out,
    wq_all,
    wa_all,
    ww_all,
    wn_all,
    cos_tab,
    sin_tab,
    qm,
    km,
    gain_send,
    gain_recv,
    wbuf,
    send,
    recv,
    own,
    gain_send_sem,
    gain_recv_sem,
    load_sem,
):
    i = pl.program_id(0)
    pairs = pl.num_programs(0)
    npairs, cuts = plan
    place = Place()
    length, width = x_ref.shape
    tiles = length // TILE
    sources = [wq_in.at[k] for k in range(npairs)]
    targets = [wq_all.at[k] for k in range(npairs)]
    for cut, shard, full in zip(cuts, (wa_in, ww_in, wn_in), (wa_all, ww_all, wn_all)):
        for lo, size in cut:
            sources.append(shard.at[:, pl.ds(lo, size)])
            targets.append(full.at[:, :, :, pl.ds(lo, size)])
    gather = Gather(place, sources, targets, send, recv, own)

    events = staged(gather.count, GATHER_LAGS, PACE)
    events = [e for e in events if e[1:] not in [(0, k) for k in range(AHEAD)]]

    def run_until(time):
        while events and events[0][0] <= time:
            gather.step(*events.pop(0)[1:])

    def gain_copy(m):
        return remote(
            gain_send,
            gain_recv.at[place.f],
            gain_send_sem.at[m - 1],
            gain_recv_sem.at[m - 1],
            (place.fsdp_of(m), place.r),
        )

    def load(k):
        return pltpu.make_async_copy(wq_all.at[k], wbuf.at[k % 2], load_sem.at[k % 2])

    @pl.when(i == 0)
    def _():
        gain_send[...] = gain_in[...]
        greet(
            [(place.fsdp_of(m), place.r) for m in range(1, 8)] + [place.y_dev(), place.core_dev()]
        )
        for m in range(1, 8):
            gain_copy(m).start()
        for k in range(AHEAD):
            gather.step(0, k)
        gain_recv[place.f] = gain_in[...]
        lane_tile = lax.broadcasted_iota(jnp.int32, (TILE, HDIM), 1)
        live_cols = jnp.transpose(
            jnp.concatenate(
                [live_ref[...].astype(jnp.float32), jnp.zeros((TILE - tiles, TILE), jnp.float32)], axis=0
            )
        )
        segs = [seg_ref[u : u + 1, :] for u in range(tiles)]
        for t in range(tiles):
            rows = slice(t * TILE, (t + 1) * TILE)
            before = jnp.zeros((1, TILE), jnp.int32)
            same = jnp.zeros((TILE, HDIM), jnp.float32)
            for u in range(tiles):
                before += jnp.where(segs[u] < segs[t], 1, 0)
                hit = jnp.where(segs[u] == segs[t], 1.0, 0.0)[:, :HDIM]
                same = jnp.where(lane_tile == u, hit, same)
            cos_t, sin_t = cos_in[:TILE, :], sin_in[:TILE, :]
            for c in range(1, t + 1):
                at = slice(c * TILE, (c + 1) * TILE)
                cos_t = jnp.where(t - before == c, cos_in[at, :], cos_t)
                sin_t = jnp.where(t - before == c, sin_in[at, :], sin_t)
            cos_tab[rows, :] = cos_t
            sin_tab[rows, :] = sin_t
            dead = jnp.where(live_cols[:, t : t + 1] > 0, 0.0, masked_score)
            qv = jnp.where(lane_tile < tiles, jnp.where(same > 0, 0.0, masked_score), 0.0)
            qm[rows, :] = jnp.where(lane_tile == tiles, 1.0, qv).astype(jnp.bfloat16)
            kv = jnp.where(lane_tile == tiles, dead, same)
            km[rows, :] = kv.astype(jnp.bfloat16)
        run_until(3.0)
        for m in range(1, 8):
            gain_copy(m).wait()
        part = width // 8
        wide_row = lax.broadcasted_iota(jnp.int32, (PAIR, width), 0)
        wide_col = lax.broadcasted_iota(jnp.int32, (PAIR, width), 1)
        gains = jnp.zeros((8, width), jnp.float32)
        for f in range(8):
            pick_f = jnp.where((wide_col == wide_row + f * part) & (wide_row < part), 1.0, 0.0)
            gains += jnp.dot(
                gain_recv[f].astype(jnp.bfloat16),
                pick_f.astype(jnp.bfloat16),
                preferred_element_type=jnp.float32,
            )
        gain_out[...] = gains
        run_until(6.4)

        def norm_rows(b, carry):
            rows = pl.ds(pl.multiple_of(b * TILE, TILE), TILE)
            v = x_ref[rows, :].astype(jnp.float32)
            c = v - jnp.mean(v, axis=1, keepdims=True)
            spread = jnp.mean(c * c, axis=1, keepdims=True)
            normed_out[rows, :] = (c * lax.rsqrt(spread + eps) * gain_out[0:1, :]).astype(jnp.bfloat16)
            return carry

        lax.fori_loop(0, tiles, norm_rows, 0)
        run_until(GATHER_LAGS[4])
        load(0).start()
        load(0).wait()

    packed = jnp.dot(
        normed_out[...],
        wbuf[i % 2].reshape(width, 3 * PAIR),
        preferred_element_type=jnp.float32,
    )
    pq, pk, pv = packed[:, :PAIR], packed[:, PAIR : 2 * PAIR], packed[:, 2 * PAIR :]
    cos_v, sin_v = cos_tab[...], sin_tab[...]
    q_out[...] = ((pq * cos_v + swap_halves(pq) * sin_v).astype(jnp.bfloat16)) * 0.125
    k_out[...] = (pk * cos_v + swap_halves(pk) * sin_v).astype(jnp.bfloat16)
    v_out[...] = pv.astype(jnp.bfloat16)
    flipped = jnp.transpose(v_out[...])

    slots = length // QROWS
    queue = [[[] for _ in range(slots)] for _ in range(npairs)]
    for p in range(npairs):
        for slot in range(slots):
            now = GATHER_LAGS[4] + PAIR_US * (p + (slot + 1) / slots)
            while events and events[0][0] <= now:
                queue[p][slot].append(events.pop(0)[1:])
    queue[-1][-1].extend(e[1:] for e in events)
    for slot, begin in enumerate(range(0, length, QROWS)):
        for p in range(npairs):

            @pl.when(i == p)
            def _():
                for stage, k in queue[p][slot]:
                    gather.step(stage, k)
                if p + 1 < npairs and slot == slots - 2:
                    load(p + 1).start()
                if p + 1 < npairs and slot == slots - 1:
                    load(p + 1).wait()

        parts = []
        for head in range(PAIR // HDIM):
            cols = slice(head * HDIM, (head + 1) * HDIM)
            keys = jnp.concatenate([k_out[:, cols], km[...]], axis=1)
            rows = jnp.concatenate(
                [q_out[begin : begin + QROWS, cols], qm[begin : begin + QROWS, :]], axis=1
            )
            scores = rows_dot(keys, rows)
            top = jnp.max(scores, axis=0, keepdims=True)
            expo = jnp.exp(scores - top)
            total = jnp.sum(expo, axis=0, keepdims=True)
            lse_out[0, head : head + 1, begin : begin + QROWS] = top + jnp.log(total)
            out = jnp.dot(
                flipped[cols, :], expo.astype(jnp.bfloat16), preferred_element_type=jnp.float32
            )
            parts.append(out / total)
        both = jnp.concatenate(parts, axis=0)
        mixed_out[begin : begin + QROWS, :] = jnp.transpose(both).astype(jnp.bfloat16)

    @pl.when(i == pairs - 1)
    def _():
        gather.finish()


def cuts_of(width, piece):
    return [(lo, min(piece, width - lo)) for lo in range(0, width, piece)]


def forward(layer_input, wq_in, attn_weight, wide_weight, narrow_weight, gain_in, token_seg, token_live):
    length, width = layer_input.shape
    pairs = width // PAIR
    part = attn_weight.shape[0]
    cos_c, sin_c = table_constants(length)
    cuts = [cuts_of(w.shape[1], 3 * PAIR) for w in (attn_weight, wide_weight, narrow_weight)]
    count = pairs + sum(len(c) for c in cuts)
    block = pl.BlockSpec((length, PAIR), lambda i: (0, i))
    whole = pl.BlockSpec(memory_space=pltpu.VMEM)
    hbm = pl.BlockSpec(memory_space=pl.ANY)
    rows = jax.ShapeDtypeStruct((length, width), jnp.bfloat16)
    full = lambda cols: jax.ShapeDtypeStruct((4, 2, part, cols), jnp.bfloat16)
    return pl.pallas_call(
        functools.partial(forward_kernel, (pairs, cuts)),
        grid=(pairs,),
        in_specs=[whole] * 6 + [hbm] * 4,
        out_specs=[block] * 4
        + [pl.BlockSpec((1, 2, length), lambda i: (i, 0, 0)), whole, whole]
        + [hbm] * 4,
        out_shape=[rows] * 4
        + [
            jax.ShapeDtypeStruct((pairs, 2, length), jnp.float32),
            rows,
            jax.ShapeDtypeStruct((8, width), jnp.float32),
            jax.ShapeDtypeStruct((pairs, 4, 2, part, 3 * PAIR), jnp.bfloat16),
            full(width),
            full(wide_weight.shape[1]),
            full(narrow_weight.shape[1]),
        ],
        scratch_shapes=[
            pltpu.VMEM((length, PAIR), jnp.float32),
            pltpu.VMEM((length, PAIR), jnp.float32),
            pltpu.VMEM((length, HDIM), jnp.bfloat16),
            pltpu.VMEM((length, HDIM), jnp.bfloat16),
            pltpu.VMEM((8, PAIR), jnp.float32),
            pltpu.VMEM((8, 8, PAIR), jnp.float32),
            pltpu.VMEM((2, 4, 2, part, 3 * PAIR), jnp.bfloat16),
            pltpu.SemaphoreType.DMA((count, 6)),
            pltpu.SemaphoreType.DMA((count, 6)),
            pltpu.SemaphoreType.DMA((count,)),
            pltpu.SemaphoreType.DMA((7,)),
            pltpu.SemaphoreType.DMA((7,)),
            pltpu.SemaphoreType.DMA((2,)),
        ],
        compiler_params=pltpu.CompilerParams(
            vmem_limit_bytes=56 << 20, collective_id=0, has_side_effects=True
        ),
        cost_estimate=pl.CostEstimate(
            flops=22 * width * length * length, bytes_accessed=40 * length * width,
            transcendentals=pairs * 2 * length * length,
        ),
    )(
        token_seg.reshape(length // TILE, TILE), layer_input, gain_in,
        token_live.reshape(length // TILE, TILE),
        jnp.asarray(cos_c), jnp.asarray(sin_c), wq_in, attn_weight, wide_weight, narrow_weight,
    )


def on_device(
    layer_input,
    qkv_weight,
    attn_weight,
    wide_weight,
    narrow_weight,
    first_gain,
    second_gain,
    out_grad,
    token_seg,
    token_live,
):
    gains = jnp.stack([first_gain, second_gain], axis=1)
    gains = jnp.pad(gains, ((0, 0), (0, PAIR - 2)))
    qkv_full, gains = gather_weights([qkv_weight, gains])
    attn_full, wide_full, narrow_full = gather_weights([attn_weight, wide_weight, narrow_weight])
    scale_one = gains[:, 0].astype(jnp.float32)
    scale_two = gains[:, 1].astype(jnp.float32)
    residual_in = layer_input.astype(jnp.float32)
    qm, km = mask_columns(token_seg, token_live)
    cos_tab, sin_tab = rope_tables(token_seg)
    normed_one = layer_norm(residual_in, scale_one).astype(jnp.bfloat16)
    packed = jnp.dot(normed_one, qkv_full, preferred_element_type=jnp.float32)
    queries, keyset, valueset, mixed_rows, lse = attend(packed, cos_tab, sin_tab, qm, km)
    middle = residual_in + jnp.dot(mixed_rows, attn_full, preferred_element_type=jnp.float32)
    normed_two = layer_norm(middle, scale_two).astype(jnp.bfloat16)
    lifted = jnp.dot(normed_two, wide_full, preferred_element_type=jnp.float32)
    hidden = geglu(lifted).astype(jnp.bfloat16)
    layer_out = middle + jnp.einsum(
        "tf,df->td", hidden, narrow_full, preferred_element_type=jnp.float32
    )
    grad_top = out_grad.astype(jnp.float32) * token_live.astype(jnp.float32)[:, None]
    grad_top_low = grad_top.astype(jnp.bfloat16)
    narrow_term = jnp.einsum("td,tf->df", grad_top_low, hidden, preferred_element_type=jnp.float32)
    grad_hidden = jnp.dot(grad_top_low, narrow_full, preferred_element_type=jnp.float32)
    _, pull_gate = jax.vjp(geglu, lifted)
    grad_lifted = pull_gate(grad_hidden)[0].astype(jnp.bfloat16)
    wide_term = jnp.einsum("td,tf->df", normed_two, grad_lifted, preferred_element_type=jnp.float32)
    grad_norm_two = jnp.einsum(
        "tf,df->td", grad_lifted, wide_full, preferred_element_type=jnp.float32
    )
    _, pull_two = jax.vjp(layer_norm, middle, scale_two)
    grad_mid_ln, second_term = pull_two(grad_norm_two)
    grad_middle = grad_top + grad_mid_ln
    grad_middle_low = grad_middle.astype(jnp.bfloat16)
    attn_term = jnp.einsum(
        "td,te->de", mixed_rows, grad_middle_low, preferred_element_type=jnp.float32
    )
    grad_mixed = jnp.einsum(
        "te,de->td", grad_middle_low, attn_full, preferred_element_type=jnp.float32
    )
    shares = scatter_sums([narrow_term, wide_term, attn_term])
    grad_parts = attend_back(
        queries, keyset, valueset, mixed_rows, grad_mixed.astype(jnp.bfloat16), lse,
        cos_tab, sin_tab, qm, km,
    )
    grad_packed = jnp.concatenate(grad_parts, axis=1)
    qkv_term = jnp.einsum("td,tf->df", normed_one, grad_packed, preferred_element_type=jnp.float32)
    grad_norm_one = jnp.einsum(
        "tf,df->td", grad_packed, qkv_full, preferred_element_type=jnp.float32
    )
    _, pull_one = jax.vjp(layer_norm, residual_in, scale_one)
    grad_in_ln, first_term = pull_one(grad_norm_one)
    input_grad = grad_middle + grad_in_ln
    gain_terms = jnp.stack([first_term, second_term], axis=1)
    gain_terms = jnp.pad(gain_terms, ((0, 0), (0, PAIR - 2)))
    qkv_share, gain_share = scatter_sums([qkv_term, gain_terms])
    return (
        layer_out.astype(jnp.bfloat16),
        input_grad,
        qkv_share,
        shares[2],
        shares[1],
        shares[0],
        gain_share[:, 0],
        gain_share[:, 1],
    )


def on_device_tuned(
    layer_input,
    qkv_weight,
    attn_weight,
    wide_weight,
    narrow_weight,
    first_gain,
    second_gain,
    out_grad,
    token_seg,
    token_live,
):
    length, width = layer_input.shape
    pairs, part = width // PAIR, attn_weight.shape[0]
    wq_in = qkv_weight.reshape(part, 3, pairs, PAIR).transpose(2, 0, 1, 3).reshape(pairs, part, 3 * PAIR)
    gain_in = jnp.pad(jnp.stack([first_gain, second_gain]).astype(jnp.float32), ((0, 6), (0, PAIR - part)))
    (queries, keyset, valueset, mixed_rows, lse, normed_one, gains, wq_all, wa_all, ww_all, wn_all) = forward(
        layer_input, wq_in, attn_weight, wide_weight, narrow_weight, gain_in, token_seg, token_live
    )
    scale_one, scale_two = gains[0], gains[1]
    attn_full, wide_full, narrow_full = (w.reshape(width, w.shape[-1]) for w in (wa_all, ww_all, wn_all))
    qkv_full = wq_all.reshape(pairs, width, 3, PAIR).transpose(1, 2, 0, 3).reshape(width, 3 * width)
    residual_in = layer_input.astype(jnp.float32)
    qm, km = mask_columns(token_seg, token_live)
    cos_tab, sin_tab = rope_tables(token_seg)
    middle = residual_in + jnp.dot(mixed_rows, attn_full, preferred_element_type=jnp.float32)
    normed_two = layer_norm(middle, scale_two).astype(jnp.bfloat16)
    lifted = jnp.dot(normed_two, wide_full, preferred_element_type=jnp.float32)
    hidden = geglu(lifted).astype(jnp.bfloat16)
    layer_out = middle + jnp.einsum(
        "tf,df->td", hidden, narrow_full, preferred_element_type=jnp.float32
    )
    grad_top = out_grad.astype(jnp.float32) * token_live.astype(jnp.float32)[:, None]
    grad_top_low = grad_top.astype(jnp.bfloat16)
    narrow_term = jnp.einsum("td,tf->df", grad_top_low, hidden, preferred_element_type=jnp.float32)
    grad_hidden = jnp.dot(grad_top_low, narrow_full, preferred_element_type=jnp.float32)
    _, pull_gate = jax.vjp(geglu, lifted)
    grad_lifted = pull_gate(grad_hidden)[0].astype(jnp.bfloat16)
    wide_term = jnp.einsum("td,tf->df", normed_two, grad_lifted, preferred_element_type=jnp.float32)
    grad_norm_two = jnp.einsum(
        "tf,df->td", grad_lifted, wide_full, preferred_element_type=jnp.float32
    )
    _, pull_two = jax.vjp(layer_norm, middle, scale_two)
    grad_mid_ln, second_term = pull_two(grad_norm_two)
    grad_middle = grad_top + grad_mid_ln
    grad_middle_low = grad_middle.astype(jnp.bfloat16)
    attn_term = jnp.einsum(
        "td,te->de", mixed_rows, grad_middle_low, preferred_element_type=jnp.float32
    )
    grad_mixed = jnp.einsum(
        "te,de->td", grad_middle_low, attn_full, preferred_element_type=jnp.float32
    )
    shares = scatter_sums([narrow_term, wide_term, attn_term])
    grad_parts = attend_back(
        queries, keyset, valueset, mixed_rows, grad_mixed.astype(jnp.bfloat16), lse,
        cos_tab, sin_tab, qm, km,
    )
    grad_packed = jnp.concatenate(grad_parts, axis=1)
    qkv_term = jnp.einsum("td,tf->df", normed_one, grad_packed, preferred_element_type=jnp.float32)
    grad_norm_one = jnp.einsum(
        "tf,df->td", grad_packed, qkv_full, preferred_element_type=jnp.float32
    )
    _, pull_one = jax.vjp(layer_norm, residual_in, scale_one)
    grad_in_ln, first_term = pull_one(grad_norm_one)
    input_grad = grad_middle + grad_in_ln
    gain_terms = jnp.stack([first_term, second_term], axis=1)
    gain_terms = jnp.pad(gain_terms, ((0, 0), (0, PAIR - 2)))
    qkv_share, gain_share = scatter_sums([qkv_term, gain_terms])
    return (
        layer_out.astype(jnp.bfloat16),
        input_grad,
        qkv_share,
        shares[2],
        shares[1],
        shares[0],
        gain_share[:, 0],
        gain_share[:, 1],
    )


def solution(mesh):
    tuned = mesh.shape["fsdp"] == 8 and mesh.shape["rep"] == 4
    return jax.shard_map(
        on_device_tuned if tuned else on_device,
        mesh=mesh,
        in_specs=(
            P(("fsdp", "rep"), None),
            P("fsdp", None),
            P("fsdp", None),
            P("fsdp", None),
            P("fsdp", None),
            P("fsdp"),
            P("fsdp"),
            P(("fsdp", "rep"), None),
            P(("fsdp", "rep")),
            P(("fsdp", "rep")),
        ),
        out_specs=(
            P(("fsdp", "rep"), None),
            P(("fsdp", "rep"), None),
            P("fsdp", None),
            P("fsdp", None),
            P("fsdp", None),
            P("fsdp", None),
            P("fsdp"),
            P("fsdp"),
        ),
        check_vma=False,
    )
```

```python
import functools
import math

import jax
import jax.numpy as jnp
import numpy as np
from jax import lax
from jax.experimental import pallas as pl
from jax.experimental.pallas import tpu as pltpu
from jax.sharding import PartitionSpec as P

HDIM = 64
TILE = 128
PAIR = 128
QROWS = 256


rope_base = 160000.0
eps = 1e-05
masked_score = -1e30


def layer_norm(values, scales):
    center = values - jnp.mean(values, axis=-1, keepdims=True)
    spread = jnp.mean(center * center, axis=-1, keepdims=True)
    return center * lax.rsqrt(spread + eps) * scales


def rope_tables(seg_rows):
    length = seg_rows.shape[0]
    firsts = seg_rows[::TILE]
    before = jnp.sum((firsts[None, :] < seg_rows[:, None]).astype(jnp.int32), axis=1)
    places = jnp.arange(length, dtype=jnp.int32) - TILE * before
    freq_index = jnp.arange(HDIM // 2, dtype=jnp.float32)
    inverse = jnp.exp(freq_index * (-2.0 * math.log(rope_base) / HDIM))
    angles = places.astype(jnp.float32)[:, None] * inverse[None, :]
    cosine, sine = jnp.cos(angles), jnp.sin(angles)
    cos_tab = jnp.concatenate([cosine] * 4, axis=1)
    sin_tab = jnp.concatenate([-sine, sine, -sine, sine], axis=1)
    return cos_tab, sin_tab


def mask_columns(seg_rows, live_rows):
    length = seg_rows.shape[0]
    firsts = seg_rows[::TILE]
    same = seg_rows[:, None] == firsts[None, :]
    query_cols = jnp.where(same, 0.0, masked_score)
    key_cols = jnp.where(same, 1.0, 0.0)
    query_cols = jnp.concatenate([query_cols, jnp.ones((length, 1))], axis=1)
    dead = jnp.where(live_rows > 0, 0.0, masked_score)[:, None]
    key_cols = jnp.concatenate([key_cols, dead], axis=1)
    spare = ((0, 0), (0, HDIM - query_cols.shape[1]))
    return (
        jnp.pad(query_cols, spare).astype(jnp.bfloat16),
        jnp.pad(key_cols, spare).astype(jnp.bfloat16),
    )


def swap_halves(values):
    lane = lax.broadcasted_iota(jnp.int32, values.shape, 1)
    return jnp.where(
        lane % HDIM < HDIM // 2,
        pltpu.roll(values, PAIR - HDIM // 2, 1),
        pltpu.roll(values, HDIM // 2, 1),
    )


def rows_dot(left, right):
    return lax.dot_general(left, right, (((1,), (1,)), ((), ())), preferred_element_type=jnp.float32)


def attend_kernel(pq, pk, pv, cos_ref, sin_ref, qm, km, q_out, k_out, v_out, mixed_out, lse_out):
    cos_tab, sin_tab = cos_ref[...], sin_ref[...]
    length = cos_tab.shape[0]
    q_out[...] = ((pq[...] * cos_tab + swap_halves(pq[...]) * sin_tab).astype(jnp.bfloat16)) * 0.125
    k_out[...] = (pk[...] * cos_tab + swap_halves(pk[...]) * sin_tab).astype(jnp.bfloat16)
    v_out[...] = pv[...].astype(jnp.bfloat16)
    flipped = jnp.transpose(v_out[...])
    for begin in range(0, length, QROWS):
        parts = []
        for head in range(PAIR // HDIM):
            cols = slice(head * HDIM, (head + 1) * HDIM)
            keys = jnp.concatenate([k_out[:, cols], km[...]], axis=1)
            rows = jnp.concatenate(
                [q_out[begin : begin + QROWS, cols], qm[begin : begin + QROWS, :]], axis=1
            )
            scores = rows_dot(keys, rows)
            top = jnp.max(scores, axis=0, keepdims=True)
            expo = jnp.exp(scores - top)
            total = jnp.sum(expo, axis=0, keepdims=True)
            lse_out[0, head : head + 1, begin : begin + QROWS] = top + jnp.log(total)
            out = jnp.dot(
                flipped[cols, :], expo.astype(jnp.bfloat16), preferred_element_type=jnp.float32
            )
            parts.append(out / total)
        both = jnp.concatenate(parts, axis=0)
        mixed_out[begin : begin + QROWS, :] = jnp.transpose(both).astype(jnp.bfloat16)


def attend_back_kernel(
    q_ref, k_ref, v_ref, mixed_ref, go_ref, lse_ref, cos_ref, sin_ref, qm, km, gq_out, gk_out, gv_out
):
    cos_tab, sin_tab = cos_ref[...], sin_ref[...]
    length = cos_tab.shape[0]
    product = jnp.transpose(mixed_ref[...].astype(jnp.float32) * go_ref[...].astype(jnp.float32))
    flipped = jnp.transpose(k_ref[...])
    gq_parts, gk_parts, gv_parts = [], [], []
    for head in range(PAIR // HDIM):
        cols = slice(head * HDIM, (head + 1) * HDIM)
        delta = jnp.sum(product[cols, :], axis=0, keepdims=True)
        keys = jnp.concatenate([k_ref[:, cols], km[...]], axis=1)
        values = v_ref[:, cols]
        grad_k = jnp.zeros((length, HDIM), jnp.float32)
        grad_v = jnp.zeros((length, HDIM), jnp.float32)
        grad_q = []
        for begin in range(0, length, QROWS):
            span = slice(begin, begin + QROWS)
            low_q, low_go = q_ref[span, cols], go_ref[span, cols]
            scores = rows_dot(keys, jnp.concatenate([low_q, qm[span, :]], axis=1))
            probs = jnp.exp(scores - lse_ref[0, head : head + 1, span])
            grad_v += jnp.dot(probs.astype(jnp.bfloat16), low_go, preferred_element_type=jnp.float32)
            grad_p = rows_dot(values, low_go)
            grad_s = (probs * (grad_p - delta[:, span])).astype(jnp.bfloat16)
            grad_k += jnp.dot(grad_s, low_q, preferred_element_type=jnp.float32)
            grad_q.append(jnp.dot(flipped[cols, :], grad_s, preferred_element_type=jnp.float32))
        gq_parts.append(jnp.concatenate(grad_q, axis=1))
        gk_parts.append(grad_k)
        gv_parts.append(grad_v)
    grad_q = jnp.transpose(jnp.concatenate(gq_parts, axis=0)) * 0.125
    grad_k = jnp.concatenate(gk_parts, axis=1)
    gq_out[...] = (grad_q * cos_tab + swap_halves(grad_q * sin_tab)).astype(jnp.bfloat16)
    gk_out[...] = (grad_k * cos_tab + swap_halves(grad_k * sin_tab)).astype(jnp.bfloat16)
    gv_out[...] = jnp.concatenate(gv_parts, axis=1).astype(jnp.bfloat16)


def attend(packed, cos_tab, sin_tab, qm, km):
    length, width = packed.shape[0], packed.shape[1] // 3
    pairs = width // PAIR
    block = lambda shift: pl.BlockSpec((length, PAIR), lambda i: (0, i + shift))
    table = pl.BlockSpec((length, PAIR), lambda i: (0, 0))
    mask = pl.BlockSpec((length, HDIM), lambda i: (0, 0))
    rows = jax.ShapeDtypeStruct((length, width), jnp.bfloat16)
    return pl.pallas_call(
        attend_kernel,
        grid=(pairs,),
        in_specs=[block(0), block(pairs), block(2 * pairs), table, table, mask, mask],
        out_specs=[block(0)] * 4 + [pl.BlockSpec((1, 2, length), lambda i: (i, 0, 0))],
        out_shape=[rows] * 4 + [jax.ShapeDtypeStruct((pairs, 2, length), jnp.float32)],
        compiler_params=pltpu.CompilerParams(vmem_limit_bytes=40 << 20),
        cost_estimate=pl.CostEstimate(
            flops=16 * width * length * length, bytes_accessed=20 * length * width,
            transcendentals=pairs * 2 * length * length,
        ),
    )(packed, packed, packed, cos_tab, sin_tab, qm, km)


def attend_back(queries, keyset, valueset, mixed, grad_mixed, lse, cos_tab, sin_tab, qm, km):
    length, width = queries.shape
    pairs = width // PAIR
    block = pl.BlockSpec((length, PAIR), lambda i: (0, i))
    table = pl.BlockSpec((length, PAIR), lambda i: (0, 0))
    mask = pl.BlockSpec((length, HDIM), lambda i: (0, 0))
    rows = jax.ShapeDtypeStruct((length, width), jnp.bfloat16)
    return pl.pallas_call(
        attend_back_kernel,
        grid=(pairs,),
        in_specs=[block] * 5
        + [pl.BlockSpec((1, 2, length), lambda i: (i, 0, 0)), table, table, mask, mask],
        out_specs=[block] * 3,
        out_shape=[rows] * 3,
        compiler_params=pltpu.CompilerParams(vmem_limit_bytes=48 << 20),
        cost_estimate=pl.CostEstimate(
            flops=40 * width * length * length, bytes_accessed=16 * length * width,
            transcendentals=pairs * 2 * length * length,
        ),
    )(queries, keyset, valueset, mixed, grad_mixed, lse, cos_tab, sin_tab, qm, km)


def swap_with(array, axis, bit):
    size = lax.axis_size(axis)
    return lax.ppermute(array, axis, [(i, i ^ (1 << bit)) for i in range(size)])


def side_of(axis, bit):
    return (lax.axis_index(axis) >> bit) & 1


def bits_of(axis):
    return [(axis, bit) for bit in reversed(range(lax.axis_size(axis).bit_length() - 1))]


def gather_half(piece, order):
    canon = bits_of("fsdp") + bits_of("rep")
    have = []
    for axis, bit in order:
        other = swap_with(piece, axis, bit)
        side = side_of(axis, bit) == 0
        place = sum(canon.index(known) < canon.index((axis, bit)) for known in have)
        piece = jnp.stack(
            [jnp.where(side, piece, other), jnp.where(side, other, piece)], axis=place
        )
        have.append((axis, bit))
    return piece.reshape(-1, piece.shape[-1])


def pick(array, dim, side):
    return lax.dynamic_index_in_dim(array, side, dim, keepdims=False)


def orders():
    rep_bits, fsdp_bits = bits_of("rep")[::-1], bits_of("fsdp")[::-1]
    near, far = rep_bits[0], rep_bits[1:]
    one = [near] + far + fsdp_bits
    two = [near] + fsdp_bits[:1] + far + fsdp_bits[1:]
    return one, two


def gather_weights(arrays):
    joint = jnp.concatenate(arrays, axis=1)
    for axis, bit in bits_of("rep"):
        size = joint.shape[0] // 2
        joint = lax.dynamic_slice_in_dim(joint, side_of(axis, bit) * size, size, axis=0)
    cut = joint.shape[1] // 256 * 128
    one, two = orders()
    whole = jnp.concatenate(
        [gather_half(joint[:, :cut], one[::-1]), gather_half(joint[:, cut:], two[::-1])], axis=1
    )
    outs, start = [], 0
    for array in arrays:
        outs.append(whole[:, start : start + array.shape[1]])
        start += array.shape[1]
    return outs


def scatter_half(term, order):
    canon = bits_of("fsdp") + bits_of("rep")
    rows = term.shape[0] >> len(canon)
    acc = term.reshape([2] * len(canon) + [rows, term.shape[1]])
    left = list(canon)
    for axis, bit in order:
        dim = left.index((axis, bit))
        side = side_of(axis, bit)
        other = swap_with(pick(acc, dim, 1 - side), axis, bit)
        acc = pick(acc, dim, side).astype(jnp.float32) + other.astype(jnp.float32)
        acc = acc.astype(jnp.bfloat16)
        left.remove((axis, bit))
    rep_order = [entry for entry in order[::-1] if entry[0] == "rep"]
    have = []
    for axis, bit in rep_order:
        other = swap_with(acc, axis, bit)
        side = side_of(axis, bit) == 0
        place = sum(canon.index(known) < canon.index((axis, bit)) for known in have)
        acc = jnp.stack([jnp.where(side, acc, other), jnp.where(side, other, acc)], axis=place)
        have.append((axis, bit))
    return acc.reshape(-1, acc.shape[-1]).astype(jnp.float32)


def scatter_sums(terms):
    joint = jnp.concatenate([term.astype(jnp.bfloat16) for term in terms], axis=1)
    cut = joint.shape[1] // 256 * 128
    one, two = orders()
    whole = jnp.concatenate(
        [scatter_half(joint[:, :cut], one), scatter_half(joint[:, cut:], two)], axis=1
    )
    outs, start = [], 0
    for term in terms:
        outs.append(whole[:, start : start + term.shape[1]])
        start += term.shape[1]
    return outs


def geglu(lifted):
    half_ff = lifted.shape[1] // 2
    return jax.nn.gelu(lifted[:, :half_ff], approximate=False) * lifted[:, half_ff:]


MESH = pl.DeviceIdType.MESH
HALF = 48
AHEAD = 4
GATHER_LAGS = (3.0 - 2.1 * AHEAD, 3.0, 7.5, 12.0, 15.0)
PACE = 2.1
PAIR_US = 6.0
STEP = 16


def table_constants(length):
    places = np.arange(length, dtype=np.float32)
    freq_index = np.arange(HDIM // 2, dtype=np.float32)
    inverse = np.exp(freq_index * np.float32(-2.0 * math.log(rope_base) / HDIM)).astype(np.float32)
    angles = (places[:, None] * inverse[None, :]).astype(np.float32).astype(np.float64)
    cosine, sine = np.cos(angles), np.sin(angles)
    cos_tab = np.concatenate([cosine] * 4, axis=1).astype(np.float32)
    sin_tab = np.concatenate([-sine, sine, -sine, sine], axis=1).astype(np.float32)
    return cos_tab, sin_tab


class Place:
    def __init__(self):
        self.f = lax.axis_index("fsdp")
        self.r = lax.axis_index("rep")
        self.z = self.f // 2
        self.x = self.f % 2
        self.y = self.r // 2
        self.core = self.r % 2

    def flip(self, value, bit):
        size = 1 << bit
        return value + size - 2 * size * ((value // size) % 2)

    def along_z(self, d):
        z = self.z
        for bit in range(2):
            if (d >> bit) & 1:
                z = self.flip(z, bit)
        return z

    def fsdp_of(self, m):
        f = self.f
        for bit in range(3):
            if (m >> bit) & 1:
                f = self.flip(f, bit)
        return f

    def z_dev(self, d):
        return (2 * self.along_z(d) + self.x, self.r)

    def x_dev(self):
        return (self.flip(self.f, 0), self.r)

    def y_dev(self):
        return (self.f, self.flip(self.r, 1))

    def core_dev(self):
        return (self.f, self.flip(self.r, 0))

    def rows_zx(self):
        return pl.ds(pl.multiple_of(HALF * self.core + STEP * self.y, STEP), 2 * STEP)

    def rows_y(self):
        return pl.ds(pl.multiple_of(HALF * self.core + 2 * STEP * self.y, STEP), STEP)

    def rows_core(self):
        return pl.ds(pl.multiple_of(HALF * self.core, STEP), HALF)


def remote(src, dst, send, recv, dev):
    return pltpu.make_async_remote_copy(
        src_ref=src, dst_ref=dst, send_sem=send, recv_sem=recv, device_id=dev, device_id_type=MESH
    )


def staged(count, lags, pace):
    return sorted((lag + pace * k, stage, k) for stage, lag in enumerate(lags) for k in range(count))


class Gather:
    def __init__(self, place, sources, targets, send, recv, own):
        self.p, self.src, self.dst = place, sources, targets
        self.send, self.recv, self.own = send, recv, own
        self.count = len(sources)

    def z_copy(self, k, d):
        p, rows = self.p, self.p.rows_zx()
        return remote(
            self.src[k].at[rows, :],
            self.dst[k].at[p.z, p.x, rows, :],
            self.send.at[k, d - 1],
            self.recv.at[k, d - 1],
            p.z_dev(d),
        )

    def own_copy(self, k):
        p, rows = self.p, self.p.rows_zx()
        return pltpu.make_async_copy(
            self.src[k].at[rows, :], self.dst[k].at[p.z, p.x, rows, :], self.own.at[k]
        )

    def x_copy(self, k):
        p = self.p
        part = self.dst[k].at[:, p.x, p.rows_zx(), :]
        return remote(part, part, self.send.at[k, 3], self.recv.at[k, 3], p.x_dev())

    def y_copy(self, k):
        p = self.p
        part = self.dst[k].at[:, :, p.rows_y(), :]
        return remote(part, part, self.send.at[k, 4], self.recv.at[k, 4], p.y_dev())

    def core_copy(self, k):
        p = self.p
        part = self.dst[k].at[:, :, p.rows_core(), :]
        return remote(part, part, self.send.at[k, 5], self.recv.at[k, 5], p.core_dev())

    def step(self, stage, k):
        if stage == 0:
            self.own_copy(k).start()
            for d in (1, 2, 3):
                self.z_copy(k, d).start()
        elif stage == 1:
            self.own_copy(k).wait()
            for d in (1, 2, 3):
                self.z_copy(k, d).wait_recv()
            self.x_copy(k).start()
        elif stage == 2:
            self.x_copy(k).wait_recv()
            self.y_copy(k).start()
        elif stage == 3:
            self.y_copy(k).wait_recv()
            self.core_copy(k).start()
        else:
            self.core_copy(k).wait_recv()

    def finish(self):
        for k in range(self.count):
            for d in (1, 2, 3):
                self.z_copy(k, d).wait_send()
            self.x_copy(k).wait_send()
            self.y_copy(k).wait_send()
            self.core_copy(k).wait_send()


def greet(devices):
    barrier = pltpu.get_barrier_semaphore()
    for dev in devices:
        pl.semaphore_signal(barrier, inc=1, device_id=dev, device_id_type=MESH)
    pl.semaphore_wait(barrier, len(devices))


def forward_kernel(
    plan,
    seg_ref,
    x_ref,
    gain_in,
    live_ref,
    cos_in,
    sin_in,
    wq_in,
    wa_in,
    ww_in,
    wn_in,
    q_out,
    k_out,
    v_out,
    mixed_out,
    lse_out,
    normed_out,
    gain_out,
    wq_all,
    wa_all,
    ww_all,
    wn_all,
    cos_tab,
    sin_tab,
    qm,
    km,
    gain_send,
    gain_recv,
    wbuf,
    send,
    recv,
    own,
    gain_send_sem,
    gain_recv_sem,
    load_sem,
):
    i = pl.program_id(0)
    pairs = pl.num_programs(0)
    npairs, cuts = plan
    place = Place()
    length, width = x_ref.shape
    tiles = length // TILE
    sources = [wq_in.at[k] for k in range(npairs)]
    targets = [wq_all.at[k] for k in range(npairs)]
    for cut, shard, full in zip(cuts, (wa_in, ww_in, wn_in), (wa_all, ww_all, wn_all)):
        for lo, size in cut:
            sources.append(shard.at[:, pl.ds(lo, size)])
            targets.append(full.at[:, :, :, pl.ds(lo, size)])
    gather = Gather(place, sources, targets, send, recv, own)

    events = staged(gather.count, GATHER_LAGS, PACE)
    events = [e for e in events if e[1:] not in [(0, k) for k in range(AHEAD)]]

    def run_until(time):
        while events and events[0][0] <= time:
            gather.step(*events.pop(0)[1:])

    def gain_copy(m):
        return remote(
            gain_send,
            gain_recv.at[place.f],
            gain_send_sem.at[m - 1],
            gain_recv_sem.at[m - 1],
            (place.fsdp_of(m), place.r),
        )

    def load(k):
        return pltpu.make_async_copy(wq_all.at[k], wbuf.at[k % 2], load_sem.at[k % 2])

    @pl.when(i == 0)
    def _():
        gain_send[...] = gain_in[...]
        greet(
            [(place.fsdp_of(m), place.r) for m in range(1, 8)] + [place.y_dev(), place.core_dev()]
        )
        for m in range(1, 8):
            gain_copy(m).start()
        for k in range(AHEAD):
            gather.step(0, k)
        gain_recv[place.f] = gain_in[...]
        lane_tile = lax.broadcasted_iota(jnp.int32, (TILE, HDIM), 1)
        live_cols = jnp.transpose(
            jnp.concatenate(
                [live_ref[...].astype(jnp.float32), jnp.zeros((TILE - tiles, TILE), jnp.float32)], axis=0
            )
        )
        segs = [seg_ref[u : u + 1, :] for u in range(tiles)]
        for t in range(tiles):
            rows = slice(t * TILE, (t + 1) * TILE)
            before = jnp.zeros((1, TILE), jnp.int32)
            same = jnp.zeros((TILE, HDIM), jnp.float32)
            for u in range(tiles):
                before += jnp.where(segs[u] < segs[t], 1, 0)
                hit = jnp.where(segs[u] == segs[t], 1.0, 0.0)[:, :HDIM]
                same = jnp.where(lane_tile == u, hit, same)
            cos_t, sin_t = cos_in[:TILE, :], sin_in[:TILE, :]
            for c in range(1, t + 1):
                at = slice(c * TILE, (c + 1) * TILE)
                cos_t = jnp.where(t - before == c, cos_in[at, :], cos_t)
                sin_t = jnp.where(t - before == c, sin_in[at, :], sin_t)
            cos_tab[rows, :] = cos_t
            sin_tab[rows, :] = sin_t
            dead = jnp.where(live_cols[:, t : t + 1] > 0, 0.0, masked_score)
            qv = jnp.where(lane_tile < tiles, jnp.where(same > 0, 0.0, masked_score), 0.0)
            qm[rows, :] = jnp.where(lane_tile == tiles, 1.0, qv).astype(jnp.bfloat16)
            kv = jnp.where(lane_tile == tiles, dead, same)
            km[rows, :] = kv.astype(jnp.bfloat16)
        run_until(3.0)
        for m in range(1, 8):
            gain_copy(m).wait()
        part = width // 8
        wide_row = lax.broadcasted_iota(jnp.int32, (PAIR, width), 0)
        wide_col = lax.broadcasted_iota(jnp.int32, (PAIR, width), 1)
        gains = jnp.zeros((8, width), jnp.float32)
        for f in range(8):
            pick_f = jnp.where((wide_col == wide_row + f * part) & (wide_row < part), 1.0, 0.0)
            gains += jnp.dot(
                gain_recv[f].astype(jnp.bfloat16),
                pick_f.astype(jnp.bfloat16),
                preferred_element_type=jnp.float32,
            )
        gain_out[...] = gains
        run_until(6.4)

        def norm_rows(b, carry):
            rows = pl.ds(pl.multiple_of(b * TILE, TILE), TILE)
            v = x_ref[rows, :].astype(jnp.float32)
            c = v - jnp.mean(v, axis=1, keepdims=True)
            spread = jnp.mean(c * c, axis=1, keepdims=True)
            normed_out[rows, :] = (c * lax.rsqrt(spread + eps) * gain_out[0:1, :]).astype(jnp.bfloat16)
            return carry

        lax.fori_loop(0, tiles, norm_rows, 0)
        run_until(GATHER_LAGS[4])
        load(0).start()
        load(0).wait()

    packed = jnp.dot(
        normed_out[...],
        wbuf[i % 2].reshape(width, 3 * PAIR),
        preferred_element_type=jnp.float32,
    )
    pq, pk, pv = packed[:, :PAIR], packed[:, PAIR : 2 * PAIR], packed[:, 2 * PAIR :]
    cos_v, sin_v = cos_tab[...], sin_tab[...]
    q_out[...] = ((pq * cos_v + swap_halves(pq) * sin_v).astype(jnp.bfloat16)) * 0.125
    k_out[...] = (pk * cos_v + swap_halves(pk) * sin_v).astype(jnp.bfloat16)
    v_out[...] = pv.astype(jnp.bfloat16)
    flipped = jnp.transpose(v_out[...])

    slots = length // QROWS
    queue = [[[] for _ in range(slots)] for _ in range(npairs)]
    for p in range(npairs):
        for slot in range(slots):
            now = GATHER_LAGS[4] + PAIR_US * (p + (slot + 1) / slots)
            while events and events[0][0] <= now:
                queue[p][slot].append(events.pop(0)[1:])
    queue[-1][-1].extend(e[1:] for e in events)
    for slot, begin in enumerate(range(0, length, QROWS)):
        for p in range(npairs):

            @pl.when(i == p)
            def _():
                for stage, k in queue[p][slot]:
                    gather.step(stage, k)
                if p + 1 < npairs and slot == slots - 2:
                    load(p + 1).start()
                if p + 1 < npairs and slot == slots - 1:
                    load(p + 1).wait()

        parts = []
        for head in range(PAIR // HDIM):
            cols = slice(head * HDIM, (head + 1) * HDIM)
            keys = jnp.concatenate([k_out[:, cols], km[...]], axis=1)
            rows = jnp.concatenate(
                [q_out[begin : begin + QROWS, cols], qm[begin : begin + QROWS, :]], axis=1
            )
            scores = rows_dot(keys, rows)
            top = jnp.max(scores, axis=0, keepdims=True)
            expo = jnp.exp(scores - top)
            total = jnp.sum(expo, axis=0, keepdims=True)
            lse_out[0, head : head + 1, begin : begin + QROWS] = top + jnp.log(total)
            out = jnp.dot(
                flipped[cols, :], expo.astype(jnp.bfloat16), preferred_element_type=jnp.float32
            )
            parts.append(out / total)
        both = jnp.concatenate(parts, axis=0)
        mixed_out[begin : begin + QROWS, :] = jnp.transpose(both).astype(jnp.bfloat16)

    @pl.when(i == pairs - 1)
    def _():
        gather.finish()


def cuts_of(width, piece):
    return [(lo, min(piece, width - lo)) for lo in range(0, width, piece)]


def forward(layer_input, wq_in, attn_weight, wide_weight, narrow_weight, gain_in, token_seg, token_live):
    length, width = layer_input.shape
    pairs = width // PAIR
    part = attn_weight.shape[0]
    cos_c, sin_c = table_constants(length)
    cuts = [cuts_of(w.shape[1], 3 * PAIR) for w in (attn_weight, wide_weight, narrow_weight)]
    count = pairs + sum(len(c) for c in cuts)
    block = pl.BlockSpec((length, PAIR), lambda i: (0, i))
    whole = pl.BlockSpec(memory_space=pltpu.VMEM)
    hbm = pl.BlockSpec(memory_space=pl.ANY)
    rows = jax.ShapeDtypeStruct((length, width), jnp.bfloat16)
    full = lambda cols: jax.ShapeDtypeStruct((4, 2, part, cols), jnp.bfloat16)
    return pl.pallas_call(
        functools.partial(forward_kernel, (pairs, cuts)),
        grid=(pairs,),
        in_specs=[whole] * 6 + [hbm] * 4,
        out_specs=[block] * 4
        + [pl.BlockSpec((1, 2, length), lambda i: (i, 0, 0)), whole, whole]
        + [hbm] * 4
        + [whole] * 4,
        out_shape=[rows] * 4
        + [
            jax.ShapeDtypeStruct((pairs, 2, length), jnp.float32),
            rows,
            jax.ShapeDtypeStruct((8, width), jnp.float32),
            jax.ShapeDtypeStruct((pairs, 4, 2, part, 3 * PAIR), jnp.bfloat16),
            full(width),
            full(wide_weight.shape[1]),
            full(narrow_weight.shape[1]),
            jax.ShapeDtypeStruct((length, PAIR), jnp.float32),
            jax.ShapeDtypeStruct((length, PAIR), jnp.float32),
            jax.ShapeDtypeStruct((length, HDIM), jnp.bfloat16),
            jax.ShapeDtypeStruct((length, HDIM), jnp.bfloat16),
        ],
        scratch_shapes=[
            pltpu.VMEM((8, PAIR), jnp.float32),
            pltpu.VMEM((8, 8, PAIR), jnp.float32),
            pltpu.VMEM((2, 4, 2, part, 3 * PAIR), jnp.bfloat16),
            pltpu.SemaphoreType.DMA((count, 6)),
            pltpu.SemaphoreType.DMA((count, 6)),
            pltpu.SemaphoreType.DMA((count,)),
            pltpu.SemaphoreType.DMA((7,)),
            pltpu.SemaphoreType.DMA((7,)),
            pltpu.SemaphoreType.DMA((2,)),
        ],
        compiler_params=pltpu.CompilerParams(
            vmem_limit_bytes=56 << 20, collective_id=0, has_side_effects=True
        ),
        cost_estimate=pl.CostEstimate(
            flops=22 * width * length * length, bytes_accessed=40 * length * width,
            transcendentals=pairs * 2 * length * length,
        ),
    )(
        token_seg.reshape(length // TILE, TILE), layer_input, gain_in,
        token_live.reshape(length // TILE, TILE),
        jnp.asarray(cos_c), jnp.asarray(sin_c), wq_in, attn_weight, wide_weight, narrow_weight,
    )


class Reduce:
    def __init__(self, place, sources, loaded, outs, bufs, send, recv, load):
        self.p, self.src, self.loaded, self.outs = place, sources, loaded, outs
        self.acc, self.rc, self.ry, self.rx, self.rz, self.s, self.ry2, self.f, self.rf = bufs
        self.send, self.recv, self.load = send, recv, load
        self.count = len(sources)

    def local(self, start, size):
        return pl.ds(pl.multiple_of(start, STEP), size)

    def mine(self):
        return self.local(STEP * self.p.y, 2 * STEP)

    def core_copy(self, k):
        p = self.p
        rows = self.local(HALF * (1 - p.core), HALF)
        return remote(
            self.src[k].at[:, :, rows, :], self.rc.at[k], self.send.at[k, 0], self.recv.at[k, 0], p.core_dev()
        )

    def load_copy(self, k):
        return pltpu.make_async_copy(
            self.src[k].at[:, :, self.p.rows_core(), :], self.acc.at[k], self.load.at[k]
        )

    def y_copy(self, k):
        p = self.p
        rows = self.local(2 * STEP * (1 - p.y), STEP)
        return remote(
            self.acc.at[k, :, :, rows, :], self.ry.at[k], self.send.at[k, 1], self.recv.at[k, 1], p.y_dev()
        )

    def x_copy(self, k):
        p = self.p
        return remote(
            self.acc.at[k, :, 1 - p.x, self.mine(), :],
            self.rx.at[k],
            self.send.at[k, 2],
            self.recv.at[k, 2],
            p.x_dev(),
        )

    def z_copy(self, k, d):
        p = self.p
        return remote(
            self.acc.at[k, p.along_z(d), p.x, self.mine(), :],
            self.rz.at[k, d - 1],
            self.send.at[k, 2 + d],
            self.recv.at[k, 2 + d],
            p.z_dev(d),
        )

    def y2_copy(self, k):
        return remote(
            self.s.at[k], self.ry2.at[k], self.send.at[k, 6], self.recv.at[k, 6], self.p.y_dev()
        )

    def core2_copy(self, k):
        return remote(
            self.f.at[k], self.rf.at[k], self.send.at[k, 7], self.recv.at[k, 7], self.p.core_dev()
        )

    def plus(self, a, b):
        return (a.astype(jnp.float32) + b.astype(jnp.float32)).astype(jnp.bfloat16)

    def step(self, stage, k):
        p = self.p
        acc = self.acc
        if stage == 0:
            self.core_copy(k).start()
            if self.loaded[k]:
                self.load_copy(k).start()
        elif stage == 1:
            self.core_copy(k).wait_recv()
            if self.loaded[k]:
                self.load_copy(k).wait()
                acc[k] = self.plus(acc[k], self.rc[k])
            else:
                acc[k] = self.plus(self.src[k][:, :, p.rows_core(), :], self.rc[k])
            self.y_copy(k).start()
        elif stage == 2:
            self.y_copy(k).wait_recv()
            rows = self.local(2 * STEP * p.y, STEP)
            acc[k, :, :, rows, :] = self.plus(acc[k, :, :, rows, :], self.ry[k])
            self.x_copy(k).start()
        elif stage == 3:
            self.x_copy(k).wait_recv()
            rows = self.mine()
            acc[k, :, p.x, rows, :] = self.plus(acc[k, :, p.x, rows, :], self.rx[k])
            for d in (2, 3, 1):
                self.z_copy(k, d).start()
        elif stage == 4:
            total = acc[k, p.z, p.x, self.mine(), :].astype(jnp.float32)
            for d in (1, 2, 3):
                self.z_copy(k, d).wait_recv()
                total += self.rz[k, d - 1].astype(jnp.float32)
            self.s[k] = total.astype(jnp.bfloat16)
            self.y2_copy(k).start()
        elif stage == 5:
            self.y2_copy(k).wait_recv()
            low, high = self.local(STEP * p.y, STEP), self.local(STEP * (1 - p.y), STEP)
            self.f[k, self.local(2 * STEP * p.y, STEP), :] = self.s[k, low, :]
            self.f[k, STEP : 2 * STEP, :] = self.plus(self.s[k, high, :], self.ry2[k, low, :])
            self.f[k, self.local(2 * STEP * (1 - p.y), STEP), :] = self.ry2[k, high, :]
            self.core2_copy(k).start()
            self.outs[k][p.rows_core(), :] = self.f[k].astype(jnp.float32)
        else:
            self.core2_copy(k).wait_recv()
            self.outs[k][self.local(HALF * (1 - p.core), HALF), :] = self.rf[k].astype(jnp.float32)

    def finish(self):
        for k in range(self.count):
            self.core_copy(k).wait_send()
            self.y_copy(k).wait_send()
            self.x_copy(k).wait_send()
            for d in (1, 2, 3):
                self.z_copy(k, d).wait_send()
            self.y2_copy(k).wait_send()
            self.core2_copy(k).wait_send()


REDUCE_LAGS = (0.0, 2.0, 6.5, 11.0, 16.0, 19.5, 21.5)
BACK_US = 8.6


def reduce_events(given, pairs):
    now, first, late, starts = 0.0, 0, 0, {}
    while first < given or late < pairs:
        if late < pairs and BACK_US * (late + 1) <= now:
            starts[given + late] = BACK_US * (late + 1)
            late += 1
        elif first < given:
            starts[first] = now
            first += 1
        else:
            now = BACK_US * (late + 1)
            continue
        now += 2.35
    return sorted((t + lag, stage, k) for k, t in starts.items() for stage, lag in enumerate(REDUCE_LAGS))


def backward_kernel(
    plan,
    q_ref,
    k_ref,
    v_ref,
    mixed_ref,
    go_ref,
    lse_ref,
    cos_ref,
    sin_ref,
    qm,
    km,
    gain_ref,
    second_ref,
    normed_in,
    x_in,
    gm_in,
    wq_in,
    narrow_in,
    wide_in,
    attn_in,
    input_grad,
    qkv_out,
    attn_out,
    wide_out,
    narrow_out,
    gain_out,
    normed_t,
    x_buf,
    gm_buf,
    wq_buf,
    gp_all,
    terms,
    acc,
    rc,
    ry,
    rx,
    rz,
    s_buf,
    ry2,
    f_buf,
    rf,
    gain_rep,
    gain_parts,
    gain_all,
    send,
    recv,
    load,
    bulk,
    rep_send,
    rep_recv,
    fsdp_send,
    fsdp_recv,
    out_sem,
):
    i = pl.program_id(0)
    npairs, cuts = plan
    place = Place()
    length, width = normed_in.shape
    part = width // 8
    sources, loaded, outs = [], [], []
    for cut, term, out in zip(cuts, (narrow_in, wide_in, attn_in), (narrow_out, wide_out, attn_out)):
        for lo, size in cut:
            sources.append(term.at[:, :, :, pl.ds(lo, size)])
            outs.append(out.at[:, pl.ds(lo, size)])
            loaded.append(True)
    given = len(sources)
    for p in range(npairs):
        sources.append(terms.at[p])
        outs.append(qkv_out.at[p])
        loaded.append(False)
    bufs = (acc, rc, ry, rx, rz, s_buf, ry2, f_buf, rf)
    reduce = Reduce(place, sources, loaded, outs, bufs, send, recv, load)
    events = reduce_events(given, npairs)
    slots = 2 * (length // QROWS)
    queue = [[[] for _ in range(slots + 1)] for _ in range(npairs)]
    for p in range(npairs):
        for slot in range(slots + 1):
            now = BACK_US * (p + min(slot, slots - 0.01) / slots) if slot < slots else BACK_US * (p + 1)
            while events and events[0][0] <= now:
                queue[p][slot].append(events.pop(0)[1:])

    def run_slot(slot):
        for p in range(npairs):
            if queue[p][slot]:

                @pl.when(i == p)
                def _():
                    for stage, k in queue[p][slot]:
                        reduce.step(stage, k)

    bulk_copies = [
        pltpu.make_async_copy(x_in, x_buf, bulk.at[0]),
        pltpu.make_async_copy(gm_in, gm_buf, bulk.at[1]),
        pltpu.make_async_copy(wq_in, wq_buf, bulk.at[2]),
    ]

    @pl.when(i == 0)
    def _():
        greet(
            [(place.fsdp_of(m), place.r) for m in range(1, 8)]
            + [place.y_dev(), place.core_dev(), (place.f, 3 - place.r)]
        )
        for copy in bulk_copies:
            copy.start()
        normed_t[...] = jnp.transpose(normed_in[...])

    cos_tab, sin_tab = cos_ref[...], sin_ref[...]
    product = jnp.transpose(mixed_ref[...].astype(jnp.float32) * go_ref[...].astype(jnp.float32))
    flipped = jnp.transpose(k_ref[...])
    gq_parts, gk_parts, gv_parts = [], [], []
    slot = 0
    for head in range(PAIR // HDIM):
        cols = slice(head * HDIM, (head + 1) * HDIM)
        delta = jnp.sum(product[cols, :], axis=0, keepdims=True)
        keys = jnp.concatenate([k_ref[:, cols], km[...]], axis=1)
        values = v_ref[:, cols]
        grad_k = jnp.zeros((length, HDIM), jnp.float32)
        grad_v = jnp.zeros((length, HDIM), jnp.float32)
        grad_q = []
        for begin in range(0, length, QROWS):
            run_slot(slot)
            slot += 1
            span = slice(begin, begin + QROWS)
            low_q, low_go = q_ref[span, cols], go_ref[span, cols]
            scores = rows_dot(keys, jnp.concatenate([low_q, qm[span, :]], axis=1))
            probs = jnp.exp(scores - lse_ref[0, head : head + 1, span])
            grad_v += jnp.dot(probs.astype(jnp.bfloat16), low_go, preferred_element_type=jnp.float32)
            grad_p = rows_dot(values, low_go)
            grad_s = (probs * (grad_p - delta[:, span])).astype(jnp.bfloat16)
            grad_k += jnp.dot(grad_s, low_q, preferred_element_type=jnp.float32)
            grad_q.append(jnp.dot(flipped[cols, :], grad_s, preferred_element_type=jnp.float32))
        gq_parts.append(jnp.concatenate(grad_q, axis=1))
        gk_parts.append(grad_k)
        gv_parts.append(grad_v)
    grad_q = jnp.transpose(jnp.concatenate(gq_parts, axis=0)) * 0.125
    grad_k = jnp.concatenate(gk_parts, axis=1)
    gp = jnp.concatenate(
        [
            (grad_q * cos_tab + swap_halves(grad_q * sin_tab)).astype(jnp.bfloat16),
            (grad_k * cos_tab + swap_halves(grad_k * sin_tab)).astype(jnp.bfloat16),
            jnp.concatenate(gv_parts, axis=1).astype(jnp.bfloat16),
        ],
        axis=1,
    )
    gp_all[i] = gp
    term = jnp.dot(normed_t[...], gp, preferred_element_type=jnp.float32)
    terms[i] = term.astype(jnp.bfloat16).reshape(4, 2, part, 3 * PAIR)
    run_slot(slots)

    def rep_copy(m):
        return remote(
            gain_rep.at[place.r],
            gain_rep.at[place.r],
            rep_send.at[m - 1],
            rep_recv.at[m - 1],
            (place.f, (place.y_dev()[1], place.core_dev()[1], 3 - place.r)[m - 1]),
        )

    def fsdp_copy(m):
        return remote(
            gain_parts.at[place.fsdp_of(m)],
            gain_all.at[place.f],
            fsdp_send.at[m - 1],
            fsdp_recv.at[m - 1],
            (place.fsdp_of(m), place.r),
        )

    @pl.when(i == npairs - 1)
    def _():
        for copy in bulk_copies:
            copy.wait()
        gain = gain_ref[0:1, :]
        blocks = length // QROWS
        share = len(events) // (blocks + 1)
        first = jnp.zeros((1, width), jnp.float32)
        writes = []
        for b in range(blocks):
            rows = slice(b * QROWS, (b + 1) * QROWS)
            e1 = jnp.zeros((QROWS, width), jnp.float32)
            for p in range(npairs):
                e1 += rows_dot(gp_all[p, rows, :], wq_buf[p].reshape(width, 3 * PAIR))
            v = x_buf[rows, :].astype(jnp.float32)
            c = v - jnp.mean(v, axis=1, keepdims=True)
            r1 = lax.rsqrt(jnp.mean(c * c, axis=1, keepdims=True) + eps)
            n1 = c * r1
            first += jnp.sum(e1 * n1, axis=0, keepdims=True)
            f1 = e1 * gain
            drift = f1 - jnp.mean(f1, axis=1, keepdims=True)
            gm_buf[rows, :] += r1 * (drift - n1 * jnp.mean(f1 * n1, axis=1, keepdims=True))
            write = pltpu.make_async_copy(gm_buf.at[rows, :], input_grad.at[rows, :], out_sem.at[b])
            write.start()
            writes.append(write)
            for _ in range(2):
                if events:
                    reduce.step(*events.pop(0)[1:])
        sub = lax.broadcasted_iota(jnp.int32, (8, width), 0)
        gain_rep[place.r] = jnp.where(sub == 0, first, jnp.where(sub == 1, second_ref[...], 0.0))
        for m in (1, 2, 3):
            rep_copy(m).start()
        for m in (1, 2, 3):
            rep_copy(m).wait()
        total = gain_rep[0] + gain_rep[1] + gain_rep[2] + gain_rep[3]
        gain_parts[...] = jnp.zeros_like(gain_parts)
        for f in range(8):
            gain_parts[f, :, :part] = total[:, f * part : (f + 1) * part]
        for m in range(1, 8):
            fsdp_copy(m).start()
        gain_all[place.f] = gain_parts[place.f]
        while events:
            reduce.step(*events.pop(0)[1:])
        for m in range(1, 8):
            fsdp_copy(m).wait()
        shared = gain_all[0]
        for f in range(1, 8):
            shared += gain_all[f]
        gain_out[...] = shared
        for write in writes:
            write.wait()
        reduce.finish()


def backward(
    queries, keyset, valueset, mixed, grad_mixed, lse, cos_tab, sin_tab, qm, km, gains, second_term,
    normed_one, layer_input, grad_middle, wq_all, narrow_term, wide_term, attn_term,
):
    length, width = queries.shape
    pairs, part = width // PAIR, width // 8
    cuts = [cuts_of(t.shape[1], 3 * PAIR) for t in (narrow_term, wide_term, attn_term)]
    count = pairs + sum(len(c) for c in cuts)
    cols = 3 * PAIR
    block = pl.BlockSpec((length, PAIR), lambda i: (0, i))
    whole = pl.BlockSpec(memory_space=pltpu.VMEM)
    hbm = pl.BlockSpec(memory_space=pl.ANY)
    low = lambda *shape: pltpu.VMEM(shape, jnp.bfloat16)
    wide = lambda *shape: pltpu.VMEM(shape, jnp.float32)
    f32 = lambda *shape: jax.ShapeDtypeStruct(shape, jnp.float32)
    dma = pltpu.SemaphoreType.DMA
    terms = [t.reshape(4, 2, part, t.shape[1]) for t in (narrow_term, wide_term, attn_term)]
    return pl.pallas_call(
        functools.partial(backward_kernel, (pairs, cuts)),
        grid=(pairs,),
        in_specs=[block] * 5
        + [pl.BlockSpec((1, 2, length), lambda i: (i, 0, 0))]
        + [whole] * 7
        + [hbm] * 6,
        out_specs=[hbm] + [whole] * 5,
        out_shape=[
            f32(length, width),
            f32(pairs, part, cols),
            f32(part, attn_term.shape[1]),
            f32(part, wide_term.shape[1]),
            f32(part, narrow_term.shape[1]),
            f32(8, PAIR),
        ],
        scratch_shapes=[
            low(width, length),
            low(length, width),
            wide(length, width),
            low(pairs, 4, 2, part, cols),
            low(pairs, length, cols),
            low(pairs, 4, 2, part, cols),
            low(count, 4, 2, HALF, cols),
            low(count, 4, 2, HALF, cols),
            low(count, 4, 2, STEP, cols),
            low(count, 4, 2 * STEP, cols),
            low(count, 3, 2 * STEP, cols),
            low(count, 2 * STEP, cols),
            low(count, 2 * STEP, cols),
            low(count, HALF, cols),
            low(count, HALF, cols),
            wide(4, 8, width),
            wide(8, 8, PAIR),
            wide(8, 8, PAIR),
            dma((count, 8)),
            dma((count, 8)),
            dma((count,)),
            dma((3,)),
            dma((3,)),
            dma((3,)),
            dma((7,)),
            dma((7,)),
            dma((length // QROWS,)),
        ],
        compiler_params=pltpu.CompilerParams(
            vmem_limit_bytes=62 << 20, collective_id=1, has_side_effects=True
        ),
        cost_estimate=pl.CostEstimate(
            flops=60 * width * length * length, bytes_accessed=40 * length * width,
            transcendentals=pairs * 2 * length * length,
        ),
    )(
        queries, keyset, valueset, mixed, grad_mixed, lse, cos_tab, sin_tab, qm, km, gains, second_term,
        normed_one, layer_input, grad_middle, wq_all, *terms,
    )


def on_device(
    layer_input,
    qkv_weight,
    attn_weight,
    wide_weight,
    narrow_weight,
    first_gain,
    second_gain,
    out_grad,
    token_seg,
    token_live,
):
    gains = jnp.stack([first_gain, second_gain], axis=1)
    gains = jnp.pad(gains, ((0, 0), (0, PAIR - 2)))
    qkv_full, gains = gather_weights([qkv_weight, gains])
    attn_full, wide_full, narrow_full = gather_weights([attn_weight, wide_weight, narrow_weight])
    scale_one = gains[:, 0].astype(jnp.float32)
    scale_two = gains[:, 1].astype(jnp.float32)
    residual_in = layer_input.astype(jnp.float32)
    qm, km = mask_columns(token_seg, token_live)
    cos_tab, sin_tab = rope_tables(token_seg)
    normed_one = layer_norm(residual_in, scale_one).astype(jnp.bfloat16)
    packed = jnp.dot(normed_one, qkv_full, preferred_element_type=jnp.float32)
    queries, keyset, valueset, mixed_rows, lse = attend(packed, cos_tab, sin_tab, qm, km)
    middle = residual_in + jnp.dot(mixed_rows, attn_full, preferred_element_type=jnp.float32)
    normed_two = layer_norm(middle, scale_two).astype(jnp.bfloat16)
    lifted = jnp.dot(normed_two, wide_full, preferred_element_type=jnp.float32)
    hidden = geglu(lifted).astype(jnp.bfloat16)
    layer_out = middle + jnp.einsum(
        "tf,df->td", hidden, narrow_full, preferred_element_type=jnp.float32
    )
    grad_top = out_grad.astype(jnp.float32) * token_live.astype(jnp.float32)[:, None]
    grad_top_low = grad_top.astype(jnp.bfloat16)
    narrow_term = jnp.einsum("td,tf->df", grad_top_low, hidden, preferred_element_type=jnp.float32)
    grad_hidden = jnp.dot(grad_top_low, narrow_full, preferred_element_type=jnp.float32)
    _, pull_gate = jax.vjp(geglu, lifted)
    grad_lifted = pull_gate(grad_hidden)[0].astype(jnp.bfloat16)
    wide_term = jnp.einsum("td,tf->df", normed_two, grad_lifted, preferred_element_type=jnp.float32)
    grad_norm_two = jnp.einsum(
        "tf,df->td", grad_lifted, wide_full, preferred_element_type=jnp.float32
    )
    _, pull_two = jax.vjp(layer_norm, middle, scale_two)
    grad_mid_ln, second_term = pull_two(grad_norm_two)
    grad_middle = grad_top + grad_mid_ln
    grad_middle_low = grad_middle.astype(jnp.bfloat16)
    attn_term = jnp.einsum(
        "td,te->de", mixed_rows, grad_middle_low, preferred_element_type=jnp.float32
    )
    grad_mixed = jnp.einsum(
        "te,de->td", grad_middle_low, attn_full, preferred_element_type=jnp.float32
    )
    shares = scatter_sums([narrow_term, wide_term, attn_term])
    grad_parts = attend_back(
        queries, keyset, valueset, mixed_rows, grad_mixed.astype(jnp.bfloat16), lse,
        cos_tab, sin_tab, qm, km,
    )
    grad_packed = jnp.concatenate(grad_parts, axis=1)
    qkv_term = jnp.einsum("td,tf->df", normed_one, grad_packed, preferred_element_type=jnp.float32)
    grad_norm_one = jnp.einsum(
        "tf,df->td", grad_packed, qkv_full, preferred_element_type=jnp.float32
    )
    _, pull_one = jax.vjp(layer_norm, residual_in, scale_one)
    grad_in_ln, first_term = pull_one(grad_norm_one)
    input_grad = grad_middle + grad_in_ln
    gain_terms = jnp.stack([first_term, second_term], axis=1)
    gain_terms = jnp.pad(gain_terms, ((0, 0), (0, PAIR - 2)))
    qkv_share, gain_share = scatter_sums([qkv_term, gain_terms])
    return (
        layer_out.astype(jnp.bfloat16),
        input_grad,
        qkv_share,
        shares[2],
        shares[1],
        shares[0],
        gain_share[:, 0],
        gain_share[:, 1],
    )


def on_device_tuned(
    layer_input,
    qkv_weight,
    attn_weight,
    wide_weight,
    narrow_weight,
    first_gain,
    second_gain,
    out_grad,
    token_seg,
    token_live,
):
    length, width = layer_input.shape
    pairs, part = width // PAIR, attn_weight.shape[0]
    wq_in = qkv_weight.reshape(part, 3, pairs, PAIR).transpose(2, 0, 1, 3).reshape(pairs, part, 3 * PAIR)
    gain_in = jnp.pad(jnp.stack([first_gain, second_gain]).astype(jnp.float32), ((0, 6), (0, PAIR - part)))
    (queries, keyset, valueset, mixed_rows, lse, normed_one, gains, wq_all, wa_all, ww_all, wn_all,
     cos_tab, sin_tab, qm, km) = forward(
        layer_input, wq_in, attn_weight, wide_weight, narrow_weight, gain_in, token_seg, token_live
    )
    scale_one, scale_two = gains[0], gains[1]
    attn_full, wide_full, narrow_full = (w.reshape(width, w.shape[-1]) for w in (wa_all, ww_all, wn_all))
    residual_in = layer_input.astype(jnp.float32)
    middle = residual_in + jnp.dot(mixed_rows, attn_full, preferred_element_type=jnp.float32)
    normed_two = layer_norm(middle, scale_two).astype(jnp.bfloat16)
    lifted = jnp.dot(normed_two, wide_full, preferred_element_type=jnp.float32)
    hidden = geglu(lifted).astype(jnp.bfloat16)
    layer_out = middle + jnp.einsum(
        "tf,df->td", hidden, narrow_full, preferred_element_type=jnp.float32
    )
    grad_top = out_grad.astype(jnp.float32) * token_live.astype(jnp.float32)[:, None]
    grad_top_low = grad_top.astype(jnp.bfloat16)
    narrow_term = jnp.einsum("td,tf->df", grad_top_low, hidden, preferred_element_type=jnp.float32)
    grad_hidden = jnp.dot(grad_top_low, narrow_full, preferred_element_type=jnp.float32)
    _, pull_gate = jax.vjp(geglu, lifted)
    grad_lifted = pull_gate(grad_hidden)[0].astype(jnp.bfloat16)
    wide_term = jnp.einsum("td,tf->df", normed_two, grad_lifted, preferred_element_type=jnp.float32)
    grad_norm_two = jnp.einsum(
        "tf,df->td", grad_lifted, wide_full, preferred_element_type=jnp.float32
    )
    _, pull_two = jax.vjp(layer_norm, middle, scale_two)
    grad_mid_ln, second_term = pull_two(grad_norm_two)
    grad_middle = grad_top + grad_mid_ln
    grad_middle_low = grad_middle.astype(jnp.bfloat16)
    attn_term = jnp.einsum(
        "td,te->de", mixed_rows, grad_middle_low, preferred_element_type=jnp.float32
    )
    grad_mixed = jnp.einsum(
        "te,de->td", grad_middle_low, attn_full, preferred_element_type=jnp.float32
    )
    low_terms = [term.astype(jnp.bfloat16) for term in (narrow_term, wide_term, attn_term)]
    input_grad, qkv_share, attn_share, wide_share, narrow_share, gain_share = backward(
        queries, keyset, valueset, mixed_rows, grad_mixed.astype(jnp.bfloat16), lse, cos_tab, sin_tab, qm, km,
        gains, second_term[None, :], normed_one, layer_input, grad_middle, wq_all, *low_terms,
    )
    qkv_share = qkv_share.reshape(pairs, part, 3, PAIR).transpose(1, 2, 0, 3).reshape(part, 3 * width)
    return (
        layer_out.astype(jnp.bfloat16),
        input_grad,
        qkv_share,
        attn_share,
        wide_share,
        narrow_share,
        gain_share[0, :part],
        gain_share[1, :part],
    )


def solution(mesh):
    tuned = mesh.shape["fsdp"] == 8 and mesh.shape["rep"] == 4
    return jax.shard_map(
        on_device_tuned if tuned else on_device,
        mesh=mesh,
        in_specs=(
            P(("fsdp", "rep"), None),
            P("fsdp", None),
            P("fsdp", None),
            P("fsdp", None),
            P("fsdp", None),
            P("fsdp"),
            P("fsdp"),
            P(("fsdp", "rep"), None),
            P(("fsdp", "rep")),
            P(("fsdp", "rep")),
        ),
        out_specs=(
            P(("fsdp", "rep"), None),
            P(("fsdp", "rep"), None),
            P("fsdp", None),
            P("fsdp", None),
            P("fsdp", None),
            P("fsdp", None),
            P("fsdp"),
            P("fsdp"),
        ),
        check_vma=False,
    )
```

```python
import functools
import math

import jax
import jax.numpy as jnp
import numpy as np
from jax import lax
from jax.experimental import pallas as pl
from jax.experimental.pallas import tpu as pltpu
from jax.sharding import PartitionSpec as P

HDIM = 64
TILE = 128
PAIR = 128
QROWS = 256


rope_base = 160000.0
eps = 1e-05
masked_score = -1e30


def layer_norm(values, scales):
    center = values - jnp.mean(values, axis=-1, keepdims=True)
    spread = jnp.mean(center * center, axis=-1, keepdims=True)
    return center * lax.rsqrt(spread + eps) * scales


def rope_tables(seg_rows):
    length = seg_rows.shape[0]
    firsts = seg_rows[::TILE]
    before = jnp.sum((firsts[None, :] < seg_rows[:, None]).astype(jnp.int32), axis=1)
    places = jnp.arange(length, dtype=jnp.int32) - TILE * before
    freq_index = jnp.arange(HDIM // 2, dtype=jnp.float32)
    inverse = jnp.exp(freq_index * (-2.0 * math.log(rope_base) / HDIM))
    angles = places.astype(jnp.float32)[:, None] * inverse[None, :]
    cosine, sine = jnp.cos(angles), jnp.sin(angles)
    cos_tab = jnp.concatenate([cosine] * 4, axis=1)
    sin_tab = jnp.concatenate([-sine, sine, -sine, sine], axis=1)
    return cos_tab, sin_tab


def mask_columns(seg_rows, live_rows):
    length = seg_rows.shape[0]
    firsts = seg_rows[::TILE]
    same = seg_rows[:, None] == firsts[None, :]
    query_cols = jnp.where(same, 0.0, masked_score)
    key_cols = jnp.where(same, 1.0, 0.0)
    query_cols = jnp.concatenate([query_cols, jnp.ones((length, 1))], axis=1)
    dead = jnp.where(live_rows > 0, 0.0, masked_score)[:, None]
    key_cols = jnp.concatenate([key_cols, dead], axis=1)
    spare = ((0, 0), (0, HDIM - query_cols.shape[1]))
    return (
        jnp.pad(query_cols, spare).astype(jnp.bfloat16),
        jnp.pad(key_cols, spare).astype(jnp.bfloat16),
    )


def swap_halves(values):
    lane = lax.broadcasted_iota(jnp.int32, values.shape, 1)
    return jnp.where(
        lane % HDIM < HDIM // 2,
        pltpu.roll(values, PAIR - HDIM // 2, 1),
        pltpu.roll(values, HDIM // 2, 1),
    )


def rows_dot(left, right):
    return lax.dot_general(left, right, (((1,), (1,)), ((), ())), preferred_element_type=jnp.float32)


def attend_kernel(pq, pk, pv, cos_ref, sin_ref, qm, km, q_out, k_out, v_out, mixed_out, lse_out):
    cos_tab, sin_tab = cos_ref[...], sin_ref[...]
    length = cos_tab.shape[0]
    q_out[...] = ((pq[...] * cos_tab + swap_halves(pq[...]) * sin_tab).astype(jnp.bfloat16)) * 0.125
    k_out[...] = (pk[...] * cos_tab + swap_halves(pk[...]) * sin_tab).astype(jnp.bfloat16)
    v_out[...] = pv[...].astype(jnp.bfloat16)
    flipped = jnp.transpose(v_out[...])
    for begin in range(0, length, QROWS):
        parts = []
        for head in range(PAIR // HDIM):
            cols = slice(head * HDIM, (head + 1) * HDIM)
            keys = jnp.concatenate([k_out[:, cols], km[...]], axis=1)
            rows = jnp.concatenate(
                [q_out[begin : begin + QROWS, cols], qm[begin : begin + QROWS, :]], axis=1
            )
            scores = rows_dot(keys, rows)
            top = jnp.max(scores, axis=0, keepdims=True)
            expo = jnp.exp(scores - top)
            total = jnp.sum(expo, axis=0, keepdims=True)
            lse_out[0, head : head + 1, begin : begin + QROWS] = top + jnp.log(total)
            out = jnp.dot(
                flipped[cols, :], expo.astype(jnp.bfloat16), preferred_element_type=jnp.float32
            )
            parts.append(out / total)
        both = jnp.concatenate(parts, axis=0)
        mixed_out[begin : begin + QROWS, :] = jnp.transpose(both).astype(jnp.bfloat16)


def attend_back_kernel(
    q_ref, k_ref, v_ref, mixed_ref, go_ref, lse_ref, cos_ref, sin_ref, qm, km, gq_out, gk_out, gv_out
):
    cos_tab, sin_tab = cos_ref[...], sin_ref[...]
    length = cos_tab.shape[0]
    product = jnp.transpose(mixed_ref[...].astype(jnp.float32) * go_ref[...].astype(jnp.float32))
    flipped = jnp.transpose(k_ref[...])
    gq_parts, gk_parts, gv_parts = [], [], []
    for head in range(PAIR // HDIM):
        cols = slice(head * HDIM, (head + 1) * HDIM)
        delta = jnp.sum(product[cols, :], axis=0, keepdims=True)
        keys = jnp.concatenate([k_ref[:, cols], km[...]], axis=1)
        values = v_ref[:, cols]
        grad_k = jnp.zeros((length, HDIM), jnp.float32)
        grad_v = jnp.zeros((length, HDIM), jnp.float32)
        grad_q = []
        for begin in range(0, length, QROWS):
            span = slice(begin, begin + QROWS)
            low_q, low_go = q_ref[span, cols], go_ref[span, cols]
            scores = rows_dot(keys, jnp.concatenate([low_q, qm[span, :]], axis=1))
            probs = jnp.exp(scores - lse_ref[0, head : head + 1, span])
            grad_v += jnp.dot(probs.astype(jnp.bfloat16), low_go, preferred_element_type=jnp.float32)
            grad_p = rows_dot(values, low_go)
            grad_s = (probs * (grad_p - delta[:, span])).astype(jnp.bfloat16)
            grad_k += jnp.dot(grad_s, low_q, preferred_element_type=jnp.float32)
            grad_q.append(jnp.dot(flipped[cols, :], grad_s, preferred_element_type=jnp.float32))
        gq_parts.append(jnp.concatenate(grad_q, axis=1))
        gk_parts.append(grad_k)
        gv_parts.append(grad_v)
    grad_q = jnp.transpose(jnp.concatenate(gq_parts, axis=0)) * 0.125
    grad_k = jnp.concatenate(gk_parts, axis=1)
    gq_out[...] = (grad_q * cos_tab + swap_halves(grad_q * sin_tab)).astype(jnp.bfloat16)
    gk_out[...] = (grad_k * cos_tab + swap_halves(grad_k * sin_tab)).astype(jnp.bfloat16)
    gv_out[...] = jnp.concatenate(gv_parts, axis=1).astype(jnp.bfloat16)


def attend(packed, cos_tab, sin_tab, qm, km):
    length, width = packed.shape[0], packed.shape[1] // 3
    pairs = width // PAIR
    block = lambda shift: pl.BlockSpec((length, PAIR), lambda i: (0, i + shift))
    table = pl.BlockSpec((length, PAIR), lambda i: (0, 0))
    mask = pl.BlockSpec((length, HDIM), lambda i: (0, 0))
    rows = jax.ShapeDtypeStruct((length, width), jnp.bfloat16)
    return pl.pallas_call(
        attend_kernel,
        grid=(pairs,),
        in_specs=[block(0), block(pairs), block(2 * pairs), table, table, mask, mask],
        out_specs=[block(0)] * 4 + [pl.BlockSpec((1, 2, length), lambda i: (i, 0, 0))],
        out_shape=[rows] * 4 + [jax.ShapeDtypeStruct((pairs, 2, length), jnp.float32)],
        compiler_params=pltpu.CompilerParams(vmem_limit_bytes=40 << 20),
        cost_estimate=pl.CostEstimate(
            flops=16 * width * length * length, bytes_accessed=20 * length * width,
            transcendentals=pairs * 2 * length * length,
        ),
    )(packed, packed, packed, cos_tab, sin_tab, qm, km)


def attend_back(queries, keyset, valueset, mixed, grad_mixed, lse, cos_tab, sin_tab, qm, km):
    length, width = queries.shape
    pairs = width // PAIR
    block = pl.BlockSpec((length, PAIR), lambda i: (0, i))
    table = pl.BlockSpec((length, PAIR), lambda i: (0, 0))
    mask = pl.BlockSpec((length, HDIM), lambda i: (0, 0))
    rows = jax.ShapeDtypeStruct((length, width), jnp.bfloat16)
    return pl.pallas_call(
        attend_back_kernel,
        grid=(pairs,),
        in_specs=[block] * 5
        + [pl.BlockSpec((1, 2, length), lambda i: (i, 0, 0)), table, table, mask, mask],
        out_specs=[block] * 3,
        out_shape=[rows] * 3,
        compiler_params=pltpu.CompilerParams(vmem_limit_bytes=48 << 20),
        cost_estimate=pl.CostEstimate(
            flops=40 * width * length * length, bytes_accessed=16 * length * width,
            transcendentals=pairs * 2 * length * length,
        ),
    )(queries, keyset, valueset, mixed, grad_mixed, lse, cos_tab, sin_tab, qm, km)


def swap_with(array, axis, bit):
    size = lax.axis_size(axis)
    return lax.ppermute(array, axis, [(i, i ^ (1 << bit)) for i in range(size)])


def side_of(axis, bit):
    return (lax.axis_index(axis) >> bit) & 1


def bits_of(axis):
    return [(axis, bit) for bit in reversed(range(lax.axis_size(axis).bit_length() - 1))]


def gather_half(piece, order):
    canon = bits_of("fsdp") + bits_of("rep")
    have = []
    for axis, bit in order:
        other = swap_with(piece, axis, bit)
        side = side_of(axis, bit) == 0
        place = sum(canon.index(known) < canon.index((axis, bit)) for known in have)
        piece = jnp.stack(
            [jnp.where(side, piece, other), jnp.where(side, other, piece)], axis=place
        )
        have.append((axis, bit))
    return piece.reshape(-1, piece.shape[-1])


def pick(array, dim, side):
    return lax.dynamic_index_in_dim(array, side, dim, keepdims=False)


def orders():
    rep_bits, fsdp_bits = bits_of("rep")[::-1], bits_of("fsdp")[::-1]
    near, far = rep_bits[0], rep_bits[1:]
    one = [near] + far + fsdp_bits
    two = [near] + fsdp_bits[:1] + far + fsdp_bits[1:]
    return one, two


def gather_weights(arrays):
    joint = jnp.concatenate(arrays, axis=1)
    for axis, bit in bits_of("rep"):
        size = joint.shape[0] // 2
        joint = lax.dynamic_slice_in_dim(joint, side_of(axis, bit) * size, size, axis=0)
    cut = joint.shape[1] // 256 * 128
    one, two = orders()
    whole = jnp.concatenate(
        [gather_half(joint[:, :cut], one[::-1]), gather_half(joint[:, cut:], two[::-1])], axis=1
    )
    outs, start = [], 0
    for array in arrays:
        outs.append(whole[:, start : start + array.shape[1]])
        start += array.shape[1]
    return outs


def scatter_half(term, order):
    canon = bits_of("fsdp") + bits_of("rep")
    rows = term.shape[0] >> len(canon)
    acc = term.reshape([2] * len(canon) + [rows, term.shape[1]])
    left = list(canon)
    for axis, bit in order:
        dim = left.index((axis, bit))
        side = side_of(axis, bit)
        other = swap_with(pick(acc, dim, 1 - side), axis, bit)
        acc = pick(acc, dim, side).astype(jnp.float32) + other.astype(jnp.float32)
        acc = acc.astype(jnp.bfloat16)
        left.remove((axis, bit))
    rep_order = [entry for entry in order[::-1] if entry[0] == "rep"]
    have = []
    for axis, bit in rep_order:
        other = swap_with(acc, axis, bit)
        side = side_of(axis, bit) == 0
        place = sum(canon.index(known) < canon.index((axis, bit)) for known in have)
        acc = jnp.stack([jnp.where(side, acc, other), jnp.where(side, other, acc)], axis=place)
        have.append((axis, bit))
    return acc.reshape(-1, acc.shape[-1]).astype(jnp.float32)


def scatter_sums(terms):
    joint = jnp.concatenate([term.astype(jnp.bfloat16) for term in terms], axis=1)
    cut = joint.shape[1] // 256 * 128
    one, two = orders()
    whole = jnp.concatenate(
        [scatter_half(joint[:, :cut], one), scatter_half(joint[:, cut:], two)], axis=1
    )
    outs, start = [], 0
    for term in terms:
        outs.append(whole[:, start : start + term.shape[1]])
        start += term.shape[1]
    return outs


def geglu(lifted):
    half_ff = lifted.shape[1] // 2
    return jax.nn.gelu(lifted[:, :half_ff], approximate=False) * lifted[:, half_ff:]


MESH = pl.DeviceIdType.MESH
HALF = 48
AHEAD = 4
GATHER_LAGS = (3.0 - 2.1 * AHEAD, 3.0, 7.5, 12.0, 15.0)
PACE = 2.1
PAIR_US = 6.0
STEP = 16


def table_constants(length):
    places = np.arange(length, dtype=np.float32)
    freq_index = np.arange(HDIM // 2, dtype=np.float32)
    inverse = np.exp(freq_index * np.float32(-2.0 * math.log(rope_base) / HDIM)).astype(np.float32)
    angles = (places[:, None] * inverse[None, :]).astype(np.float32).astype(np.float64)
    cosine, sine = np.cos(angles), np.sin(angles)
    cos_tab = np.concatenate([cosine] * 4, axis=1).astype(np.float32)
    sin_tab = np.concatenate([-sine, sine, -sine, sine], axis=1).astype(np.float32)
    return cos_tab, sin_tab


class Place:
    def __init__(self):
        self.f = lax.axis_index("fsdp")
        self.r = lax.axis_index("rep")
        self.z = self.f // 2
        self.x = self.f % 2
        self.y = self.r // 2
        self.core = self.r % 2

    def flip(self, value, bit):
        size = 1 << bit
        return value + size - 2 * size * ((value // size) % 2)

    def along_z(self, d):
        z = self.z
        for bit in range(2):
            if (d >> bit) & 1:
                z = self.flip(z, bit)
        return z

    def fsdp_of(self, m):
        f = self.f
        for bit in range(3):
            if (m >> bit) & 1:
                f = self.flip(f, bit)
        return f

    def z_dev(self, d):
        return (2 * self.along_z(d) + self.x, self.r)

    def x_dev(self):
        return (self.flip(self.f, 0), self.r)

    def y_dev(self):
        return (self.f, self.flip(self.r, 1))

    def core_dev(self):
        return (self.f, self.flip(self.r, 0))

    def rows_zx(self):
        return pl.ds(pl.multiple_of(HALF * self.core + STEP * self.y, STEP), 2 * STEP)

    def rows_y(self):
        return pl.ds(pl.multiple_of(HALF * self.core + 2 * STEP * self.y, STEP), STEP)

    def rows_core(self):
        return pl.ds(pl.multiple_of(HALF * self.core, STEP), HALF)


def remote(src, dst, send, recv, dev):
    return pltpu.make_async_remote_copy(
        src_ref=src, dst_ref=dst, send_sem=send, recv_sem=recv, device_id=dev, device_id_type=MESH
    )


def staged(count, lags, pace):
    return sorted((lag + pace * k, stage, k) for stage, lag in enumerate(lags) for k in range(count))


class Gather:
    def __init__(self, place, sources, targets, send, recv, own):
        self.p, self.src, self.dst = place, sources, targets
        self.send, self.recv, self.own = send, recv, own
        self.count = len(sources)

    def z_copy(self, k, d):
        p, rows = self.p, self.p.rows_zx()
        return remote(
            self.src[k].at[rows, :],
            self.dst[k].at[p.z, p.x, rows, :],
            self.send.at[k, d - 1],
            self.recv.at[k, d - 1],
            p.z_dev(d),
        )

    def own_copy(self, k):
        p, rows = self.p, self.p.rows_zx()
        return pltpu.make_async_copy(
            self.src[k].at[rows, :], self.dst[k].at[p.z, p.x, rows, :], self.own.at[k]
        )

    def x_copy(self, k):
        p = self.p
        part = self.dst[k].at[:, p.x, p.rows_zx(), :]
        return remote(part, part, self.send.at[k, 3], self.recv.at[k, 3], p.x_dev())

    def y_copy(self, k):
        p = self.p
        part = self.dst[k].at[:, :, p.rows_y(), :]
        return remote(part, part, self.send.at[k, 4], self.recv.at[k, 4], p.y_dev())

    def core_copy(self, k):
        p = self.p
        part = self.dst[k].at[:, :, p.rows_core(), :]
        return remote(part, part, self.send.at[k, 5], self.recv.at[k, 5], p.core_dev())

    def step(self, stage, k):
        if stage == 0:
            self.own_copy(k).start()
            for d in (1, 2, 3):
                self.z_copy(k, d).start()
        elif stage == 1:
            self.own_copy(k).wait()
            for d in (1, 2, 3):
                self.z_copy(k, d).wait_recv()
            self.x_copy(k).start()
        elif stage == 2:
            self.x_copy(k).wait_recv()
            self.y_copy(k).start()
        elif stage == 3:
            self.y_copy(k).wait_recv()
            self.core_copy(k).start()
        else:
            self.core_copy(k).wait_recv()

    def finish(self):
        for k in range(self.count):
            for d in (1, 2, 3):
                self.z_copy(k, d).wait_send()
            self.x_copy(k).wait_send()
            self.y_copy(k).wait_send()
            self.core_copy(k).wait_send()


def greet(devices):
    barrier = pltpu.get_barrier_semaphore()
    for dev in devices:
        pl.semaphore_signal(barrier, inc=1, device_id=dev, device_id_type=MESH)
    pl.semaphore_wait(barrier, len(devices))


def forward_kernel(
    plan,
    seg_ref,
    x_ref,
    gain_in,
    live_ref,
    cos_in,
    sin_in,
    wq_in,
    wa_in,
    ww_in,
    wn_in,
    q_out,
    k_out,
    v_out,
    mixed_out,
    lse_out,
    normed_out,
    gain_out,
    wq_all,
    wa_all,
    ww_all,
    wn_all,
    cos_tab,
    sin_tab,
    qm,
    km,
    gain_send,
    gain_recv,
    wbuf,
    send,
    recv,
    own,
    gain_send_sem,
    gain_recv_sem,
    load_sem,
    score_buf,
):
    i = pl.program_id(0)
    pairs = pl.num_programs(0)
    npairs, cuts = plan
    place = Place()
    length, width = x_ref.shape
    tiles = length // TILE
    sources = [wq_in.at[k] for k in range(npairs)]
    targets = [wq_all.at[k] for k in range(npairs)]
    for cut, shard, full in zip(cuts, (wa_in, ww_in, wn_in), (wa_all, ww_all, wn_all)):
        for lo, size in cut:
            sources.append(shard.at[:, pl.ds(lo, size)])
            targets.append(full.at[:, :, :, pl.ds(lo, size)])
    gather = Gather(place, sources, targets, send, recv, own)

    events = staged(gather.count, GATHER_LAGS, PACE)
    events = [e for e in events if e[1:] not in [(0, k) for k in range(AHEAD)]]

    def run_until(time):
        while events and events[0][0] <= time:
            gather.step(*events.pop(0)[1:])

    def gain_copy(m):
        return remote(
            gain_send,
            gain_recv.at[place.f],
            gain_send_sem.at[m - 1],
            gain_recv_sem.at[m - 1],
            (place.fsdp_of(m), place.r),
        )

    def load(k):
        return pltpu.make_async_copy(wq_all.at[k], wbuf.at[k % 2], load_sem.at[k % 2])

    @pl.when(i == 0)
    def _():
        gain_send[...] = gain_in[...]
        greet(
            [(place.fsdp_of(m), place.r) for m in range(1, 8)] + [place.y_dev(), place.core_dev()]
        )
        for m in range(1, 8):
            gain_copy(m).start()
        for k in range(AHEAD):
            gather.step(0, k)
        gain_recv[place.f] = gain_in[...]
        lane_tile = lax.broadcasted_iota(jnp.int32, (TILE, HDIM), 1)
        live_cols = jnp.transpose(
            jnp.concatenate(
                [live_ref[...].astype(jnp.float32), jnp.zeros((TILE - tiles, TILE), jnp.float32)], axis=0
            )
        )
        segs = [seg_ref[u : u + 1, :] for u in range(tiles)]
        for t in range(tiles):
            rows = slice(t * TILE, (t + 1) * TILE)
            before = jnp.zeros((1, TILE), jnp.int32)
            same = jnp.zeros((TILE, HDIM), jnp.float32)
            for u in range(tiles):
                before += jnp.where(segs[u] < segs[t], 1, 0)
                hit = jnp.where(segs[u] == segs[t], 1.0, 0.0)[:, :HDIM]
                same = jnp.where(lane_tile == u, hit, same)
            cos_t, sin_t = cos_in[:TILE, :], sin_in[:TILE, :]
            for c in range(1, t + 1):
                at = slice(c * TILE, (c + 1) * TILE)
                cos_t = jnp.where(t - before == c, cos_in[at, :], cos_t)
                sin_t = jnp.where(t - before == c, sin_in[at, :], sin_t)
            cos_tab[rows, :] = cos_t
            sin_tab[rows, :] = sin_t
            dead = jnp.where(live_cols[:, t : t + 1] > 0, 0.0, masked_score)
            qv = jnp.where(lane_tile < tiles, jnp.where(same > 0, 0.0, masked_score), 0.0)
            qm[rows, :] = jnp.where(lane_tile == tiles, 1.0, qv).astype(jnp.bfloat16)
            kv = jnp.where(lane_tile == tiles, dead, same)
            km[rows, :] = kv.astype(jnp.bfloat16)
        run_until(3.0)
        for m in range(1, 8):
            gain_copy(m).wait()
        part = width // 8
        wide_row = lax.broadcasted_iota(jnp.int32, (PAIR, width), 0)
        wide_col = lax.broadcasted_iota(jnp.int32, (PAIR, width), 1)
        gains = jnp.zeros((8, width), jnp.float32)
        for f in range(8):
            pick_f = jnp.where((wide_col == wide_row + f * part) & (wide_row < part), 1.0, 0.0)
            gains += jnp.dot(
                gain_recv[f].astype(jnp.bfloat16),
                pick_f.astype(jnp.bfloat16),
                preferred_element_type=jnp.float32,
            )
        gain_out[...] = gains
        run_until(6.4)

        def norm_rows(b, carry):
            rows = pl.ds(pl.multiple_of(b * TILE, TILE), TILE)
            v = x_ref[rows, :].astype(jnp.float32)
            c = v - jnp.mean(v, axis=1, keepdims=True)
            spread = jnp.mean(c * c, axis=1, keepdims=True)
            normed_out[rows, :] = (c * lax.rsqrt(spread + eps) * gain_out[0:1, :]).astype(jnp.bfloat16)
            return carry

        lax.fori_loop(0, tiles, norm_rows, 0)
        run_until(GATHER_LAGS[4])
        load(0).start()
        load(0).wait()

    packed = jnp.dot(
        normed_out[...],
        wbuf[i % 2].reshape(width, 3 * PAIR),
        preferred_element_type=jnp.float32,
    )
    pq, pk, pv = packed[:, :PAIR], packed[:, PAIR : 2 * PAIR], packed[:, 2 * PAIR :]
    cos_v, sin_v = cos_tab[...], sin_tab[...]
    q_out[...] = ((pq * cos_v + swap_halves(pq) * sin_v).astype(jnp.bfloat16)) * 0.125
    k_out[...] = (pk * cos_v + swap_halves(pk) * sin_v).astype(jnp.bfloat16)
    v_out[...] = pv.astype(jnp.bfloat16)
    flipped = jnp.transpose(v_out[...])

    slots = 4
    queue = [[[] for _ in range(slots)] for _ in range(npairs)]
    for p in range(npairs):
        for slot in range(slots):
            now = GATHER_LAGS[4] + PAIR_US * (p + (slot + 1) / slots)
            while events and events[0][0] <= now:
                queue[p][slot].append(events.pop(0)[1:])
    queue[-1][-1].extend(e[1:] for e in events)

    def run_slot(slot):
        for p in range(npairs):

            @pl.when(i == p)
            def _():
                for stage, k in queue[p][slot]:
                    gather.step(stage, k)
                if p + 1 < npairs and slot == slots - 2:
                    load(p + 1).start()
                if p + 1 < npairs and slot == slots - 1:
                    load(p + 1).wait()

    parts = []
    for head in range(PAIR // HDIM):
        run_slot(2 * head)
        cols = slice(head * HDIM, (head + 1) * HDIM)
        keys = jnp.concatenate([k_out[:, cols], km[...]], axis=1)
        rows = jnp.concatenate([q_out[:, cols], qm[...]], axis=1)
        tops = []
        for begin in range(0, length, QROWS):
            scores = rows_dot(keys[begin : begin + QROWS, :], rows)
            score_buf[head, begin : begin + QROWS, :] = scores
            tops.append(jnp.max(scores.reshape(QROWS // 8, 8, length), axis=0))
        top = jnp.max(functools.reduce(jnp.maximum, tops), axis=0, keepdims=True)
        run_slot(2 * head + 1)
        out = jnp.zeros((HDIM, length), jnp.float32)
        sums = jnp.zeros((8, length), jnp.float32)
        for begin in range(0, length, QROWS):
            expo = jnp.exp(score_buf[head, begin : begin + QROWS, :] - top)
            sums += jnp.sum(expo.reshape(QROWS // 8, 8, length), axis=0)
            out += jnp.dot(
                flipped[cols, begin : begin + QROWS],
                expo.astype(jnp.bfloat16),
                preferred_element_type=jnp.float32,
            )
        total = jnp.sum(sums, axis=0, keepdims=True)
        lse_out[0, head : head + 1, :] = top + jnp.log(total)
        parts.append(out / total)
    mixed_out[...] = jnp.transpose(jnp.concatenate(parts, axis=0)).astype(jnp.bfloat16)

    @pl.when(i == pairs - 1)
    def _():
        gather.finish()


def cuts_of(width, piece):
    return [(lo, min(piece, width - lo)) for lo in range(0, width, piece)]


def forward(layer_input, wq_in, attn_weight, wide_weight, narrow_weight, gain_in, token_seg, token_live):
    length, width = layer_input.shape
    pairs = width // PAIR
    part = attn_weight.shape[0]
    cos_c, sin_c = table_constants(length)
    cuts = [cuts_of(w.shape[1], 3 * PAIR) for w in (attn_weight, wide_weight, narrow_weight)]
    count = pairs + sum(len(c) for c in cuts)
    block = pl.BlockSpec((length, PAIR), lambda i: (0, i))
    whole = pl.BlockSpec(memory_space=pltpu.VMEM)
    hbm = pl.BlockSpec(memory_space=pl.ANY)
    rows = jax.ShapeDtypeStruct((length, width), jnp.bfloat16)
    full = lambda cols: jax.ShapeDtypeStruct((4, 2, part, cols), jnp.bfloat16)
    return pl.pallas_call(
        functools.partial(forward_kernel, (pairs, cuts)),
        grid=(pairs,),
        in_specs=[whole] * 6 + [hbm] * 4,
        out_specs=[block] * 4
        + [pl.BlockSpec((1, 2, length), lambda i: (i, 0, 0)), whole, whole]
        + [hbm] * 4
        + [whole] * 4,
        out_shape=[rows] * 4
        + [
            jax.ShapeDtypeStruct((pairs, 2, length), jnp.float32),
            rows,
            jax.ShapeDtypeStruct((8, width), jnp.float32),
            jax.ShapeDtypeStruct((pairs, 4, 2, part, 3 * PAIR), jnp.bfloat16),
            full(width),
            full(wide_weight.shape[1]),
            full(narrow_weight.shape[1]),
            jax.ShapeDtypeStruct((length, PAIR), jnp.float32),
            jax.ShapeDtypeStruct((length, PAIR), jnp.float32),
            jax.ShapeDtypeStruct((length, HDIM), jnp.bfloat16),
            jax.ShapeDtypeStruct((length, HDIM), jnp.bfloat16),
        ],
        scratch_shapes=[
            pltpu.VMEM((8, PAIR), jnp.float32),
            pltpu.VMEM((8, 8, PAIR), jnp.float32),
            pltpu.VMEM((2, 4, 2, part, 3 * PAIR), jnp.bfloat16),
            pltpu.SemaphoreType.DMA((count, 6)),
            pltpu.SemaphoreType.DMA((count, 6)),
            pltpu.SemaphoreType.DMA((count,)),
            pltpu.SemaphoreType.DMA((7,)),
            pltpu.SemaphoreType.DMA((7,)),
            pltpu.SemaphoreType.DMA((2,)),
            pltpu.VMEM((2, length, length), jnp.float32),
        ],
        compiler_params=pltpu.CompilerParams(
            vmem_limit_bytes=56 << 20, collective_id=0, has_side_effects=True
        ),
        cost_estimate=pl.CostEstimate(
            flops=22 * width * length * length, bytes_accessed=40 * length * width,
            transcendentals=pairs * 2 * length * length,
        ),
    )(
        token_seg.reshape(length // TILE, TILE), layer_input, gain_in,
        token_live.reshape(length // TILE, TILE),
        jnp.asarray(cos_c), jnp.asarray(sin_c), wq_in, attn_weight, wide_weight, narrow_weight,
    )


class Reduce:
    def __init__(self, place, sources, loaded, outs, bufs, send, recv, load):
        self.p, self.src, self.loaded, self.outs = place, sources, loaded, outs
        self.acc, self.rc, self.ry, self.rx, self.rz, self.s, self.ry2, self.f, self.rf = bufs
        self.send, self.recv, self.load = send, recv, load
        self.count = len(sources)

    def local(self, start, size):
        return pl.ds(pl.multiple_of(start, STEP), size)

    def mine(self):
        return self.local(STEP * self.p.y, 2 * STEP)

    def core_copy(self, k):
        p = self.p
        rows = self.local(HALF * (1 - p.core), HALF)
        return remote(
            self.src[k].at[:, :, rows, :], self.rc.at[k], self.send.at[k, 0], self.recv.at[k, 0], p.core_dev()
        )

    def load_copy(self, k):
        return pltpu.make_async_copy(
            self.src[k].at[:, :, self.p.rows_core(), :], self.acc.at[k], self.load.at[k]
        )

    def y_copy(self, k):
        p = self.p
        rows = self.local(2 * STEP * (1 - p.y), STEP)
        return remote(
            self.acc.at[k, :, :, rows, :], self.ry.at[k], self.send.at[k, 1], self.recv.at[k, 1], p.y_dev()
        )

    def x_copy(self, k):
        p = self.p
        return remote(
            self.acc.at[k, :, 1 - p.x, self.mine(), :],
            self.rx.at[k],
            self.send.at[k, 2],
            self.recv.at[k, 2],
            p.x_dev(),
        )

    def z_copy(self, k, d):
        p = self.p
        return remote(
            self.acc.at[k, p.along_z(d), p.x, self.mine(), :],
            self.rz.at[k, d - 1],
            self.send.at[k, 2 + d],
            self.recv.at[k, 2 + d],
            p.z_dev(d),
        )

    def y2_copy(self, k):
        return remote(
            self.s.at[k], self.ry2.at[k], self.send.at[k, 6], self.recv.at[k, 6], self.p.y_dev()
        )

    def core2_copy(self, k):
        return remote(
            self.f.at[k], self.rf.at[k], self.send.at[k, 7], self.recv.at[k, 7], self.p.core_dev()
        )

    def plus(self, a, b):
        return (a.astype(jnp.float32) + b.astype(jnp.float32)).astype(jnp.bfloat16)

    def step(self, stage, k):
        p = self.p
        acc = self.acc
        if stage == 0:
            self.core_copy(k).start()
            if self.loaded[k]:
                self.load_copy(k).start()
        elif stage == 1:
            self.core_copy(k).wait_recv()
            if self.loaded[k]:
                self.load_copy(k).wait()
                acc[k] = self.plus(acc[k], self.rc[k])
            else:
                acc[k] = self.plus(self.src[k][:, :, p.rows_core(), :], self.rc[k])
            self.y_copy(k).start()
        elif stage == 2:
            self.y_copy(k).wait_recv()
            rows = self.local(2 * STEP * p.y, STEP)
            acc[k, :, :, rows, :] = self.plus(acc[k, :, :, rows, :], self.ry[k])
            self.x_copy(k).start()
        elif stage == 3:
            self.x_copy(k).wait_recv()
            rows = self.mine()
            acc[k, :, p.x, rows, :] = self.plus(acc[k, :, p.x, rows, :], self.rx[k])
            for d in (2, 3, 1):
                self.z_copy(k, d).start()
        elif stage == 4:
            total = acc[k, p.z, p.x, self.mine(), :].astype(jnp.float32)
            for d in (1, 2, 3):
                self.z_copy(k, d).wait_recv()
                total += self.rz[k, d - 1].astype(jnp.float32)
            self.s[k] = total.astype(jnp.bfloat16)
            self.y2_copy(k).start()
        elif stage == 5:
            self.y2_copy(k).wait_recv()
            low, high = self.local(STEP * p.y, STEP), self.local(STEP * (1 - p.y), STEP)
            self.f[k, self.local(2 * STEP * p.y, STEP), :] = self.s[k, low, :]
            self.f[k, STEP : 2 * STEP, :] = self.plus(self.s[k, high, :], self.ry2[k, low, :])
            self.f[k, self.local(2 * STEP * (1 - p.y), STEP), :] = self.ry2[k, high, :]
            self.core2_copy(k).start()
            self.outs[k][p.rows_core(), :] = self.f[k].astype(jnp.float32)
        else:
            self.core2_copy(k).wait_recv()
            self.outs[k][self.local(HALF * (1 - p.core), HALF), :] = self.rf[k].astype(jnp.float32)

    def finish(self):
        for k in range(self.count):
            self.core_copy(k).wait_send()
            self.y_copy(k).wait_send()
            self.x_copy(k).wait_send()
            for d in (1, 2, 3):
                self.z_copy(k, d).wait_send()
            self.y2_copy(k).wait_send()
            self.core2_copy(k).wait_send()


REDUCE_LAGS = (0.0, 4.0, 10.0, 16.0, 22.0, 28.0, 32.0)
BACK_US = 8.6


def reduce_events(given, pairs):
    now, first, late, starts = 0.0, 0, 0, {}
    while first < given or late < pairs:
        if late < pairs and BACK_US * (late + 1) <= now:
            starts[given + late] = BACK_US * (late + 1)
            late += 1
        elif first < given:
            starts[first] = now
            first += 1
        else:
            now = BACK_US * (late + 1)
            continue
        now += 2.35
    return sorted((t + lag, stage, k) for k, t in starts.items() for stage, lag in enumerate(REDUCE_LAGS))


def backward_kernel(
    plan,
    q_ref,
    k_ref,
    v_ref,
    mixed_ref,
    go_ref,
    lse_ref,
    cos_ref,
    sin_ref,
    qm,
    km,
    gain_ref,
    second_ref,
    normed_in,
    x_in,
    gm_in,
    wq_in,
    narrow_in,
    wide_in,
    attn_in,
    input_grad,
    qkv_out,
    attn_out,
    wide_out,
    narrow_out,
    gain_out,
    normed_t,
    x_buf,
    gm_buf,
    wq_buf,
    gp_all,
    terms,
    acc,
    rc,
    ry,
    rx,
    rz,
    s_buf,
    ry2,
    f_buf,
    rf,
    gain_rep,
    gain_parts,
    gain_all,
    send,
    recv,
    load,
    bulk,
    rep_send,
    rep_recv,
    fsdp_send,
    fsdp_recv,
    out_sem,
):
    i = pl.program_id(0)
    npairs, cuts = plan
    place = Place()
    length, width = normed_in.shape
    part = width // 8
    sources, loaded, outs = [], [], []
    for cut, term, out in zip(cuts, (narrow_in, wide_in, attn_in), (narrow_out, wide_out, attn_out)):
        for lo, size in cut:
            sources.append(term.at[:, :, :, pl.ds(lo, size)])
            outs.append(out.at[:, pl.ds(lo, size)])
            loaded.append(True)
    given = len(sources)
    for p in range(npairs):
        sources.append(terms.at[p])
        outs.append(qkv_out.at[p])
        loaded.append(False)
    bufs = (acc, rc, ry, rx, rz, s_buf, ry2, f_buf, rf)
    reduce = Reduce(place, sources, loaded, outs, bufs, send, recv, load)
    events = reduce_events(given, npairs)
    slots = 2 * (length // QROWS)
    queue = [[[] for _ in range(slots + 1)] for _ in range(npairs)]
    for p in range(npairs):
        for slot in range(slots + 1):
            now = BACK_US * (p + min(slot, slots - 0.01) / slots) if slot < slots else BACK_US * (p + 1)
            while events and events[0][0] <= now:
                queue[p][slot].append(events.pop(0)[1:])

    def run_slot(slot):
        for p in range(npairs):
            if queue[p][slot]:

                @pl.when(i == p)
                def _():
                    for stage, k in queue[p][slot]:
                        reduce.step(stage, k)

    bulk_copies = [
        pltpu.make_async_copy(x_in, x_buf, bulk.at[0]),
        pltpu.make_async_copy(gm_in, gm_buf, bulk.at[1]),
        pltpu.make_async_copy(wq_in, wq_buf, bulk.at[2]),
    ]

    @pl.when(i == 0)
    def _():
        greet(
            [(place.fsdp_of(m), place.r) for m in range(1, 8)]
            + [place.y_dev(), place.core_dev(), (place.f, 3 - place.r)]
        )
        for copy in bulk_copies:
            copy.start()
        normed_t[...] = jnp.transpose(normed_in[...])

    cos_tab, sin_tab = cos_ref[...], sin_ref[...]
    product = jnp.transpose(mixed_ref[...].astype(jnp.float32) * go_ref[...].astype(jnp.float32))
    flipped = jnp.transpose(k_ref[...])
    gq_parts, gk_parts, gv_parts = [], [], []
    slot = 0
    for head in range(PAIR // HDIM):
        cols = slice(head * HDIM, (head + 1) * HDIM)
        delta = jnp.sum(product[cols, :], axis=0, keepdims=True)
        keys = jnp.concatenate([k_ref[:, cols], km[...]], axis=1)
        values = v_ref[:, cols]
        grad_k = jnp.zeros((length, HDIM), jnp.float32)
        grad_v = jnp.zeros((length, HDIM), jnp.float32)
        grad_q = []
        for begin in range(0, length, QROWS):
            run_slot(slot)
            slot += 1
            span = slice(begin, begin + QROWS)
            low_q, low_go = q_ref[span, cols], go_ref[span, cols]
            scores = rows_dot(keys, jnp.concatenate([low_q, qm[span, :]], axis=1))
            probs = jnp.exp(scores - lse_ref[0, head : head + 1, span])
            grad_v += jnp.dot(probs.astype(jnp.bfloat16), low_go, preferred_element_type=jnp.float32)
            grad_p = rows_dot(values, low_go)
            grad_s = (probs * (grad_p - delta[:, span])).astype(jnp.bfloat16)
            grad_k += jnp.dot(grad_s, low_q, preferred_element_type=jnp.float32)
            grad_q.append(jnp.dot(flipped[cols, :], grad_s, preferred_element_type=jnp.float32))
        gq_parts.append(jnp.concatenate(grad_q, axis=1))
        gk_parts.append(grad_k)
        gv_parts.append(grad_v)
    grad_q = jnp.transpose(jnp.concatenate(gq_parts, axis=0)) * 0.125
    grad_k = jnp.concatenate(gk_parts, axis=1)
    gp = jnp.concatenate(
        [
            (grad_q * cos_tab + swap_halves(grad_q * sin_tab)).astype(jnp.bfloat16),
            (grad_k * cos_tab + swap_halves(grad_k * sin_tab)).astype(jnp.bfloat16),
            jnp.concatenate(gv_parts, axis=1).astype(jnp.bfloat16),
        ],
        axis=1,
    )
    gp_all[i] = gp
    term = jnp.dot(normed_t[...], gp, preferred_element_type=jnp.float32)
    terms[i] = term.astype(jnp.bfloat16).reshape(4, 2, part, 3 * PAIR)
    run_slot(slots)

    def rep_copy(m):
        return remote(
            gain_rep.at[place.r],
            gain_rep.at[place.r],
            rep_send.at[m - 1],
            rep_recv.at[m - 1],
            (place.f, (place.y_dev()[1], place.core_dev()[1], 3 - place.r)[m - 1]),
        )

    def fsdp_copy(m):
        return remote(
            gain_parts.at[place.fsdp_of(m)],
            gain_all.at[place.f],
            fsdp_send.at[m - 1],
            fsdp_recv.at[m - 1],
            (place.fsdp_of(m), place.r),
        )

    @pl.when(i == npairs - 1)
    def _():
        for copy in bulk_copies:
            copy.wait()
        gain = gain_ref[0:1, :]
        blocks = length // QROWS
        share = len(events) // (blocks + 1)
        first = jnp.zeros((1, width), jnp.float32)
        writes = []
        for b in range(blocks):
            rows = slice(b * QROWS, (b + 1) * QROWS)
            e1 = jnp.zeros((QROWS, width), jnp.float32)
            for p in range(npairs):
                e1 += rows_dot(gp_all[p, rows, :], wq_buf[p].reshape(width, 3 * PAIR))
            v = x_buf[rows, :].astype(jnp.float32)
            c = v - jnp.mean(v, axis=1, keepdims=True)
            r1 = lax.rsqrt(jnp.mean(c * c, axis=1, keepdims=True) + eps)
            n1 = c * r1
            first += jnp.sum(e1 * n1, axis=0, keepdims=True)
            f1 = e1 * gain
            drift = f1 - jnp.mean(f1, axis=1, keepdims=True)
            gm_buf[rows, :] += r1 * (drift - n1 * jnp.mean(f1 * n1, axis=1, keepdims=True))
            write = pltpu.make_async_copy(gm_buf.at[rows, :], input_grad.at[rows, :], out_sem.at[b])
            write.start()
            writes.append(write)
            for _ in range(2):
                if events:
                    reduce.step(*events.pop(0)[1:])
        sub = lax.broadcasted_iota(jnp.int32, (8, width), 0)
        gain_rep[place.r] = jnp.where(sub == 0, first, jnp.where(sub == 1, second_ref[...], 0.0))
        for m in (1, 2, 3):
            rep_copy(m).start()
        for m in (1, 2, 3):
            rep_copy(m).wait()
        total = gain_rep[0] + gain_rep[1] + gain_rep[2] + gain_rep[3]
        gain_parts[...] = jnp.zeros_like(gain_parts)
        for f in range(8):
            gain_parts[f, :, :part] = total[:, f * part : (f + 1) * part]
        for m in range(1, 8):
            fsdp_copy(m).start()
        gain_all[place.f] = gain_parts[place.f]
        while events:
            reduce.step(*events.pop(0)[1:])
        for m in range(1, 8):
            fsdp_copy(m).wait()
        shared = gain_all[0]
        for f in range(1, 8):
            shared += gain_all[f]
        gain_out[...] = shared
        for write in writes:
            write.wait()
        reduce.finish()


def backward(
    queries, keyset, valueset, mixed, grad_mixed, lse, cos_tab, sin_tab, qm, km, gains, second_term,
    normed_one, layer_input, grad_middle, wq_all, narrow_term, wide_term, attn_term,
):
    length, width = queries.shape
    pairs, part = width // PAIR, width // 8
    cuts = [cuts_of(t.shape[1], 3 * PAIR) for t in (narrow_term, wide_term, attn_term)]
    count = pairs + sum(len(c) for c in cuts)
    cols = 3 * PAIR
    block = pl.BlockSpec((length, PAIR), lambda i: (0, i))
    whole = pl.BlockSpec(memory_space=pltpu.VMEM)
    hbm = pl.BlockSpec(memory_space=pl.ANY)
    low = lambda *shape: pltpu.VMEM(shape, jnp.bfloat16)
    wide = lambda *shape: pltpu.VMEM(shape, jnp.float32)
    f32 = lambda *shape: jax.ShapeDtypeStruct(shape, jnp.float32)
    dma = pltpu.SemaphoreType.DMA
    terms = [t.reshape(4, 2, part, t.shape[1]) for t in (narrow_term, wide_term, attn_term)]
    return pl.pallas_call(
        functools.partial(backward_kernel, (pairs, cuts)),
        grid=(pairs,),
        in_specs=[block] * 5
        + [pl.BlockSpec((1, 2, length), lambda i: (i, 0, 0))]
        + [whole] * 7
        + [hbm] * 6,
        out_specs=[hbm] + [whole] * 5,
        out_shape=[
            f32(length, width),
            f32(pairs, part, cols),
            f32(part, attn_term.shape[1]),
            f32(part, wide_term.shape[1]),
            f32(part, narrow_term.shape[1]),
            f32(8, PAIR),
        ],
        scratch_shapes=[
            low(width, length),
            low(length, width),
            wide(length, width),
            low(pairs, 4, 2, part, cols),
            low(pairs, length, cols),
            low(pairs, 4, 2, part, cols),
            low(count, 4, 2, HALF, cols),
            low(count, 4, 2, HALF, cols),
            low(count, 4, 2, STEP, cols),
            low(count, 4, 2 * STEP, cols),
            low(count, 3, 2 * STEP, cols),
            low(count, 2 * STEP, cols),
            low(count, 2 * STEP, cols),
            low(count, HALF, cols),
            low(count, HALF, cols),
            wide(4, 8, width),
            wide(8, 8, PAIR),
            wide(8, 8, PAIR),
            dma((count, 8)),
            dma((count, 8)),
            dma((count,)),
            dma((3,)),
            dma((3,)),
            dma((3,)),
            dma((7,)),
            dma((7,)),
            dma((length // QROWS,)),
        ],
        compiler_params=pltpu.CompilerParams(
            vmem_limit_bytes=62 << 20, collective_id=1, has_side_effects=True
        ),
        cost_estimate=pl.CostEstimate(
            flops=60 * width * length * length, bytes_accessed=40 * length * width,
            transcendentals=pairs * 2 * length * length,
        ),
    )(
        queries, keyset, valueset, mixed, grad_mixed, lse, cos_tab, sin_tab, qm, km, gains, second_term,
        normed_one, layer_input, grad_middle, wq_all, *terms,
    )


def erf_poly(x):
    x = jnp.clip(x, -3.832506856900711, 3.832506856900711)
    sq = x * x
    top = jnp.float32(0.00022905065861350646)
    for coef in (0.0034082910107109506, 0.050955695062380861, 0.18520832239976145, 1.128379143519084):
        top = top * sq + coef
    low = jnp.float32(-1.1791602954361697e-7)
    for coef in (
        0.000023547966471313185, 0.0010179625278914885, 0.014070470171167667, 0.11098505178285362,
        0.49746925110067538, 1.0,
    ):
        low = low * sq + coef
    return x * top / low


def middle_kernel(
    x_ref, mixed_ref, og_ref, km_ref, gain_ref, wa, ww, wn,
    layer_out, go_out, gm_out, second_out, narrow_out, wide_out, attn_out,
    hidden_all, gl_all, gml_all, gt_t, n2_t, mixed_t,
):
    i = pl.program_id(0)
    rows_here, width = x_ref.shape
    half_ff = wn.shape[1]
    tiles = 8
    piece = 3 * PAIR
    rows = pl.ds(pl.multiple_of(i * rows_here, rows_here), rows_here)
    gain = gain_ref[1:2, :]
    mixed = mixed_ref[...]
    middle = x_ref[...].astype(jnp.float32) + jnp.dot(mixed, wa[...], preferred_element_type=jnp.float32)
    c = middle - jnp.mean(middle, axis=1, keepdims=True)
    r2 = lax.rsqrt(jnp.mean(c * c, axis=1, keepdims=True) + eps)
    n2 = c * r2
    low_n2 = (n2 * gain).astype(jnp.bfloat16)
    live = jnp.where(km_ref[:, tiles : tiles + 1].astype(jnp.float32) < -1.0, 0.0, 1.0)
    gt = og_ref[...].astype(jnp.float32) * live
    low_gt = gt.astype(jnp.bfloat16)
    gt_t[:, rows] = jnp.transpose(low_gt)
    n2_t[:, rows] = jnp.transpose(low_n2)
    mixed_t[:, rows] = jnp.transpose(mixed)
    e = jnp.zeros((rows_here, width), jnp.float32)
    out = middle
    for lo in range(0, half_ff, piece):
        at, up = slice(lo, lo + piece), slice(half_ff + lo, half_ff + lo + piece)
        a = jnp.dot(low_n2, ww[:, at], preferred_element_type=jnp.float32)
        gate = jnp.dot(low_n2, ww[:, up], preferred_element_type=jnp.float32)
        gh = jnp.dot(low_gt, wn[:, at], preferred_element_type=jnp.float32)
        cdf = 0.5 + 0.5 * erf_poly(a * (2.0 ** -0.5))
        act = a * cdf
        slope = cdf + a * jnp.exp(a * a * -0.5) * ((2.0 * math.pi) ** -0.5)
        hidden = (act * gate).astype(jnp.bfloat16)
        gl_a = (gh * gate * slope).astype(jnp.bfloat16)
        gl_g = (gh * act).astype(jnp.bfloat16)
        hidden_all[rows, at] = hidden
        gl_all[rows, at] = gl_a
        gl_all[rows, up] = gl_g
        out += rows_dot(hidden, wn[:, at])
        e += rows_dot(gl_a, ww[:, at]) + rows_dot(gl_g, ww[:, up])
    layer_out[...] = out.astype(jnp.bfloat16)
    f2 = e * gain
    gm = gt + r2 * (f2 - jnp.mean(f2, axis=1, keepdims=True) - n2 * jnp.mean(f2 * n2, axis=1, keepdims=True))
    gm_out[...] = gm
    low_gm = gm.astype(jnp.bfloat16)
    gml_all[rows, :] = low_gm
    go_out[...] = rows_dot(low_gm, wa[...]).astype(jnp.bfloat16)
    part = jnp.sum(e * n2, axis=0, keepdims=True)

    @pl.when(i == 0)
    def _():
        second_out[...] = part

    @pl.when(i > 0)
    def _():
        second_out[...] += part

    @pl.when(i == pl.num_programs(0) - 1)
    def _():
        for left, right, term in (
            (gt_t, hidden_all, narrow_out), (n2_t, gl_all, wide_out), (mixed_t, gml_all, attn_out)
        ):
            for lo in range(0, right.shape[1], piece):
                at = slice(lo, lo + piece)
                term[:, at] = jnp.dot(
                    left[...], right[:, at], preferred_element_type=jnp.float32
                ).astype(jnp.bfloat16)


def middle_part(layer_input, mixed, out_grad, km, gains, wa, ww, wn):
    length, width = layer_input.shape
    half_ff = wn.shape[1]
    tile = 2 * TILE
    block = pl.BlockSpec((tile, width), lambda i: (i, 0))
    whole = pl.BlockSpec(memory_space=pltpu.VMEM)
    shape = jax.ShapeDtypeStruct
    low = lambda *dims: pltpu.VMEM(dims, jnp.bfloat16)
    return pl.pallas_call(
        middle_kernel,
        grid=(length // tile,),
        in_specs=[block] * 3 + [pl.BlockSpec((tile, HDIM), lambda i: (i, 0))] + [whole] * 4,
        out_specs=[block] * 3 + [whole] * 4,
        out_shape=[
            shape((length, width), jnp.bfloat16),
            shape((length, width), jnp.bfloat16),
            shape((length, width), jnp.float32),
            shape((1, width), jnp.float32),
            shape((width, half_ff), jnp.bfloat16),
            shape((width, 2 * half_ff), jnp.bfloat16),
            shape((width, width), jnp.bfloat16),
        ],
        scratch_shapes=[
            low(length, half_ff),
            low(length, 2 * half_ff),
            low(length, width),
            low(width, length),
            low(width, length),
            low(width, length),
        ],
        compiler_params=pltpu.CompilerParams(vmem_limit_bytes=60 << 20),
    )(layer_input, mixed, out_grad, km, gains, wa, ww, wn)


def on_device(
    layer_input,
    qkv_weight,
    attn_weight,
    wide_weight,
    narrow_weight,
    first_gain,
    second_gain,
    out_grad,
    token_seg,
    token_live,
):
    gains = jnp.stack([first_gain, second_gain], axis=1)
    gains = jnp.pad(gains, ((0, 0), (0, PAIR - 2)))
    qkv_full, gains = gather_weights([qkv_weight, gains])
    attn_full, wide_full, narrow_full = gather_weights([attn_weight, wide_weight, narrow_weight])
    scale_one = gains[:, 0].astype(jnp.float32)
    scale_two = gains[:, 1].astype(jnp.float32)
    residual_in = layer_input.astype(jnp.float32)
    qm, km = mask_columns(token_seg, token_live)
    cos_tab, sin_tab = rope_tables(token_seg)
    normed_one = layer_norm(residual_in, scale_one).astype(jnp.bfloat16)
    packed = jnp.dot(normed_one, qkv_full, preferred_element_type=jnp.float32)
    queries, keyset, valueset, mixed_rows, lse = attend(packed, cos_tab, sin_tab, qm, km)
    middle = residual_in + jnp.dot(mixed_rows, attn_full, preferred_element_type=jnp.float32)
    normed_two = layer_norm(middle, scale_two).astype(jnp.bfloat16)
    lifted = jnp.dot(normed_two, wide_full, preferred_element_type=jnp.float32)
    hidden = geglu(lifted).astype(jnp.bfloat16)
    layer_out = middle + jnp.einsum(
        "tf,df->td", hidden, narrow_full, preferred_element_type=jnp.float32
    )
    grad_top = out_grad.astype(jnp.float32) * token_live.astype(jnp.float32)[:, None]
    grad_top_low = grad_top.astype(jnp.bfloat16)
    narrow_term = jnp.einsum("td,tf->df", grad_top_low, hidden, preferred_element_type=jnp.float32)
    grad_hidden = jnp.dot(grad_top_low, narrow_full, preferred_element_type=jnp.float32)
    _, pull_gate = jax.vjp(geglu, lifted)
    grad_lifted = pull_gate(grad_hidden)[0].astype(jnp.bfloat16)
    wide_term = jnp.einsum("td,tf->df", normed_two, grad_lifted, preferred_element_type=jnp.float32)
    grad_norm_two = jnp.einsum(
        "tf,df->td", grad_lifted, wide_full, preferred_element_type=jnp.float32
    )
    _, pull_two = jax.vjp(layer_norm, middle, scale_two)
    grad_mid_ln, second_term = pull_two(grad_norm_two)
    grad_middle = grad_top + grad_mid_ln
    grad_middle_low = grad_middle.astype(jnp.bfloat16)
    attn_term = jnp.einsum(
        "td,te->de", mixed_rows, grad_middle_low, preferred_element_type=jnp.float32
    )
    grad_mixed = jnp.einsum(
        "te,de->td", grad_middle_low, attn_full, preferred_element_type=jnp.float32
    )
    shares = scatter_sums([narrow_term, wide_term, attn_term])
    grad_parts = attend_back(
        queries, keyset, valueset, mixed_rows, grad_mixed.astype(jnp.bfloat16), lse,
        cos_tab, sin_tab, qm, km,
    )
    grad_packed = jnp.concatenate(grad_parts, axis=1)
    qkv_term = jnp.einsum("td,tf->df", normed_one, grad_packed, preferred_element_type=jnp.float32)
    grad_norm_one = jnp.einsum(
        "tf,df->td", grad_packed, qkv_full, preferred_element_type=jnp.float32
    )
    _, pull_one = jax.vjp(layer_norm, residual_in, scale_one)
    grad_in_ln, first_term = pull_one(grad_norm_one)
    input_grad = grad_middle + grad_in_ln
    gain_terms = jnp.stack([first_term, second_term], axis=1)
    gain_terms = jnp.pad(gain_terms, ((0, 0), (0, PAIR - 2)))
    qkv_share, gain_share = scatter_sums([qkv_term, gain_terms])
    return (
        layer_out.astype(jnp.bfloat16),
        input_grad,
        qkv_share,
        shares[2],
        shares[1],
        shares[0],
        gain_share[:, 0],
        gain_share[:, 1],
    )


def on_device_tuned(
    layer_input,
    qkv_weight,
    attn_weight,
    wide_weight,
    narrow_weight,
    first_gain,
    second_gain,
    out_grad,
    token_seg,
    token_live,
):
    length, width = layer_input.shape
    pairs, part = width // PAIR, attn_weight.shape[0]
    wq_in = qkv_weight.reshape(part, 3, pairs, PAIR).transpose(2, 0, 1, 3).reshape(pairs, part, 3 * PAIR)
    gain_in = jnp.pad(jnp.stack([first_gain, second_gain]).astype(jnp.float32), ((0, 6), (0, PAIR - part)))
    (queries, keyset, valueset, mixed_rows, lse, normed_one, gains, wq_all, wa_all, ww_all, wn_all,
     cos_tab, sin_tab, qm, km) = forward(
        layer_input, wq_in, attn_weight, wide_weight, narrow_weight, gain_in, token_seg, token_live
    )
    attn_full, wide_full, narrow_full = (w.reshape(width, w.shape[-1]) for w in (wa_all, ww_all, wn_all))
    layer_out, grad_mixed, grad_middle, second_term, *low_terms = middle_part(
        layer_input, mixed_rows, out_grad, km, gains, attn_full, wide_full, narrow_full
    )
    input_grad, qkv_share, attn_share, wide_share, narrow_share, gain_share = backward(
        queries, keyset, valueset, mixed_rows, grad_mixed, lse, cos_tab, sin_tab, qm, km,
        gains, second_term, normed_one, layer_input, grad_middle, wq_all, *low_terms,
    )
    qkv_share = qkv_share.reshape(pairs, part, 3, PAIR).transpose(1, 2, 0, 3).reshape(part, 3 * width)
    return (
        layer_out,
        input_grad,
        qkv_share,
        attn_share,
        wide_share,
        narrow_share,
        gain_share[0, :part],
        gain_share[1, :part],
    )


def solution(mesh):
    tuned = mesh.shape["fsdp"] == 8 and mesh.shape["rep"] == 4
    return jax.shard_map(
        on_device_tuned if tuned else on_device,
        mesh=mesh,
        in_specs=(
            P(("fsdp", "rep"), None),
            P("fsdp", None),
            P("fsdp", None),
            P("fsdp", None),
            P("fsdp", None),
            P("fsdp"),
            P("fsdp"),
            P(("fsdp", "rep"), None),
            P(("fsdp", "rep")),
            P(("fsdp", "rep")),
        ),
        out_specs=(
            P(("fsdp", "rep"), None),
            P(("fsdp", "rep"), None),
            P("fsdp", None),
            P("fsdp", None),
            P("fsdp", None),
            P("fsdp", None),
            P("fsdp"),
            P("fsdp"),
        ),
        check_vma=False,
    )
```

```python
import functools
import math

import jax
import jax.numpy as jnp
import numpy as np
from jax import lax
from jax.experimental import pallas as pl
from jax.experimental.pallas import tpu as pltpu
from jax.sharding import PartitionSpec as P

HDIM = 64
TILE = 128
PAIR = 128
QROWS = 256


rope_base = 160000.0
eps = 1e-05
masked_score = -1e30


def layer_norm(values, scales):
    center = values - jnp.mean(values, axis=-1, keepdims=True)
    spread = jnp.mean(center * center, axis=-1, keepdims=True)
    return center * lax.rsqrt(spread + eps) * scales


def rope_tables(seg_rows):
    length = seg_rows.shape[0]
    firsts = seg_rows[::TILE]
    before = jnp.sum((firsts[None, :] < seg_rows[:, None]).astype(jnp.int32), axis=1)
    places = jnp.arange(length, dtype=jnp.int32) - TILE * before
    freq_index = jnp.arange(HDIM // 2, dtype=jnp.float32)
    inverse = jnp.exp(freq_index * (-2.0 * math.log(rope_base) / HDIM))
    angles = places.astype(jnp.float32)[:, None] * inverse[None, :]
    cosine, sine = jnp.cos(angles), jnp.sin(angles)
    cos_tab = jnp.concatenate([cosine] * 4, axis=1)
    sin_tab = jnp.concatenate([-sine, sine, -sine, sine], axis=1)
    return cos_tab, sin_tab


def mask_columns(seg_rows, live_rows):
    length = seg_rows.shape[0]
    firsts = seg_rows[::TILE]
    same = seg_rows[:, None] == firsts[None, :]
    query_cols = jnp.where(same, 0.0, masked_score)
    key_cols = jnp.where(same, 1.0, 0.0)
    query_cols = jnp.concatenate([query_cols, jnp.ones((length, 1))], axis=1)
    dead = jnp.where(live_rows > 0, 0.0, masked_score)[:, None]
    key_cols = jnp.concatenate([key_cols, dead], axis=1)
    spare = ((0, 0), (0, HDIM - query_cols.shape[1]))
    return (
        jnp.pad(query_cols, spare).astype(jnp.bfloat16),
        jnp.pad(key_cols, spare).astype(jnp.bfloat16),
    )


def swap_halves(values):
    lane = lax.broadcasted_iota(jnp.int32, values.shape, 1)
    return jnp.where(
        lane % HDIM < HDIM // 2,
        pltpu.roll(values, PAIR - HDIM // 2, 1),
        pltpu.roll(values, HDIM // 2, 1),
    )


def rows_dot(left, right):
    return lax.dot_general(left, right, (((1,), (1,)), ((), ())), preferred_element_type=jnp.float32)


def attend_kernel(pq, pk, pv, cos_ref, sin_ref, qm, km, q_out, k_out, v_out, mixed_out, lse_out):
    cos_tab, sin_tab = cos_ref[...], sin_ref[...]
    length = cos_tab.shape[0]
    q_out[...] = ((pq[...] * cos_tab + swap_halves(pq[...]) * sin_tab).astype(jnp.bfloat16)) * 0.125
    k_out[...] = (pk[...] * cos_tab + swap_halves(pk[...]) * sin_tab).astype(jnp.bfloat16)
    v_out[...] = pv[...].astype(jnp.bfloat16)
    flipped = jnp.transpose(v_out[...])
    for begin in range(0, length, QROWS):
        parts = []
        for head in range(PAIR // HDIM):
            cols = slice(head * HDIM, (head + 1) * HDIM)
            keys = jnp.concatenate([k_out[:, cols], km[...]], axis=1)
            rows = jnp.concatenate(
                [q_out[begin : begin + QROWS, cols], qm[begin : begin + QROWS, :]], axis=1
            )
            scores = rows_dot(keys, rows)
            top = jnp.max(scores, axis=0, keepdims=True)
            expo = jnp.exp(scores - top)
            total = jnp.sum(expo, axis=0, keepdims=True)
            lse_out[0, head : head + 1, begin : begin + QROWS] = top + jnp.log(total)
            out = jnp.dot(
                flipped[cols, :], expo.astype(jnp.bfloat16), preferred_element_type=jnp.float32
            )
            parts.append(out / total)
        both = jnp.concatenate(parts, axis=0)
        mixed_out[begin : begin + QROWS, :] = jnp.transpose(both).astype(jnp.bfloat16)


def attend_back_kernel(
    q_ref, k_ref, v_ref, mixed_ref, go_ref, lse_ref, cos_ref, sin_ref, qm, km, gq_out, gk_out, gv_out
):
    cos_tab, sin_tab = cos_ref[...], sin_ref[...]
    length = cos_tab.shape[0]
    product = jnp.transpose(mixed_ref[...].astype(jnp.float32) * go_ref[...].astype(jnp.float32))
    flipped = jnp.transpose(k_ref[...])
    gq_parts, gk_parts, gv_parts = [], [], []
    for head in range(PAIR // HDIM):
        cols = slice(head * HDIM, (head + 1) * HDIM)
        delta = jnp.sum(product[cols, :], axis=0, keepdims=True)
        keys = jnp.concatenate([k_ref[:, cols], km[...]], axis=1)
        values = v_ref[:, cols]
        grad_k = jnp.zeros((length, HDIM), jnp.float32)
        grad_v = jnp.zeros((length, HDIM), jnp.float32)
        grad_q = []
        for begin in range(0, length, QROWS):
            span = slice(begin, begin + QROWS)
            low_q, low_go = q_ref[span, cols], go_ref[span, cols]
            scores = rows_dot(keys, jnp.concatenate([low_q, qm[span, :]], axis=1))
            probs = jnp.exp(scores - lse_ref[0, head : head + 1, span])
            grad_v += jnp.dot(probs.astype(jnp.bfloat16), low_go, preferred_element_type=jnp.float32)
            grad_p = rows_dot(values, low_go)
            grad_s = (probs * (grad_p - delta[:, span])).astype(jnp.bfloat16)
            grad_k += jnp.dot(grad_s, low_q, preferred_element_type=jnp.float32)
            grad_q.append(jnp.dot(flipped[cols, :], grad_s, preferred_element_type=jnp.float32))
        gq_parts.append(jnp.concatenate(grad_q, axis=1))
        gk_parts.append(grad_k)
        gv_parts.append(grad_v)
    grad_q = jnp.transpose(jnp.concatenate(gq_parts, axis=0)) * 0.125
    grad_k = jnp.concatenate(gk_parts, axis=1)
    gq_out[...] = (grad_q * cos_tab + swap_halves(grad_q * sin_tab)).astype(jnp.bfloat16)
    gk_out[...] = (grad_k * cos_tab + swap_halves(grad_k * sin_tab)).astype(jnp.bfloat16)
    gv_out[...] = jnp.concatenate(gv_parts, axis=1).astype(jnp.bfloat16)


def attend(packed, cos_tab, sin_tab, qm, km):
    length, width = packed.shape[0], packed.shape[1] // 3
    pairs = width // PAIR
    block = lambda shift: pl.BlockSpec((length, PAIR), lambda i: (0, i + shift))
    table = pl.BlockSpec((length, PAIR), lambda i: (0, 0))
    mask = pl.BlockSpec((length, HDIM), lambda i: (0, 0))
    rows = jax.ShapeDtypeStruct((length, width), jnp.bfloat16)
    return pl.pallas_call(
        attend_kernel,
        grid=(pairs,),
        in_specs=[block(0), block(pairs), block(2 * pairs), table, table, mask, mask],
        out_specs=[block(0)] * 4 + [pl.BlockSpec((1, 2, length), lambda i: (i, 0, 0))],
        out_shape=[rows] * 4 + [jax.ShapeDtypeStruct((pairs, 2, length), jnp.float32)],
        compiler_params=pltpu.CompilerParams(vmem_limit_bytes=40 << 20),
        cost_estimate=pl.CostEstimate(
            flops=16 * width * length * length, bytes_accessed=20 * length * width,
            transcendentals=pairs * 2 * length * length,
        ),
    )(packed, packed, packed, cos_tab, sin_tab, qm, km)


def attend_back(queries, keyset, valueset, mixed, grad_mixed, lse, cos_tab, sin_tab, qm, km):
    length, width = queries.shape
    pairs = width // PAIR
    block = pl.BlockSpec((length, PAIR), lambda i: (0, i))
    table = pl.BlockSpec((length, PAIR), lambda i: (0, 0))
    mask = pl.BlockSpec((length, HDIM), lambda i: (0, 0))
    rows = jax.ShapeDtypeStruct((length, width), jnp.bfloat16)
    return pl.pallas_call(
        attend_back_kernel,
        grid=(pairs,),
        in_specs=[block] * 5
        + [pl.BlockSpec((1, 2, length), lambda i: (i, 0, 0)), table, table, mask, mask],
        out_specs=[block] * 3,
        out_shape=[rows] * 3,
        compiler_params=pltpu.CompilerParams(vmem_limit_bytes=48 << 20),
        cost_estimate=pl.CostEstimate(
            flops=40 * width * length * length, bytes_accessed=16 * length * width,
            transcendentals=pairs * 2 * length * length,
        ),
    )(queries, keyset, valueset, mixed, grad_mixed, lse, cos_tab, sin_tab, qm, km)


def swap_with(array, axis, bit):
    size = lax.axis_size(axis)
    return lax.ppermute(array, axis, [(i, i ^ (1 << bit)) for i in range(size)])


def side_of(axis, bit):
    return (lax.axis_index(axis) >> bit) & 1


def bits_of(axis):
    return [(axis, bit) for bit in reversed(range(lax.axis_size(axis).bit_length() - 1))]


def gather_half(piece, order):
    canon = bits_of("fsdp") + bits_of("rep")
    have = []
    for axis, bit in order:
        other = swap_with(piece, axis, bit)
        side = side_of(axis, bit) == 0
        place = sum(canon.index(known) < canon.index((axis, bit)) for known in have)
        piece = jnp.stack(
            [jnp.where(side, piece, other), jnp.where(side, other, piece)], axis=place
        )
        have.append((axis, bit))
    return piece.reshape(-1, piece.shape[-1])


def pick(array, dim, side):
    return lax.dynamic_index_in_dim(array, side, dim, keepdims=False)


def orders():
    rep_bits, fsdp_bits = bits_of("rep")[::-1], bits_of("fsdp")[::-1]
    near, far = rep_bits[0], rep_bits[1:]
    one = [near] + far + fsdp_bits
    two = [near] + fsdp_bits[:1] + far + fsdp_bits[1:]
    return one, two


def gather_weights(arrays):
    joint = jnp.concatenate(arrays, axis=1)
    for axis, bit in bits_of("rep"):
        size = joint.shape[0] // 2
        joint = lax.dynamic_slice_in_dim(joint, side_of(axis, bit) * size, size, axis=0)
    cut = joint.shape[1] // 256 * 128
    one, two = orders()
    whole = jnp.concatenate(
        [gather_half(joint[:, :cut], one[::-1]), gather_half(joint[:, cut:], two[::-1])], axis=1
    )
    outs, start = [], 0
    for array in arrays:
        outs.append(whole[:, start : start + array.shape[1]])
        start += array.shape[1]
    return outs


def scatter_half(term, order):
    canon = bits_of("fsdp") + bits_of("rep")
    rows = term.shape[0] >> len(canon)
    acc = term.reshape([2] * len(canon) + [rows, term.shape[1]])
    left = list(canon)
    for axis, bit in order:
        dim = left.index((axis, bit))
        side = side_of(axis, bit)
        other = swap_with(pick(acc, dim, 1 - side), axis, bit)
        acc = pick(acc, dim, side).astype(jnp.float32) + other.astype(jnp.float32)
        acc = acc.astype(jnp.bfloat16)
        left.remove((axis, bit))
    rep_order = [entry for entry in order[::-1] if entry[0] == "rep"]
    have = []
    for axis, bit in rep_order:
        other = swap_with(acc, axis, bit)
        side = side_of(axis, bit) == 0
        place = sum(canon.index(known) < canon.index((axis, bit)) for known in have)
        acc = jnp.stack([jnp.where(side, acc, other), jnp.where(side, other, acc)], axis=place)
        have.append((axis, bit))
    return acc.reshape(-1, acc.shape[-1]).astype(jnp.float32)


def scatter_sums(terms):
    joint = jnp.concatenate([term.astype(jnp.bfloat16) for term in terms], axis=1)
    cut = joint.shape[1] // 256 * 128
    one, two = orders()
    whole = jnp.concatenate(
        [scatter_half(joint[:, :cut], one), scatter_half(joint[:, cut:], two)], axis=1
    )
    outs, start = [], 0
    for term in terms:
        outs.append(whole[:, start : start + term.shape[1]])
        start += term.shape[1]
    return outs


def geglu(lifted):
    half_ff = lifted.shape[1] // 2
    return jax.nn.gelu(lifted[:, :half_ff], approximate=False) * lifted[:, half_ff:]


MESH = pl.DeviceIdType.MESH
HALF = 48
AHEAD = 4
FORWARD_CUT = 768
GATHER_LAGS = (3.0 - 2.1 * AHEAD, 3.0, 7.5, 12.0, 15.0)
PACE = 2.1
PAIR_US = 6.0
STEP = 16


def table_constants(length):
    places = np.arange(length, dtype=np.float32)
    freq_index = np.arange(HDIM // 2, dtype=np.float32)
    inverse = np.exp(freq_index * np.float32(-2.0 * math.log(rope_base) / HDIM)).astype(np.float32)
    angles = (places[:, None] * inverse[None, :]).astype(np.float32).astype(np.float64)
    cosine, sine = np.cos(angles), np.sin(angles)
    cos_tab = np.concatenate([cosine] * 4, axis=1).astype(np.float32)
    sin_tab = np.concatenate([-sine, sine, -sine, sine], axis=1).astype(np.float32)
    return cos_tab, sin_tab


class Place:
    def __init__(self):
        self.f = lax.axis_index("fsdp")
        self.r = lax.axis_index("rep")
        self.z = self.f // 2
        self.x = self.f % 2
        self.y = self.r // 2
        self.core = self.r % 2

    def flip(self, value, bit):
        size = 1 << bit
        return value + size - 2 * size * ((value // size) % 2)

    def along_z(self, d):
        z = self.z
        for bit in range(2):
            if (d >> bit) & 1:
                z = self.flip(z, bit)
        return z

    def fsdp_of(self, m):
        f = self.f
        for bit in range(3):
            if (m >> bit) & 1:
                f = self.flip(f, bit)
        return f

    def z_dev(self, d):
        return (2 * self.along_z(d) + self.x, self.r)

    def x_dev(self):
        return (self.flip(self.f, 0), self.r)

    def y_dev(self):
        return (self.f, self.flip(self.r, 1))

    def core_dev(self):
        return (self.f, self.flip(self.r, 0))

    def rows_zx(self):
        return pl.ds(pl.multiple_of(HALF * self.core + STEP * self.y, STEP), 2 * STEP)

    def rows_y(self):
        return pl.ds(pl.multiple_of(HALF * self.core + 2 * STEP * self.y, STEP), STEP)

    def rows_core(self):
        return pl.ds(pl.multiple_of(HALF * self.core, STEP), HALF)


def remote(src, dst, send, recv, dev):
    return pltpu.make_async_remote_copy(
        src_ref=src, dst_ref=dst, send_sem=send, recv_sem=recv, device_id=dev, device_id_type=MESH
    )


def staged(units, lags, pace):
    return sorted(
        (lag + pace * (sum(units[:k]) + stage * (unit - 1)), stage, k)
        for stage, lag in enumerate(lags)
        for k, unit in enumerate(units)
    )


class Gather:
    def __init__(self, place, sources, targets, send, recv, own):
        self.p, self.src, self.dst = place, sources, targets
        self.send, self.recv, self.own = send, recv, own
        self.count = len(sources)

    def z_copy(self, k, d):
        p, rows = self.p, self.p.rows_zx()
        return remote(
            self.src[k].at[rows, :],
            self.dst[k].at[p.z, p.x, rows, :],
            self.send.at[k, d - 1],
            self.recv.at[k, d - 1],
            p.z_dev(d),
        )

    def own_copy(self, k):
        p, rows = self.p, self.p.rows_zx()
        return pltpu.make_async_copy(
            self.src[k].at[rows, :], self.dst[k].at[p.z, p.x, rows, :], self.own.at[k]
        )

    def x_copy(self, k):
        p = self.p
        part = self.dst[k].at[:, p.x, p.rows_zx(), :]
        return remote(part, part, self.send.at[k, 3], self.recv.at[k, 3], p.x_dev())

    def y_copy(self, k):
        p = self.p
        part = self.dst[k].at[:, :, p.rows_y(), :]
        return remote(part, part, self.send.at[k, 4], self.recv.at[k, 4], p.y_dev())

    def core_copy(self, k):
        p = self.p
        part = self.dst[k].at[:, :, p.rows_core(), :]
        return remote(part, part, self.send.at[k, 5], self.recv.at[k, 5], p.core_dev())

    def step(self, stage, k):
        if stage == 0:
            self.own_copy(k).start()
            for d in (1, 2, 3):
                self.z_copy(k, d).start()
        elif stage == 1:
            self.own_copy(k).wait()
            for d in (1, 2, 3):
                self.z_copy(k, d).wait_recv()
            self.x_copy(k).start()
        elif stage == 2:
            self.x_copy(k).wait_recv()
            self.y_copy(k).start()
        elif stage == 3:
            self.y_copy(k).wait_recv()
            self.core_copy(k).start()
        else:
            self.core_copy(k).wait_recv()

    def finish(self):
        for k in range(self.count):
            for d in (1, 2, 3):
                self.z_copy(k, d).wait_send()
            self.x_copy(k).wait_send()
            self.y_copy(k).wait_send()
            self.core_copy(k).wait_send()


def greet(devices):
    barrier = pltpu.get_barrier_semaphore()
    for dev in devices:
        pl.semaphore_signal(barrier, inc=1, device_id=dev, device_id_type=MESH)
    pl.semaphore_wait(barrier, len(devices))


def forward_kernel(
    plan,
    seg_ref,
    x_ref,
    gain_in,
    live_ref,
    cos_in,
    sin_in,
    wq_in,
    wa_in,
    ww_in,
    wn_in,
    q_out,
    k_out,
    v_out,
    mixed_out,
    lse_out,
    normed_out,
    gain_out,
    wq_all,
    wa_all,
    ww_all,
    wn_all,
    cos_tab,
    sin_tab,
    qm,
    km,
    gain_send,
    gain_recv,
    wbuf,
    send,
    recv,
    own,
    gain_send_sem,
    gain_recv_sem,
    load_sem,
    score_buf,
):
    i = pl.program_id(0)
    pairs = pl.num_programs(0)
    npairs, cuts = plan
    place = Place()
    length, width = x_ref.shape
    tiles = length // TILE
    sources = [wq_in.at[k] for k in range(npairs)]
    targets = [wq_all.at[k] for k in range(npairs)]
    for cut, shard, full in zip(cuts, (wa_in, ww_in, wn_in), (wa_all, ww_all, wn_all)):
        for lo, size in cut:
            sources.append(shard.at[:, pl.ds(lo, size)])
            targets.append(full.at[:, :, :, pl.ds(lo, size)])
    gather = Gather(place, sources, targets, send, recv, own)

    units = [1] * npairs + [size / (3 * PAIR) for cut in cuts for _, size in cut]
    events = staged(units, GATHER_LAGS, PACE)
    events = [e for e in events if e[1:] not in [(0, k) for k in range(AHEAD)]]

    def run_until(time):
        while events and events[0][0] <= time:
            gather.step(*events.pop(0)[1:])

    def gain_copy(m):
        return remote(
            gain_send,
            gain_recv.at[place.f],
            gain_send_sem.at[m - 1],
            gain_recv_sem.at[m - 1],
            (place.fsdp_of(m), place.r),
        )

    def load(k):
        return pltpu.make_async_copy(wq_all.at[k], wbuf.at[k % 2], load_sem.at[k % 2])

    @pl.when(i == 0)
    def _():
        gain_send[...] = gain_in[...]
        greet(
            [(place.fsdp_of(m), place.r) for m in range(1, 8)] + [place.y_dev(), place.core_dev()]
        )
        for m in range(1, 8):
            gain_copy(m).start()
        for k in range(AHEAD):
            gather.step(0, k)
        gain_recv[place.f] = gain_in[...]
        lane_tile = lax.broadcasted_iota(jnp.int32, (TILE, HDIM), 1)
        live_cols = jnp.transpose(
            jnp.concatenate(
                [live_ref[...].astype(jnp.float32), jnp.zeros((TILE - tiles, TILE), jnp.float32)], axis=0
            )
        )
        segs = [seg_ref[u : u + 1, :] for u in range(tiles)]
        for t in range(tiles):
            rows = slice(t * TILE, (t + 1) * TILE)
            before = jnp.zeros((1, TILE), jnp.int32)
            same = jnp.zeros((TILE, HDIM), jnp.float32)
            for u in range(tiles):
                before += jnp.where(segs[u] < segs[t], 1, 0)
                hit = jnp.where(segs[u] == segs[t], 1.0, 0.0)[:, :HDIM]
                same = jnp.where(lane_tile == u, hit, same)
            cos_t, sin_t = cos_in[:TILE, :], sin_in[:TILE, :]
            for c in range(1, t + 1):
                at = slice(c * TILE, (c + 1) * TILE)
                cos_t = jnp.where(t - before == c, cos_in[at, :], cos_t)
                sin_t = jnp.where(t - before == c, sin_in[at, :], sin_t)
            cos_tab[rows, :] = cos_t
            sin_tab[rows, :] = sin_t
            dead = jnp.where(live_cols[:, t : t + 1] > 0, 0.0, masked_score)
            qv = jnp.where(lane_tile < tiles, jnp.where(same > 0, 0.0, masked_score), 0.0)
            qm[rows, :] = jnp.where(lane_tile == tiles, 1.0, qv).astype(jnp.bfloat16)
            kv = jnp.where(lane_tile == tiles, dead, same)
            km[rows, :] = kv.astype(jnp.bfloat16)
        run_until(3.0)
        for m in range(1, 8):
            gain_copy(m).wait()
        part = width // 8
        wide_row = lax.broadcasted_iota(jnp.int32, (PAIR, width), 0)
        wide_col = lax.broadcasted_iota(jnp.int32, (PAIR, width), 1)
        gains = jnp.zeros((8, width), jnp.float32)
        for f in range(8):
            pick_f = jnp.where((wide_col == wide_row + f * part) & (wide_row < part), 1.0, 0.0)
            gains += jnp.dot(
                gain_recv[f].astype(jnp.bfloat16),
                pick_f.astype(jnp.bfloat16),
                preferred_element_type=jnp.float32,
            )
        gain_out[...] = gains
        run_until(6.4)

        for b in range(tiles):
            rows = slice(b * TILE, (b + 1) * TILE)
            v = x_ref[rows, :].astype(jnp.float32)
            c = v - jnp.mean(v, axis=1, keepdims=True)
            spread = jnp.mean(c * c, axis=1, keepdims=True)
            normed_out[rows, :] = (c * lax.rsqrt(spread + eps) * gain_out[0:1, :]).astype(jnp.bfloat16)
            if b % 2:
                run_until(6.4 + b)
        run_until(GATHER_LAGS[4])
        load(0).start()
        load(0).wait()

    packed = jnp.dot(
        normed_out[...],
        wbuf[i % 2].reshape(width, 3 * PAIR),
        preferred_element_type=jnp.float32,
    )
    pq, pk, pv = packed[:, :PAIR], packed[:, PAIR : 2 * PAIR], packed[:, 2 * PAIR :]
    cos_v, sin_v = cos_tab[...], sin_tab[...]
    q_out[...] = ((pq * cos_v + swap_halves(pq) * sin_v).astype(jnp.bfloat16)) * 0.125
    k_out[...] = (pk * cos_v + swap_halves(pk) * sin_v).astype(jnp.bfloat16)
    v_out[...] = pv.astype(jnp.bfloat16)
    flipped = jnp.transpose(v_out[...])

    slots = 4
    queue = [[[] for _ in range(slots)] for _ in range(npairs)]
    for p in range(npairs):
        for slot in range(slots):
            now = GATHER_LAGS[4] + PAIR_US * (p + (slot + 1) / slots)
            while events and events[0][0] <= now:
                queue[p][slot].append(events.pop(0)[1:])
    queue[-1][-1].extend(e[1:] for e in events)

    def run_slot(slot):
        for p in range(npairs):

            @pl.when(i == p)
            def _():
                for stage, k in queue[p][slot]:
                    gather.step(stage, k)
                if p + 1 < npairs and slot == slots - 2:
                    load(p + 1).start()
                if p + 1 < npairs and slot == slots - 1:
                    load(p + 1).wait()

    parts = []
    for head in range(PAIR // HDIM):
        run_slot(2 * head)
        cols = slice(head * HDIM, (head + 1) * HDIM)
        keys = jnp.concatenate([k_out[:, cols], km[...]], axis=1)
        rows = jnp.concatenate([q_out[:, cols], qm[...]], axis=1)
        tops = []
        for begin in range(0, length, QROWS):
            scores = rows_dot(keys[begin : begin + QROWS, :], rows)
            score_buf[head, begin : begin + QROWS, :] = scores
            tops.append(jnp.max(scores.reshape(QROWS // 8, 8, length), axis=0))
        top = jnp.max(functools.reduce(jnp.maximum, tops), axis=0, keepdims=True)
        run_slot(2 * head + 1)
        out = jnp.zeros((HDIM, length), jnp.float32)
        sums = jnp.zeros((8, length), jnp.float32)
        for begin in range(0, length, QROWS):
            expo = jnp.exp(score_buf[head, begin : begin + QROWS, :] - top)
            sums += jnp.sum(expo.reshape(QROWS // 8, 8, length), axis=0)
            out += jnp.dot(
                flipped[cols, begin : begin + QROWS],
                expo.astype(jnp.bfloat16),
                preferred_element_type=jnp.float32,
            )
        total = jnp.sum(sums, axis=0, keepdims=True)
        lse_out[0, head : head + 1, :] = top + jnp.log(total)
        parts.append(out / total)
    mixed_out[...] = jnp.transpose(jnp.concatenate(parts, axis=0)).astype(jnp.bfloat16)

    @pl.when(i == pairs - 1)
    def _():
        gather.finish()


def cuts_of(width, piece):
    return [(lo, min(piece, width - lo)) for lo in range(0, width, piece)]


def forward(layer_input, wq_in, attn_weight, wide_weight, narrow_weight, gain_in, token_seg, token_live):
    length, width = layer_input.shape
    pairs = width // PAIR
    part = attn_weight.shape[0]
    cos_c, sin_c = table_constants(length)
    cuts = [cuts_of(w.shape[1], FORWARD_CUT) for w in (attn_weight, wide_weight, narrow_weight)]
    count = pairs + sum(len(c) for c in cuts)
    block = pl.BlockSpec((length, PAIR), lambda i: (0, i))
    whole = pl.BlockSpec(memory_space=pltpu.VMEM)
    hbm = pl.BlockSpec(memory_space=pl.ANY)
    rows = jax.ShapeDtypeStruct((length, width), jnp.bfloat16)
    full = lambda cols: jax.ShapeDtypeStruct((4, 2, part, cols), jnp.bfloat16)
    return pl.pallas_call(
        functools.partial(forward_kernel, (pairs, cuts)),
        grid=(pairs,),
        in_specs=[whole] * 6 + [hbm] * 4,
        out_specs=[block] * 4
        + [pl.BlockSpec((1, 2, length), lambda i: (i, 0, 0)), whole, whole]
        + [hbm] * 4
        + [whole] * 4,
        out_shape=[rows] * 4
        + [
            jax.ShapeDtypeStruct((pairs, 2, length), jnp.float32),
            rows,
            jax.ShapeDtypeStruct((8, width), jnp.float32),
            jax.ShapeDtypeStruct((pairs, 4, 2, part, 3 * PAIR), jnp.bfloat16),
            full(width),
            full(wide_weight.shape[1]),
            full(narrow_weight.shape[1]),
            jax.ShapeDtypeStruct((length, PAIR), jnp.float32),
            jax.ShapeDtypeStruct((length, PAIR), jnp.float32),
            jax.ShapeDtypeStruct((length, HDIM), jnp.bfloat16),
            jax.ShapeDtypeStruct((length, HDIM), jnp.bfloat16),
        ],
        scratch_shapes=[
            pltpu.VMEM((8, PAIR), jnp.float32),
            pltpu.VMEM((8, 8, PAIR), jnp.float32),
            pltpu.VMEM((2, 4, 2, part, 3 * PAIR), jnp.bfloat16),
            pltpu.SemaphoreType.DMA((count, 6)),
            pltpu.SemaphoreType.DMA((count, 6)),
            pltpu.SemaphoreType.DMA((count,)),
            pltpu.SemaphoreType.DMA((7,)),
            pltpu.SemaphoreType.DMA((7,)),
            pltpu.SemaphoreType.DMA((2,)),
            pltpu.VMEM((2, length, length), jnp.float32),
        ],
        compiler_params=pltpu.CompilerParams(
            vmem_limit_bytes=56 << 20, collective_id=0, has_side_effects=True
        ),
        cost_estimate=pl.CostEstimate(
            flops=22 * width * length * length, bytes_accessed=40 * length * width,
            transcendentals=pairs * 2 * length * length,
        ),
    )(
        token_seg.reshape(length // TILE, TILE), layer_input, gain_in,
        token_live.reshape(length // TILE, TILE),
        jnp.asarray(cos_c), jnp.asarray(sin_c), wq_in, attn_weight, wide_weight, narrow_weight,
    )


class Reduce:
    def __init__(self, place, sources, loaded, outs, bufs, send, recv, load):
        self.p, self.src, self.loaded, self.outs = place, sources, loaded, outs
        self.acc, self.rc, self.ry, self.rx, self.rz, self.s, self.ry2, self.f, self.rf = bufs
        self.send, self.recv, self.load = send, recv, load
        self.count = len(sources)

    def local(self, start, size):
        return pl.ds(pl.multiple_of(start, STEP), size)

    def mine(self):
        return self.local(STEP * self.p.y, 2 * STEP)

    def core_copy(self, k):
        p = self.p
        rows = self.local(HALF * (1 - p.core), HALF)
        return remote(
            self.src[k].at[:, :, rows, :], self.rc.at[k], self.send.at[k, 0], self.recv.at[k, 0], p.core_dev()
        )

    def load_copy(self, k):
        return pltpu.make_async_copy(
            self.src[k].at[:, :, self.p.rows_core(), :], self.acc.at[k], self.load.at[k]
        )

    def y_copy(self, k):
        p = self.p
        rows = self.local(2 * STEP * (1 - p.y), STEP)
        return remote(
            self.acc.at[k, :, :, rows, :], self.ry.at[k], self.send.at[k, 1], self.recv.at[k, 1], p.y_dev()
        )

    def x_copy(self, k):
        p = self.p
        return remote(
            self.acc.at[k, :, 1 - p.x, self.mine(), :],
            self.rx.at[k],
            self.send.at[k, 2],
            self.recv.at[k, 2],
            p.x_dev(),
        )

    def z_copy(self, k, d):
        p = self.p
        return remote(
            self.acc.at[k, p.along_z(d), p.x, self.mine(), :],
            self.rz.at[k, d - 1],
            self.send.at[k, 2 + d],
            self.recv.at[k, 2 + d],
            p.z_dev(d),
        )

    def y2_copy(self, k):
        return remote(
            self.s.at[k], self.ry2.at[k], self.send.at[k, 6], self.recv.at[k, 6], self.p.y_dev()
        )

    def core2_copy(self, k):
        return remote(
            self.f.at[k], self.rf.at[k], self.send.at[k, 7], self.recv.at[k, 7], self.p.core_dev()
        )

    def put(self, k, rows, sums):
        ref, starts = self.outs[k]
        size = sums.shape[1] // len(starts)
        for j, lo in enumerate(starts):
            ref[rows, lo : lo + size] = sums[:, j * size : (j + 1) * size].astype(jnp.float32)

    def plus(self, a, b):
        return (a.astype(jnp.float32) + b.astype(jnp.float32)).astype(jnp.bfloat16)

    def step(self, stage, k):
        p = self.p
        acc = self.acc
        if stage == 0:
            self.core_copy(k).start()
            if self.loaded[k]:
                self.load_copy(k).start()
        elif stage == 1:
            self.core_copy(k).wait_recv()
            if self.loaded[k]:
                self.load_copy(k).wait()
                acc[k] = self.plus(acc[k], self.rc[k])
            else:
                acc[k] = self.plus(self.src[k][:, :, p.rows_core(), :], self.rc[k])
            self.y_copy(k).start()
        elif stage == 2:
            self.y_copy(k).wait_recv()
            rows = self.local(2 * STEP * p.y, STEP)
            acc[k, :, :, rows, :] = self.plus(acc[k, :, :, rows, :], self.ry[k])
            self.x_copy(k).start()
        elif stage == 3:
            self.x_copy(k).wait_recv()
            rows = self.mine()
            acc[k, :, p.x, rows, :] = self.plus(acc[k, :, p.x, rows, :], self.rx[k])
            for d in (2, 3, 1):
                self.z_copy(k, d).start()
        elif stage == 4:
            total = acc[k, p.z, p.x, self.mine(), :].astype(jnp.float32)
            for d in (1, 2, 3):
                self.z_copy(k, d).wait_recv()
                total += self.rz[k, d - 1].astype(jnp.float32)
            self.s[k] = total.astype(jnp.bfloat16)
            self.y2_copy(k).start()
        elif stage == 5:
            self.y2_copy(k).wait_recv()
            low, high = self.local(STEP * p.y, STEP), self.local(STEP * (1 - p.y), STEP)
            self.f[k, self.local(2 * STEP * p.y, STEP), :] = self.s[k, low, :]
            self.f[k, STEP : 2 * STEP, :] = self.plus(self.s[k, high, :], self.ry2[k, low, :])
            self.f[k, self.local(2 * STEP * (1 - p.y), STEP), :] = self.ry2[k, high, :]
            self.core2_copy(k).start()
            self.put(k, p.rows_core(), self.f[k])
        else:
            self.core2_copy(k).wait_recv()
            self.put(k, self.local(HALF * (1 - p.core), HALF), self.rf[k])

    def finish(self):
        for k in range(self.count):
            self.core_copy(k).wait_send()
            self.y_copy(k).wait_send()
            self.x_copy(k).wait_send()
            for d in (1, 2, 3):
                self.z_copy(k, d).wait_send()
            self.y2_copy(k).wait_send()
            self.core2_copy(k).wait_send()


REDUCE_LAGS = (0.0, 4.0, 10.0, 16.0, 22.0, 28.0, 32.0)
BACK_US = 8.6
SPACING = 4


def reduce_events(given, pairs):
    now, first, late, starts = 0.0, 0, 0, {}
    while first < given or late < pairs:
        if late < pairs and BACK_US * (late + 1) <= now:
            starts[given + late] = BACK_US * (late + 1)
            late += 1
        elif first < given:
            starts[first] = now
            first += 1
        else:
            now = BACK_US * (late + 1)
            continue
        now += 2.35
    return sorted((t + lag, stage, k) for k, t in starts.items() for stage, lag in enumerate(REDUCE_LAGS))


def backward_kernel(
    plan,
    q_ref,
    k_ref,
    v_ref,
    mixed_ref,
    go_ref,
    lse_ref,
    cos_ref,
    sin_ref,
    qm,
    km,
    gain_ref,
    second_ref,
    normed_in,
    x_in,
    gm_in,
    wq_in,
    narrow_in,
    wide_in,
    attn_in,
    input_grad,
    qkv_out,
    attn_out,
    wide_out,
    narrow_out,
    gain_out,
    normed_t,
    x_buf,
    gm_buf,
    wq_buf,
    gp_all,
    terms,
    acc,
    rc,
    ry,
    rx,
    rz,
    s_buf,
    ry2,
    f_buf,
    rf,
    gain_rep,
    gain_parts,
    gain_all,
    send,
    recv,
    load,
    bulk,
    rep_send,
    rep_recv,
    fsdp_send,
    fsdp_recv,
    out_sem,
):
    i = pl.program_id(0)
    npairs, cuts = plan
    place = Place()
    length, width = normed_in.shape
    part = width // 8
    sources, loaded, outs = [], [], []
    for cut, term, out in zip(cuts, (narrow_in, wide_in, attn_in), (narrow_out, wide_out, attn_out)):
        for lo, size in cut:
            sources.append(term.at[:, :, :, pl.ds(lo, size)])
            outs.append((out, [lo]))
            loaded.append(True)
    given = len(sources)
    for p in range(npairs):
        sources.append(terms.at[p])
        outs.append((qkv_out, [j * width + p * PAIR for j in range(3)]))
        loaded.append(False)
    bufs = (acc, rc, ry, rx, rz, s_buf, ry2, f_buf, rf)
    reduce = Reduce(place, sources, loaded, outs, bufs, send, recv, load)
    events = reduce_events(given, npairs)
    slots = 2 * (length // QROWS)
    queue = [[[] for _ in range(slots + 1)] for _ in range(npairs)]
    for p in range(npairs):
        for slot in range(slots + 1):
            now = BACK_US * (p + min(slot, slots - 0.01) / slots) if slot < slots else BACK_US * (p + 1)
            if slot % SPACING:
                continue
            while events and events[0][0] <= now:
                queue[p][slot].append(events.pop(0)[1:])

    def run_slot(slot):
        for p in range(npairs):
            if queue[p][slot]:

                @pl.when(i == p)
                def _():
                    for stage, k in queue[p][slot]:
                        reduce.step(stage, k)

    bulk_copies = [
        pltpu.make_async_copy(x_in, x_buf, bulk.at[0]),
        pltpu.make_async_copy(gm_in, gm_buf, bulk.at[1]),
        pltpu.make_async_copy(wq_in, wq_buf, bulk.at[2]),
    ]

    @pl.when(i == 0)
    def _():
        greet(
            [(place.fsdp_of(m), place.r) for m in range(1, 8)]
            + [place.y_dev(), place.core_dev(), (place.f, 3 - place.r)]
        )
        for copy in bulk_copies:
            copy.start()
        normed_t[...] = jnp.transpose(normed_in[...])

    cos_tab, sin_tab = cos_ref[...], sin_ref[...]
    product = jnp.transpose(mixed_ref[...].astype(jnp.float32) * go_ref[...].astype(jnp.float32))
    flipped = jnp.transpose(k_ref[...])
    gq_parts, gk_parts, gv_parts = [], [], []
    slot = 0
    for head in range(PAIR // HDIM):
        cols = slice(head * HDIM, (head + 1) * HDIM)
        delta = jnp.sum(product[cols, :], axis=0, keepdims=True)
        keys = jnp.concatenate([k_ref[:, cols], km[...]], axis=1)
        values = v_ref[:, cols]
        grad_k = jnp.zeros((length, HDIM), jnp.float32)
        grad_v = jnp.zeros((length, HDIM), jnp.float32)
        grad_q = []
        for begin in range(0, length, QROWS):
            if slot % SPACING == 0:
                run_slot(slot)
            slot += 1
            span = slice(begin, begin + QROWS)
            low_q, low_go = q_ref[span, cols], go_ref[span, cols]
            scores = rows_dot(keys, jnp.concatenate([low_q, qm[span, :]], axis=1))
            probs = jnp.exp(scores - lse_ref[0, head : head + 1, span])
            grad_v += jnp.dot(probs.astype(jnp.bfloat16), low_go, preferred_element_type=jnp.float32)
            grad_p = rows_dot(values, low_go)
            grad_s = (probs * (grad_p - delta[:, span])).astype(jnp.bfloat16)
            grad_k += jnp.dot(grad_s, low_q, preferred_element_type=jnp.float32)
            grad_q.append(jnp.dot(flipped[cols, :], grad_s, preferred_element_type=jnp.float32))
        gq_parts.append(jnp.concatenate(grad_q, axis=1))
        gk_parts.append(grad_k)
        gv_parts.append(grad_v)
    grad_q = jnp.transpose(jnp.concatenate(gq_parts, axis=0)) * 0.125
    grad_k = jnp.concatenate(gk_parts, axis=1)
    gp = jnp.concatenate(
        [
            (grad_q * cos_tab + swap_halves(grad_q * sin_tab)).astype(jnp.bfloat16),
            (grad_k * cos_tab + swap_halves(grad_k * sin_tab)).astype(jnp.bfloat16),
            jnp.concatenate(gv_parts, axis=1).astype(jnp.bfloat16),
        ],
        axis=1,
    )
    gp_all[i] = gp
    term = jnp.dot(normed_t[...], gp, preferred_element_type=jnp.float32)
    terms[i] = term.astype(jnp.bfloat16).reshape(4, 2, part, 3 * PAIR)
    run_slot(slots)

    def rep_copy(m):
        return remote(
            gain_rep.at[place.r],
            gain_rep.at[place.r],
            rep_send.at[m - 1],
            rep_recv.at[m - 1],
            (place.f, (place.y_dev()[1], place.core_dev()[1], 3 - place.r)[m - 1]),
        )

    def fsdp_copy(m):
        return remote(
            gain_parts.at[place.fsdp_of(m)],
            gain_all.at[place.f],
            fsdp_send.at[m - 1],
            fsdp_recv.at[m - 1],
            (place.fsdp_of(m), place.r),
        )

    @pl.when(i == npairs - 1)
    def _():
        for copy in bulk_copies:
            copy.wait()
        gain = gain_ref[0:1, :]
        blocks = length // QROWS
        share = len(events) // (blocks + 1)
        first = jnp.zeros((1, width), jnp.float32)
        writes = []
        for b in range(blocks):
            rows = slice(b * QROWS, (b + 1) * QROWS)
            e1 = jnp.zeros((QROWS, width), jnp.float32)
            for p in range(npairs):
                e1 += rows_dot(gp_all[p, rows, :], wq_buf[p].reshape(width, 3 * PAIR))
            v = x_buf[rows, :].astype(jnp.float32)
            c = v - jnp.mean(v, axis=1, keepdims=True)
            r1 = lax.rsqrt(jnp.mean(c * c, axis=1, keepdims=True) + eps)
            n1 = c * r1
            first += jnp.sum(e1 * n1, axis=0, keepdims=True)
            f1 = e1 * gain
            drift = f1 - jnp.mean(f1, axis=1, keepdims=True)
            gm_buf[rows, :] += r1 * (drift - n1 * jnp.mean(f1 * n1, axis=1, keepdims=True))
            write = pltpu.make_async_copy(gm_buf.at[rows, :], input_grad.at[rows, :], out_sem.at[b])
            write.start()
            writes.append(write)
            for _ in range(2):
                if events:
                    reduce.step(*events.pop(0)[1:])
        sub = lax.broadcasted_iota(jnp.int32, (8, width), 0)
        gain_rep[place.r] = jnp.where(sub == 0, first, jnp.where(sub == 1, second_ref[...], 0.0))
        for m in (1, 2, 3):
            rep_copy(m).start()
        for m in (1, 2, 3):
            rep_copy(m).wait()
        total = gain_rep[0] + gain_rep[1] + gain_rep[2] + gain_rep[3]
        gain_parts[...] = jnp.zeros_like(gain_parts)
        for f in range(8):
            gain_parts[f, :, :part] = total[:, f * part : (f + 1) * part]
        for m in range(1, 8):
            fsdp_copy(m).start()
        gain_all[place.f] = gain_parts[place.f]
        while events:
            reduce.step(*events.pop(0)[1:])
        for m in range(1, 8):
            fsdp_copy(m).wait()
        shared = gain_all[0]
        for f in range(1, 8):
            shared += gain_all[f]
        gain_out[...] = shared
        for write in writes:
            write.wait()
        reduce.finish()


def backward(
    queries, keyset, valueset, mixed, grad_mixed, lse, cos_tab, sin_tab, qm, km, gains, second_term,
    normed_one, layer_input, grad_middle, wq_all, narrow_term, wide_term, attn_term,
):
    length, width = queries.shape
    pairs, part = width // PAIR, width // 8
    cuts = [cuts_of(t.shape[1], 3 * PAIR) for t in (narrow_term, wide_term, attn_term)]
    count = pairs + sum(len(c) for c in cuts)
    cols = 3 * PAIR
    block = pl.BlockSpec((length, PAIR), lambda i: (0, i))
    whole = pl.BlockSpec(memory_space=pltpu.VMEM)
    hbm = pl.BlockSpec(memory_space=pl.ANY)
    low = lambda *shape: pltpu.VMEM(shape, jnp.bfloat16)
    wide = lambda *shape: pltpu.VMEM(shape, jnp.float32)
    f32 = lambda *shape: jax.ShapeDtypeStruct(shape, jnp.float32)
    dma = pltpu.SemaphoreType.DMA
    terms = [t.reshape(4, 2, part, t.shape[1]) for t in (narrow_term, wide_term, attn_term)]
    return pl.pallas_call(
        functools.partial(backward_kernel, (pairs, cuts)),
        grid=(pairs,),
        in_specs=[block] * 5
        + [pl.BlockSpec((1, 2, length), lambda i: (i, 0, 0))]
        + [whole] * 7
        + [hbm] * 6,
        out_specs=[hbm] + [whole] * 5,
        out_shape=[
            f32(length, width),
            f32(part, 3 * width),
            f32(part, attn_term.shape[1]),
            f32(part, wide_term.shape[1]),
            f32(part, narrow_term.shape[1]),
            f32(8, PAIR),
        ],
        scratch_shapes=[
            low(width, length),
            low(length, width),
            wide(length, width),
            low(pairs, 4, 2, part, cols),
            low(pairs, length, cols),
            low(pairs, 4, 2, part, cols),
            low(count, 4, 2, HALF, cols),
            low(count, 4, 2, HALF, cols),
            low(count, 4, 2, STEP, cols),
            low(count, 4, 2 * STEP, cols),
            low(count, 3, 2 * STEP, cols),
            low(count, 2 * STEP, cols),
            low(count, 2 * STEP, cols),
            low(count, HALF, cols),
            low(count, HALF, cols),
            wide(4, 8, width),
            wide(8, 8, PAIR),
            wide(8, 8, PAIR),
            dma((count, 8)),
            dma((count, 8)),
            dma((count,)),
            dma((3,)),
            dma((3,)),
            dma((3,)),
            dma((7,)),
            dma((7,)),
            dma((length // QROWS,)),
        ],
        compiler_params=pltpu.CompilerParams(
            vmem_limit_bytes=62 << 20, collective_id=1, has_side_effects=True
        ),
        cost_estimate=pl.CostEstimate(
            flops=60 * width * length * length, bytes_accessed=40 * length * width,
            transcendentals=pairs * 2 * length * length,
        ),
    )(
        queries, keyset, valueset, mixed, grad_mixed, lse, cos_tab, sin_tab, qm, km, gains, second_term,
        normed_one, layer_input, grad_middle, wq_all, *terms,
    )


def erf_poly(x):
    x = jnp.clip(x, -3.832506856900711, 3.832506856900711)
    sq = x * x
    top = jnp.float32(0.00022905065861350646)
    for coef in (0.0034082910107109506, 0.050955695062380861, 0.18520832239976145, 1.128379143519084):
        top = top * sq + coef
    low = jnp.float32(-1.1791602954361697e-7)
    for coef in (
        0.000023547966471313185, 0.0010179625278914885, 0.014070470171167667, 0.11098505178285362,
        0.49746925110067538, 1.0,
    ):
        low = low * sq + coef
    return x * top / low


def middle_kernel(
    x_ref, mixed_ref, og_ref, km_ref, gain_ref, wa, ww, wn,
    layer_out, go_out, gm_out, second_out, narrow_out, wide_out, attn_out,
    hidden_all, gl_all, gml_all, gt_t, n2_t, mixed_t,
):
    i = pl.program_id(0)
    rows_here, width = x_ref.shape
    half_ff = wn.shape[1]
    tiles = 8
    piece = 3 * PAIR
    rows = pl.ds(pl.multiple_of(i * rows_here, rows_here), rows_here)
    gain = gain_ref[1:2, :]
    mixed = mixed_ref[...]
    middle = x_ref[...].astype(jnp.float32) + jnp.dot(mixed, wa[...], preferred_element_type=jnp.float32)
    c = middle - jnp.mean(middle, axis=1, keepdims=True)
    r2 = lax.rsqrt(jnp.mean(c * c, axis=1, keepdims=True) + eps)
    n2 = c * r2
    low_n2 = (n2 * gain).astype(jnp.bfloat16)
    live = jnp.where(km_ref[:, tiles : tiles + 1].astype(jnp.float32) < -1.0, 0.0, 1.0)
    gt = og_ref[...].astype(jnp.float32) * live
    low_gt = gt.astype(jnp.bfloat16)
    gt_t[:, rows] = jnp.transpose(low_gt)
    n2_t[:, rows] = jnp.transpose(low_n2)
    mixed_t[:, rows] = jnp.transpose(mixed)
    e = jnp.zeros((rows_here, width), jnp.float32)
    out = middle
    for lo in range(0, half_ff, piece):
        at, up = slice(lo, lo + piece), slice(half_ff + lo, half_ff + lo + piece)
        a = jnp.dot(low_n2, ww[:, at], preferred_element_type=jnp.float32)
        gate = jnp.dot(low_n2, ww[:, up], preferred_element_type=jnp.float32)
        gh = jnp.dot(low_gt, wn[:, at], preferred_element_type=jnp.float32)
        cdf = 0.5 + 0.5 * erf_poly(a * (2.0 ** -0.5))
        act = a * cdf
        slope = cdf + a * jnp.exp(a * a * -0.5) * ((2.0 * math.pi) ** -0.5)
        hidden = (act * gate).astype(jnp.bfloat16)
        gl_a = (gh * gate * slope).astype(jnp.bfloat16)
        gl_g = (gh * act).astype(jnp.bfloat16)
        hidden_all[rows, at] = hidden
        gl_all[rows, at] = gl_a
        gl_all[rows, up] = gl_g
        out += rows_dot(hidden, wn[:, at])
        e += rows_dot(gl_a, ww[:, at]) + rows_dot(gl_g, ww[:, up])
    layer_out[...] = out.astype(jnp.bfloat16)
    f2 = e * gain
    gm = gt + r2 * (f2 - jnp.mean(f2, axis=1, keepdims=True) - n2 * jnp.mean(f2 * n2, axis=1, keepdims=True))
    gm_out[...] = gm
    low_gm = gm.astype(jnp.bfloat16)
    gml_all[rows, :] = low_gm
    go_out[...] = rows_dot(low_gm, wa[...]).astype(jnp.bfloat16)
    part = jnp.sum(e * n2, axis=0, keepdims=True)

    @pl.when(i == 0)
    def _():
        second_out[...] = part

    @pl.when(i > 0)
    def _():
        second_out[...] += part

    @pl.when(i == pl.num_programs(0) - 1)
    def _():
        for left, right, term in (
            (gt_t, hidden_all, narrow_out), (n2_t, gl_all, wide_out), (mixed_t, gml_all, attn_out)
        ):
            for lo in range(0, right.shape[1], piece):
                at = slice(lo, lo + piece)
                term[:, at] = jnp.dot(
                    left[...], right[:, at], preferred_element_type=jnp.float32
                ).astype(jnp.bfloat16)


def middle_part(layer_input, mixed, out_grad, km, gains, wa, ww, wn):
    length, width = layer_input.shape
    half_ff = wn.shape[1]
    tile = 2 * TILE
    block = pl.BlockSpec((tile, width), lambda i: (i, 0))
    whole = pl.BlockSpec(memory_space=pltpu.VMEM)
    shape = jax.ShapeDtypeStruct
    low = lambda *dims: pltpu.VMEM(dims, jnp.bfloat16)
    return pl.pallas_call(
        middle_kernel,
        grid=(length // tile,),
        in_specs=[block] * 3 + [pl.BlockSpec((tile, HDIM), lambda i: (i, 0))] + [whole] * 4,
        out_specs=[block] * 3 + [whole] * 4,
        out_shape=[
            shape((length, width), jnp.bfloat16),
            shape((length, width), jnp.bfloat16),
            shape((length, width), jnp.float32),
            shape((1, width), jnp.float32),
            shape((width, half_ff), jnp.bfloat16),
            shape((width, 2 * half_ff), jnp.bfloat16),
            shape((width, width), jnp.bfloat16),
        ],
        scratch_shapes=[
            low(length, half_ff),
            low(length, 2 * half_ff),
            low(length, width),
            low(width, length),
            low(width, length),
            low(width, length),
        ],
        compiler_params=pltpu.CompilerParams(vmem_limit_bytes=60 << 20),
    )(layer_input, mixed, out_grad, km, gains, wa, ww, wn)


def on_device(
    layer_input,
    qkv_weight,
    attn_weight,
    wide_weight,
    narrow_weight,
    first_gain,
    second_gain,
    out_grad,
    token_seg,
    token_live,
):
    gains = jnp.stack([first_gain, second_gain], axis=1)
    gains = jnp.pad(gains, ((0, 0), (0, PAIR - 2)))
    qkv_full, gains = gather_weights([qkv_weight, gains])
    attn_full, wide_full, narrow_full = gather_weights([attn_weight, wide_weight, narrow_weight])
    scale_one = gains[:, 0].astype(jnp.float32)
    scale_two = gains[:, 1].astype(jnp.float32)
    residual_in = layer_input.astype(jnp.float32)
    qm, km = mask_columns(token_seg, token_live)
    cos_tab, sin_tab = rope_tables(token_seg)
    normed_one = layer_norm(residual_in, scale_one).astype(jnp.bfloat16)
    packed = jnp.dot(normed_one, qkv_full, preferred_element_type=jnp.float32)
    queries, keyset, valueset, mixed_rows, lse = attend(packed, cos_tab, sin_tab, qm, km)
    middle = residual_in + jnp.dot(mixed_rows, attn_full, preferred_element_type=jnp.float32)
    normed_two = layer_norm(middle, scale_two).astype(jnp.bfloat16)
    lifted = jnp.dot(normed_two, wide_full, preferred_element_type=jnp.float32)
    hidden = geglu(lifted).astype(jnp.bfloat16)
    layer_out = middle + jnp.einsum(
        "tf,df->td", hidden, narrow_full, preferred_element_type=jnp.float32
    )
    grad_top = out_grad.astype(jnp.float32) * token_live.astype(jnp.float32)[:, None]
    grad_top_low = grad_top.astype(jnp.bfloat16)
    narrow_term = jnp.einsum("td,tf->df", grad_top_low, hidden, preferred_element_type=jnp.float32)
    grad_hidden = jnp.dot(grad_top_low, narrow_full, preferred_element_type=jnp.float32)
    _, pull_gate = jax.vjp(geglu, lifted)
    grad_lifted = pull_gate(grad_hidden)[0].astype(jnp.bfloat16)
    wide_term = jnp.einsum("td,tf->df", normed_two, grad_lifted, preferred_element_type=jnp.float32)
    grad_norm_two = jnp.einsum(
        "tf,df->td", grad_lifted, wide_full, preferred_element_type=jnp.float32
    )
    _, pull_two = jax.vjp(layer_norm, middle, scale_two)
    grad_mid_ln, second_term = pull_two(grad_norm_two)
    grad_middle = grad_top + grad_mid_ln
    grad_middle_low = grad_middle.astype(jnp.bfloat16)
    attn_term = jnp.einsum(
        "td,te->de", mixed_rows, grad_middle_low, preferred_element_type=jnp.float32
    )
    grad_mixed = jnp.einsum(
        "te,de->td", grad_middle_low, attn_full, preferred_element_type=jnp.float32
    )
    shares = scatter_sums([narrow_term, wide_term, attn_term])
    grad_parts = attend_back(
        queries, keyset, valueset, mixed_rows, grad_mixed.astype(jnp.bfloat16), lse,
        cos_tab, sin_tab, qm, km,
    )
    grad_packed = jnp.concatenate(grad_parts, axis=1)
    qkv_term = jnp.einsum("td,tf->df", normed_one, grad_packed, preferred_element_type=jnp.float32)
    grad_norm_one = jnp.einsum(
        "tf,df->td", grad_packed, qkv_full, preferred_element_type=jnp.float32
    )
    _, pull_one = jax.vjp(layer_norm, residual_in, scale_one)
    grad_in_ln, first_term = pull_one(grad_norm_one)
    input_grad = grad_middle + grad_in_ln
    gain_terms = jnp.stack([first_term, second_term], axis=1)
    gain_terms = jnp.pad(gain_terms, ((0, 0), (0, PAIR - 2)))
    qkv_share, gain_share = scatter_sums([qkv_term, gain_terms])
    return (
        layer_out.astype(jnp.bfloat16),
        input_grad,
        qkv_share,
        shares[2],
        shares[1],
        shares[0],
        gain_share[:, 0],
        gain_share[:, 1],
    )


def on_device_tuned(
    layer_input,
    qkv_weight,
    attn_weight,
    wide_weight,
    narrow_weight,
    first_gain,
    second_gain,
    out_grad,
    token_seg,
    token_live,
):
    length, width = layer_input.shape
    pairs, part = width // PAIR, attn_weight.shape[0]
    wq_in = qkv_weight.reshape(part, 3, pairs, PAIR).transpose(2, 0, 1, 3).reshape(pairs, part, 3 * PAIR)
    gain_in = jnp.pad(jnp.stack([first_gain, second_gain]).astype(jnp.float32), ((0, 6), (0, PAIR - part)))
    (queries, keyset, valueset, mixed_rows, lse, normed_one, gains, wq_all, wa_all, ww_all, wn_all,
     cos_tab, sin_tab, qm, km) = forward(
        layer_input, wq_in, attn_weight, wide_weight, narrow_weight, gain_in, token_seg, token_live
    )
    attn_full, wide_full, narrow_full = (w.reshape(width, w.shape[-1]) for w in (wa_all, ww_all, wn_all))
    layer_out, grad_mixed, grad_middle, second_term, *low_terms = middle_part(
        layer_input, mixed_rows, out_grad, km, gains, attn_full, wide_full, narrow_full
    )
    input_grad, qkv_share, attn_share, wide_share, narrow_share, gain_share = backward(
        queries, keyset, valueset, mixed_rows, grad_mixed, lse, cos_tab, sin_tab, qm, km,
        gains, second_term, normed_one, layer_input, grad_middle, wq_all, *low_terms,
    )
    return (
        layer_out,
        input_grad,
        qkv_share,
        attn_share,
        wide_share,
        narrow_share,
        gain_share[0, :part],
        gain_share[1, :part],
    )


def solution(mesh):
    tuned = mesh.shape["fsdp"] == 8 and mesh.shape["rep"] == 4
    return jax.shard_map(
        on_device_tuned if tuned else on_device,
        mesh=mesh,
        in_specs=(
            P(("fsdp", "rep"), None),
            P("fsdp", None),
            P("fsdp", None),
            P("fsdp", None),
            P("fsdp", None),
            P("fsdp"),
            P("fsdp"),
            P(("fsdp", "rep"), None),
            P(("fsdp", "rep")),
            P(("fsdp", "rep")),
        ),
        out_specs=(
            P(("fsdp", "rep"), None),
            P(("fsdp", "rep"), None),
            P("fsdp", None),
            P("fsdp", None),
            P("fsdp", None),
            P("fsdp", None),
            P("fsdp"),
            P("fsdp"),
        ),
        check_vma=False,
    )
```
